32 devices in a mesh: row: 4 (over y, x), col: 8 (over z, core).
Axes of the slice: x: 2, y: 2, z: 4, core: 2. Of those that a mesh axis runs over, the one named last changes fastest.
Arguments:
- activations: bfloat16 [8, 256, 8192], P('row')
- out_grads: bfloat16 [8, 256, 28672], P('row', None, 'col')
- valid_len: int32 [8], P('row'), may hold values from 1 to 256, 1024 in all
- weight: bfloat16 [8192, 28672], P('row', 'col'), may hold values from -0.0625 to 0.0625
- sketch: bfloat16 [28672, 512], P('col'), may hold values from -6 to 6
Outputs:
- basis: float32 [8192, 512], P(('row', 'col'))
- coeffs: float32 [512, 28672], P('row', 'col')
The draws below stay inside these ranges and needn't reach their ends.
Inputs may be any that keep to these rules, and one draw needn't show every extreme that they name: `valid_len`: valid tokens of each sequence; at least one sequence fills all 256 slots.
All inputs are finite; a program needn't handle non-finite values. No bound on the sum of `valid_len` on one device may be relied on, other than what follows from the above.
Results may differ from the reference program's by a relative error of at most 0.01.
Values may be sent and summed in bfloat16 or wider, within the bound.
No kernel may reach another device: no remote copies, remote signals or barrier semaphores. Data moves between devices by JAX's collectives and lax.ppermute only.
A program may use at most 128 MiB of HBM per device.

```python
import math
import jax
import jax.numpy as jnp
import numpy as np
from jax import lax

D = 8192
FF = 28672
RANK = 512
LEN = 256
SEQS = 8
N_COL = 8


def draw_activations(key, part):
    key_scale = jax.random.fold_in(key, 0)
    key_base = jax.random.fold_in(key, 1)
    key_mix = jax.random.fold_in(key, 3)
    feature_scale = jnp.exp(jax.random.uniform(key_scale, (D,), jnp.float32, jnp.log(0.3), jnp.log(3.0)))
    feature_scale = feature_scale * (1.0 + 0.8 * jnp.arange(D, dtype=jnp.float32) / D)
    seq_feature = jnp.exp(jax.random.uniform(key_mix, (SEQS, 1, D), jnp.float32, jnp.log(0.1), jnp.log(10.0)))
    base = jax.random.normal(key_base, (SEQS, LEN, D), jnp.float32)
    return (base * seq_feature * feature_scale).astype(jnp.bfloat16)


def draw_out_grads(key, part):
    key_scale, key_base = jax.random.split(key, 2)
    column_scale = jnp.exp(jax.random.uniform(key_scale, (FF,), jnp.float32, jnp.log(0.5), jnp.log(2.0)))
    column_scale = column_scale * (0.6 + 1.2 * jnp.arange(FF, dtype=jnp.float32) / FF)
    base = jnp.clip(jax.random.normal(key_base, (SEQS, LEN, FF), jnp.float32), -4.0, 4.0)
    return (base * column_scale).astype(jnp.bfloat16)


def level_of(stream_key, extent, cuts, low, largest):
    loudness, own = 1.0, jax.random.fold_in(stream_key, 6)
    for position, blocks in cuts:
        steps = jnp.exp(jax.random.uniform(jax.random.fold_in(own, position), (blocks,), jnp.float32, low / len(cuts), largest / len(cuts)))
        loudness = loudness * jnp.repeat(steps, extent[position] // blocks).reshape([-1 if axis == position else 1 for axis in range(len(extent))])
    return loudness


def length_profile(number_of, total, reach, lean):
    weights = [(1 << 20) // math.isqrt(grade ** lean) + 1 for grade in range(2, number_of + 1)]
    surplus, counts = total - reach - (number_of - 1), [1] * (number_of - 1)
    while surplus > 0:
        free = [i for i in range(number_of - 1) if counts[i] < reach]
        pool, left = sum([weights[i] for i in free]), surplus
        for i in free:
            addition = min(reach - counts[i], max(1, left * weights[i] // pool), surplus)
            counts[i] = counts[i] + addition
            surplus = surplus - addition
    return np.array([reach] + counts)


def uneven(own_key, amount, total, limit, lean):
    if amount == 2:
        one = jax.random.randint(own_key, (), max(1, total - limit), min(limit, total - 1) + 1)
        return jnp.stack([one, total - one])
    tallies = jnp.asarray(length_profile(amount, total, limit, lean), jnp.int32)
    twos = (amount - 1) // 2
    giver, taker = tallies[1:1 + 2 * twos:2], tallies[2:2 + 2 * twos:2]
    room = jnp.minimum(giver - 1, limit - taker)
    shifted = jax.random.randint(jax.random.fold_in(own_key, 1), (twos,), 0, 1 << 20) % (room + 1)
    tallies = tallies.at[1:1 + 2 * twos:2].set(giver - shifted).at[2:2 + 2 * twos:2].set(taker + shifted)
    return tallies[jax.random.permutation(jax.random.fold_in(own_key, 2), amount)]


def bell_draw(rng, dims, spread, reach, pieces=(), held_as=jnp.bfloat16):
    result = spread * jax.random.normal(rng, dims, jnp.float32)
    if pieces:
        result = result * level_of(rng, dims, pieces, -0.22, 0.18)
    return jnp.clip(result, -reach, reach).astype(held_as)


def setup_inputs(seed: int = 0) -> dict:
    splits = jax.random.split(jax.random.key(seed), 6)
    activations = draw_activations(jax.random.fold_in(splits[5], 71), 0)
    out_grads = draw_out_grads(jax.random.fold_in(splits[5], 71), 0)
    valid_len = uneven(splits[2], SEQS, SEQS * LEN // 2, LEN, 0).astype(jnp.int32)
    weight = bell_draw(splits[3], (D, FF), D ** -0.5, 0.0625, ((0, 4), (1, 8)))
    sketch = bell_draw(splits[4], (FF, RANK), 1.0, 6.0, ((0, 8),))
    return dict(activations=activations, out_grads=out_grads, valid_len=valid_len, weight=weight, sketch=sketch)


def contract_rows(left, right):
    return lax.dot_general(left.astype(jnp.float32), right.astype(jnp.float32), (((0,), (0,)), ((), ())), preferred_element_type=jnp.float32)

def orthonormal(sketch_rows):
    gram = lax.dot_general(sketch_rows, sketch_rows, (((0,), (0,)), ((), ())), precision=lax.Precision.HIGHEST)
    factor_low = jnp.linalg.cholesky(gram)
    return lax.linalg.triangular_solve(factor_low, sketch_rows, left_side=False, lower=True, transpose_a=True)

def reference(activations, out_grads, valid_len, weight, sketch):
    block_cols = FF // N_COL
    positions = jnp.arange(LEN, dtype=jnp.int32)

    def seq_mass(seq_index):
        valid = (positions < valid_len[seq_index]).astype(jnp.bfloat16)
        inputs = activations[seq_index]
        masked = out_grads[seq_index] * valid[:, None]

        def add_block(running, block_index):
            columns = lax.dynamic_slice_in_dim(masked, (block_index * block_cols).astype(jnp.int32), block_cols, 1)
            grad_block = contract_rows(inputs, columns)
            return (running + lax.optimization_barrier(jnp.sum(grad_block * grad_block, axis=1)), None)
        mass, unused = lax.scan(add_block, jnp.zeros((D,), jnp.float32), jnp.arange(N_COL, dtype=jnp.int32))
        return mass
    fisher = lax.optimization_barrier(jnp.sum(lax.map(seq_mass, jnp.arange(SEQS, dtype=jnp.int32)), axis=0))
    total_mass = jnp.sum(fisher)
    row_scale = jnp.sqrt(fisher / (total_mass / D + 1e-06))
    first_sketch = (row_scale[:, None] * jnp.dot(weight.astype(jnp.float32), sketch.astype(jnp.float32), preferred_element_type=jnp.float32)).astype(jnp.bfloat16)
    scaled = (row_scale[:, None] * weight.astype(jnp.float32)).astype(jnp.bfloat16)
    projected = contract_rows(scaled, first_sketch).astype(jnp.bfloat16)
    second_sketch = jnp.dot(scaled.astype(jnp.float32), projected.astype(jnp.float32), preferred_element_type=jnp.float32)
    second_basis = orthonormal(second_sketch)
    coeff_raw = contract_rows(second_basis.astype(jnp.bfloat16), scaled)
    return (second_basis * D ** 0.5, coeff_raw * FF ** 0.5)
```

```python
import functools
import math

import jax
import jax.numpy as jnp
from jax import lax
from jax.experimental import pallas as pl
from jax.experimental.pallas import tpu as pltpu
from jax.sharding import PartitionSpec as P

AXES = ("row", "col")
F32 = jnp.float32
BF16 = jnp.bfloat16


def swap(block, row_bit, col_bit):
    rows, cols = lax.axis_size("row"), lax.axis_size("col")
    pairs = []
    for row in range(rows):
        for col in range(cols):
            other = (row ^ row_bit(col & 1)) * cols + (col ^ col_bit(col & 1))
            pairs.append((row * cols + col, other))
    return lax.ppermute(block, AXES, pairs)


class Halving:
    def __init__(self, axis):
        self.axis = axis
        self.size = lax.axis_size(axis)
        bits = list(range(self.size.bit_length() - 1))
        if axis == "col":
            self.orders = (bits, bits[:1] + bits[:0:-1])
        else:
            self.orders = (bits, bits[::-1])
        self.me = lax.axis_index(axis)
        self.odd = lax.axis_index("col") & 1
        steps = len(bits)
        self.masks = tuple(
            [
                sum(1 << order[t] for t in range(steps) if v >> (steps - 1 - t) & 1)
                for v in range(self.size)
            ]
            for order in self.orders
        )
        if axis == "col":
            half = self.size // 2
            even, odd = (masks[:half] for masks in self.masks)
            self.masks = (even + [1 ^ mask for mask in odd], odd + [1 ^ mask for mask in even])

    def block(self, v):
        even, odd = (masks[v] for masks in self.masks)
        return self.me ^ (even if even == odd else jnp.where(self.odd == 0, even, odd))

    def step(self, t, block):
        even, odd = (1 << order[t] for order in self.orders)
        pick = lambda parity: odd if parity else even
        none = lambda parity: 0
        return swap(block, *((none, pick) if self.axis == "col" else (pick, none)))

    def scatter_sum(self, parts):
        pick = lambda v: lax.dynamic_index_in_dim(parts, self.block(v), 0, keepdims=False)
        now = [pick(v) for v in range(self.size)]
        for t in range(len(self.orders[0])):
            half = len(now) // 2
            wire = F32 if t == 0 and self.axis == "col" else BF16
            came = self.step(t, jnp.stack([x.astype(wire) for x in now[half:]]))
            now = [now[v].astype(F32) + came[v].astype(F32) for v in range(half)]
        return now[0]

    def gather(self, own):
        now = own[None]
        for t in reversed(range(len(self.orders[0]))):
            now = jnp.concatenate([now, self.step(t, now)])
        return now

    def in_order(self, virtual):
        places = []
        for masks in self.masks:
            inverse = [0] * self.size
            for v, mask in enumerate(masks):
                inverse[mask] = v
            places.append(jnp.array(inverse, jnp.int32))
        place = jnp.where(self.odd == 0, places[0], places[1])
        take = lambda j: lax.dynamic_index_in_dim(
            virtual, place[self.me ^ j], 0, keepdims=False
        )
        return jnp.concatenate([take(j) for j in range(self.size)])


def sum_everywhere(value, row=True, col=True):
    none = lambda parity: 0
    if col:
        for bit in range(lax.axis_size("col").bit_length() - 1):
            value = value + swap(value, none, lambda parity: 1 << bit)
    if row:
        steps = lax.axis_size("row").bit_length() - 1
        for t in range(steps):
            pick = lambda parity: 1 << (steps - 1 - t if parity else t)
            value = value + swap(value, pick, none)
    return value


def token_gram_kernel(valid_ref, grads_ref, high_ref, low_ref, scale_ref):
    seq = pl.program_id(0)
    length = grads_ref.shape[1]
    tokens = lax.broadcasted_iota(jnp.int32, (length, 1), 0)
    grads = grads_ref[0].astype(F32)
    grads = jnp.where(tokens < valid_ref[seq], grads, 0.0)
    largest = jnp.max(jnp.abs(grads), axis=1, keepdims=True)
    scale = jnp.ones_like(largest)
    shrink = jnp.ones_like(largest)
    for power in (16, 48, 80):
        step = 2.0 ** (power + 16)
        high, low = largest >= 2.0**power, largest < 2.0**-power
        scale = jnp.where(high, step, jnp.where(low, 1.0 / step, scale))
        shrink = jnp.where(high, 1.0 / step, jnp.where(low, step, shrink))
    near = (grads * shrink).astype(BF16)
    gram = lax.dot_general(near, near, (((1,), (1,)), ((), ())), preferred_element_type=F32)
    high = gram.astype(BF16)
    high_ref[0] = high
    low_ref[0] = (gram - high.astype(F32)).astype(BF16)
    scale_ref[0] = jnp.broadcast_to(scale, (length, 128))


def row_mass_kernel(acts_ref, high_ref, low_ref, scale_ref, mass_ref):
    total = jnp.zeros((1, acts_ref.shape[2]), F32)
    for seq in range(acts_ref.shape[0]):
        acts = acts_ref[seq].astype(F32) * scale_ref[seq][:, :1]
        short = acts.astype(BF16)
        spread = jnp.dot(high_ref[seq], short, preferred_element_type=F32)
        spread = spread + jnp.dot(low_ref[seq], short, preferred_element_type=F32)
        total = total + jnp.sum(spread * acts, axis=0, keepdims=True)
    mass_ref[...] = total


def local_mass(activations, out_grads, valid_len):
    seqs, length, width = activations.shape
    cols = out_grads.shape[2]
    square = jax.ShapeDtypeStruct((seqs, length, length), BF16)
    whole = lambda seq, valid: (seq, 0, 0)
    high, low, scale = pl.pallas_call(
        token_gram_kernel,
        out_shape=(square, square, jax.ShapeDtypeStruct((seqs, length, 128), F32)),
        grid_spec=pltpu.PrefetchScalarGridSpec(
            num_scalar_prefetch=1,
            grid=(seqs,),
            in_specs=[pl.BlockSpec((1, length, cols), whole)],
            out_specs=(
                pl.BlockSpec((1, length, length), whole),
                pl.BlockSpec((1, length, length), whole),
                pl.BlockSpec((1, length, 128), whole),
            ),
        ),
        compiler_params=pltpu.CompilerParams(vmem_limit_bytes=48 << 20),
        cost_estimate=pl.CostEstimate(
            flops=2 * seqs * length * length * cols,
            bytes_accessed=2 * out_grads.size,
            transcendentals=0,
        ),
        name="token_gram",
    )(valid_len, out_grads)
    tile = math.gcd(width, 1024)
    fixed = lambda i: (0, 0, 0)
    mass = pl.pallas_call(
        row_mass_kernel,
        out_shape=jax.ShapeDtypeStruct((1, width), F32),
        grid=(width // tile,),
        in_specs=[
            pl.BlockSpec((seqs, length, tile), lambda i: (0, 0, i)),
            pl.BlockSpec((seqs, length, length), fixed),
            pl.BlockSpec((seqs, length, length), fixed),
            pl.BlockSpec((seqs, length, 128), fixed),
        ],
        out_specs=pl.BlockSpec((1, tile), lambda i: (0, i)),
        compiler_params=pltpu.CompilerParams(vmem_limit_bytes=48 << 20),
        cost_estimate=pl.CostEstimate(
            flops=4 * seqs * length * length * width,
            bytes_accessed=2 * activations.size,
            transcendentals=0,
        ),
        name="row_mass",
    )(activations, high, low, scale)
    return mass.reshape(width)


def invert_block(tile):
    size = tile.shape[0]
    groups = [tile[i : i + 8] for i in range(0, size, 8)]
    lane = lax.broadcasted_iota(jnp.int32, (8, size), 1)
    sub = lax.broadcasted_iota(jnp.int32, (8, size), 0)
    done = []
    for g in range(size // 8):
        base = 8 * g
        inside = (lane >= base) & (lane < base + 8)
        now = groups[g]
        column = [jnp.broadcast_to(now[:, base + j : base + j + 1], (8, size)) for j in range(8)]
        now = jnp.where(inside, jnp.where(lane - base == sub, 1.0, 0.0), now)
        out = jnp.zeros((8, size), F32)
        for k in range(8):
            here = sub == k
            pivot = jnp.broadcast_to(column[k][k : k + 1], (8, size))
            row = jnp.broadcast_to(now[k : k + 1], (8, size))
            out = jnp.where(here, row * lax.rsqrt(pivot), out)
            inverse = 1.0 / pivot
            row = row * inverse
            now = jnp.where(here, row, now - column[k] * row)
            for j in range(k + 1, 8):
                part = jnp.broadcast_to(column[j][k : k + 1], (8, size)) * inverse
                column[j] = jnp.where(here, part, column[j] - column[k] * part)
        done.append(jnp.where(lane < base + 8, out, 0.0))
        rows = [jnp.broadcast_to(now[s : s + 1], (8, size)) for s in range(8)]
        for i in range(g + 1, size // 8):
            left = groups[i]
            kept = jnp.where(inside, 0.0, left)
            for s in range(8):
                weight = jnp.broadcast_to(left[:, base + s : base + s + 1], (8, size))
                kept = kept - weight * rows[s]
            groups[i] = kept
    return jnp.concatenate(done)


def inverse_factor_kernel(gram_ref, out_ref, work_ref):
    size = gram_ref.shape[0]
    block = 128
    count = size // block
    work_ref[...] = gram_ref[...]
    lane = lax.broadcasted_iota(jnp.int32, (block, size), 1)

    def step(k, carry):
        base = pl.multiple_of(k * block, block)
        here = pl.ds(base, block)
        small = invert_block(work_ref[here, here])
        inside = (lane >= base) & (lane < base + block)
        eye = lax.broadcasted_iota(jnp.int32, (block, size), 0) == lane - base
        rows = jnp.where(inside, jnp.where(eye, 1.0, 0.0), work_ref[here, :])
        rows = jnp.dot(small, rows, precision=lax.Precision.HIGHEST, preferred_element_type=F32)
        out_ref[here, :] = jnp.where(lane < base + block, rows, 0.0)
        work_ref[here, :] = rows

        def update(i, carry):
            there = pl.ds(pl.multiple_of(i * block, block), block)
            left = work_ref[here, there]
            old = jnp.where(inside, 0.0, work_ref[there, :])
            work_ref[there, :] = old - lax.dot_general(
                left,
                rows,
                (((0,), (0,)), ((), ())),
                precision=lax.Precision.HIGHEST,
                preferred_element_type=F32,
            )
            return carry

        return lax.fori_loop(k + 1, count, update, carry)

    lax.fori_loop(0, count, step, 0)


def inverse_factor(gram):
    size = gram.shape[0]
    return pl.pallas_call(
        inverse_factor_kernel,
        out_shape=jax.ShapeDtypeStruct((size, size), F32),
        in_specs=[pl.BlockSpec(memory_space=pltpu.VMEM)],
        out_specs=pl.BlockSpec(memory_space=pltpu.VMEM),
        scratch_shapes=[pltpu.VMEM((size, size), F32)],
        compiler_params=pltpu.CompilerParams(vmem_limit_bytes=32 << 20),
        cost_estimate=pl.CostEstimate(
            flops=40 * size**3, bytes_accessed=8 * size * size, transcendentals=size
        ),
        name="inverse_factor",
    )(gram)


def split(value):
    high = lax.reduce_precision(value, 8, 7)
    return high.astype(BF16), (value - high).astype(BF16)


def dot(left, right, dims=((1,), (0,))):
    return lax.dot_general(left, right, (dims, ((), ())), preferred_element_type=F32)


def local(activations, out_grads, valid_len, weight, sketch):
    width = activations.shape[2]
    rows_here, cols_here = weight.shape
    rank = sketch.shape[1]
    row_count, col_count = lax.axis_size("row"), lax.axis_size("col")
    row, col = lax.axis_index("row"), lax.axis_index("col")
    own_rows, own_cols = rows_here // col_count, cols_here // row_count
    over_col, over_row = Halving("col"), Halving("row")

    raw = dot(weight, sketch).reshape(col_count, own_rows, rank)
    raw = over_col.scatter_sum(raw)

    mass = local_mass(activations, out_grads, valid_len)
    fisher = sum_everywhere(mass.reshape(-1, 128)).reshape(width)
    mean = jnp.sum(fisher) / width + 1e-06
    square_scale = lax.dynamic_slice_in_dim(fisher, row * rows_here, rows_here) / mean
    own_square = lax.dynamic_slice_in_dim(square_scale, col * own_rows, own_rows)

    first = (own_square[:, None] * raw).astype(BF16)
    first = over_col.in_order(over_col.gather(first))

    parts = dot(weight, first, ((0,), (0,))).astype(BF16).reshape(row_count, own_cols, rank)
    projected = over_row.scatter_sum(parts).astype(BF16)
    projected = over_row.in_order(over_row.gather(projected))

    second = dot(weight, projected).reshape(col_count, own_rows, rank)
    second = over_col.scatter_sum(second).astype(BF16)
    second = over_col.in_order(over_col.gather(second))

    weighted = square_scale[:, None] * second.astype(F32)
    high, low = split(weighted)
    half = rank // 2
    cut = lambda value: lax.dynamic_slice_in_dim(value, (col & 1) * half, half, 1)
    gram = dot(cut(high), second, ((0,), (0,))) + dot(cut(low), second, ((0,), (0,)))
    gram = sum_everywhere(gram, col=False)
    other = swap(gram, lambda parity: 0, lambda parity: 1)
    even = (col & 1) == 0
    gram = jnp.concatenate([jnp.where(even, gram, other), jnp.where(even, other, gram)])

    inverse = inverse_factor(gram)
    inv_high, inv_low = split(inverse)
    nt = ((1,), (1,))
    group_basis = dot(second, inv_high, nt) + dot(second, inv_low, nt)
    parts = dot((square_scale[:, None] * group_basis).astype(BF16), weight, ((0,), (0,)))
    coeffs = over_row.scatter_sum(parts.astype(BF16).reshape(row_count, -1, cols_here))
    own_basis = lax.dynamic_slice_in_dim(group_basis, col * own_rows, own_rows)
    basis = own_basis * (jnp.sqrt(own_square)[:, None] * math.sqrt(width))
    return basis, coeffs * math.sqrt(cols_here * col_count)


def solution(mesh):
    placed = (
        P("row", None, None),
        P("row", None, "col"),
        P("row"),
        P("row", "col"),
        P("col", None),
    )
    return jax.shard_map(
        local,
        mesh=mesh,
        in_specs=placed,
        out_specs=(P(("row", "col"), None), P("row", "col")),
        check_vma=False,
    )
```

```python
import functools
import math

import jax
import jax.numpy as jnp
from jax import lax
from jax.experimental import pallas as pl
from jax.experimental.pallas import tpu as pltpu
from jax.sharding import PartitionSpec as P

AXES = ("row", "col")
F32 = jnp.float32
BF16 = jnp.bfloat16


def swap(block, row_bit, col_bit):
    rows, cols = lax.axis_size("row"), lax.axis_size("col")
    pairs = []
    for row in range(rows):
        for col in range(cols):
            other = (row ^ row_bit(col & 1)) * cols + (col ^ col_bit(col & 1))
            pairs.append((row * cols + col, other))
    return lax.ppermute(block, AXES, pairs)


class Halving:
    def __init__(self, axis):
        self.axis = axis
        self.size = lax.axis_size(axis)
        bits = list(range(self.size.bit_length() - 1))
        if axis == "col":
            self.orders = (bits, bits[:1] + bits[:0:-1])
        else:
            self.orders = (bits, bits[::-1])
        self.me = lax.axis_index(axis)
        self.odd = lax.axis_index("col") & 1
        steps = len(bits)
        self.masks = tuple(
            [
                sum(1 << order[t] for t in range(steps) if v >> (steps - 1 - t) & 1)
                for v in range(self.size)
            ]
            for order in self.orders
        )
        if axis == "col":
            half = self.size // 2
            even, odd = (masks[:half] for masks in self.masks)
            self.masks = (even + [1 ^ mask for mask in odd], odd + [1 ^ mask for mask in even])

    def block(self, v):
        even, odd = (masks[v] for masks in self.masks)
        return self.me ^ (even if even == odd else jnp.where(self.odd == 0, even, odd))

    def step(self, t, block):
        even, odd = (1 << order[t] for order in self.orders)
        pick = lambda parity: odd if parity else even
        none = lambda parity: 0
        return swap(block, *((none, pick) if self.axis == "col" else (pick, none)))

    def sending_first(self):
        half = self.size // 2
        places = [*range(half, self.size), *range(half)]
        return jnp.stack([self.block(v) for v in places]).astype(jnp.int32)

    def scatter_sum(self, send, keep):
        for t in range(len(self.orders[0])):
            now = keep.astype(F32) + self.step(t, send).astype(F32)
            half = now.shape[0] // 2
            send, keep = now[half:].astype(BF16), now[:half]
        return keep[0] if keep.shape[0] else now[0]

    def gather(self, own):
        now = own[None]
        for t in reversed(range(len(self.orders[0]))):
            came = self.step(t, now)
            if t:
                now = jnp.concatenate([now, came])
        return now, came

    def in_order(self, halves, axis):
        virtual = jnp.concatenate(halves)
        places = []
        for masks in self.masks:
            inverse = [0] * self.size
            for v, mask in enumerate(masks):
                inverse[mask] = v
            places.append(jnp.array(inverse, jnp.int32))
        place = jnp.where(self.odd == 0, places[0], places[1])
        take = lambda j: lax.dynamic_index_in_dim(
            virtual, place[self.me ^ j], 0, keepdims=False
        )
        return jnp.concatenate([take(j) for j in range(self.size)], axis)


def sum_everywhere(value, row=True, col=True):
    none = lambda parity: 0
    if col:
        for bit in range(lax.axis_size("col").bit_length() - 1):
            value = value + swap(value, none, lambda parity: 1 << bit)
    if row:
        steps = lax.axis_size("row").bit_length() - 1
        for t in range(steps):
            pick = lambda parity: 1 << (steps - 1 - t if parity else t)
            value = value + swap(value, pick, none)
    return value


def token_gram_kernel(valid_ref, grads_ref, high_ref, low_ref, scale_ref):
    seq = pl.program_id(0)
    length = grads_ref.shape[1]
    tokens = lax.broadcasted_iota(jnp.int32, (length, 1), 0)
    grads = grads_ref[0].astype(F32)
    grads = jnp.where(tokens < valid_ref[seq], grads, 0.0)
    largest = jnp.max(jnp.abs(grads), axis=1, keepdims=True)
    scale = jnp.ones_like(largest)
    shrink = jnp.ones_like(largest)
    for power in (16, 48, 80):
        step = 2.0 ** (power + 16)
        high, low = largest >= 2.0**power, largest < 2.0**-power
        scale = jnp.where(high, step, jnp.where(low, 1.0 / step, scale))
        shrink = jnp.where(high, 1.0 / step, jnp.where(low, step, shrink))
    near = (grads * shrink).astype(BF16)
    gram = lax.dot_general(near, near, (((1,), (1,)), ((), ())), preferred_element_type=F32)
    high = gram.astype(BF16)
    high_ref[0] = high
    low_ref[0] = (gram - high.astype(F32)).astype(BF16)
    scale_ref[0] = jnp.broadcast_to(scale, (length, 128))


def row_mass_kernel(acts_ref, high_ref, low_ref, scale_ref, mass_ref):
    total = jnp.zeros((1, acts_ref.shape[2]), F32)
    for seq in range(acts_ref.shape[0]):
        acts = acts_ref[seq].astype(F32) * scale_ref[seq][:, :1]
        short = acts.astype(BF16)
        spread = jnp.dot(high_ref[seq], short, preferred_element_type=F32)
        spread = spread + jnp.dot(low_ref[seq], short, preferred_element_type=F32)
        total = total + jnp.sum(spread * acts, axis=0, keepdims=True)
    mass_ref[...] = total


def local_mass(activations, out_grads, valid_len):
    seqs, length, width = activations.shape
    cols = out_grads.shape[2]
    square = jax.ShapeDtypeStruct((seqs, length, length), BF16)
    whole = lambda seq, valid: (seq, 0, 0)
    high, low, scale = pl.pallas_call(
        token_gram_kernel,
        out_shape=(square, square, jax.ShapeDtypeStruct((seqs, length, 128), F32)),
        grid_spec=pltpu.PrefetchScalarGridSpec(
            num_scalar_prefetch=1,
            grid=(seqs,),
            in_specs=[pl.BlockSpec((1, length, cols), whole)],
            out_specs=(
                pl.BlockSpec((1, length, length), whole),
                pl.BlockSpec((1, length, length), whole),
                pl.BlockSpec((1, length, 128), whole),
            ),
        ),
        compiler_params=pltpu.CompilerParams(vmem_limit_bytes=48 << 20),
        cost_estimate=pl.CostEstimate(
            flops=2 * seqs * length * length * cols,
            bytes_accessed=2 * out_grads.size,
            transcendentals=0,
        ),
        name="token_gram",
    )(valid_len, out_grads)
    tile = math.gcd(width, 1024)
    fixed = lambda i: (0, 0, 0)
    mass = pl.pallas_call(
        row_mass_kernel,
        out_shape=jax.ShapeDtypeStruct((1, width), F32),
        grid=(width // tile,),
        in_specs=[
            pl.BlockSpec((seqs, length, tile), lambda i: (0, 0, i)),
            pl.BlockSpec((seqs, length, length), fixed),
            pl.BlockSpec((seqs, length, length), fixed),
            pl.BlockSpec((seqs, length, 128), fixed),
        ],
        out_specs=pl.BlockSpec((1, tile), lambda i: (0, i)),
        compiler_params=pltpu.CompilerParams(vmem_limit_bytes=48 << 20),
        cost_estimate=pl.CostEstimate(
            flops=4 * seqs * length * length * width,
            bytes_accessed=2 * activations.size,
            transcendentals=0,
        ),
        name="row_mass",
    )(activations, high, low, scale)
    return mass.reshape(width)


def invert_block(tile):
    size = tile.shape[0]
    groups = [tile[i : i + 8] for i in range(0, size, 8)]
    lane = lax.broadcasted_iota(jnp.int32, (8, size), 1)
    sub = lax.broadcasted_iota(jnp.int32, (8, size), 0)
    done = []
    for g in range(size // 8):
        base = 8 * g
        inside = (lane >= base) & (lane < base + 8)
        now = groups[g]
        column = [jnp.broadcast_to(now[:, base + j : base + j + 1], (8, size)) for j in range(8)]
        now = jnp.where(inside, jnp.where(lane - base == sub, 1.0, 0.0), now)
        out = jnp.zeros((8, size), F32)
        for k in range(8):
            here = sub == k
            pivot = jnp.broadcast_to(column[k][k : k + 1], (8, size))
            row = jnp.broadcast_to(now[k : k + 1], (8, size))
            out = jnp.where(here, row * lax.rsqrt(pivot), out)
            inverse = 1.0 / pivot
            row = row * inverse
            now = jnp.where(here, row, now - column[k] * row)
            for j in range(k + 1, 8):
                part = jnp.broadcast_to(column[j][k : k + 1], (8, size)) * inverse
                column[j] = jnp.where(here, part, column[j] - column[k] * part)
        done.append(jnp.where(lane < base + 8, out, 0.0))
        rows = [jnp.broadcast_to(now[s : s + 1], (8, size)) for s in range(8)]
        for i in range(g + 1, size // 8):
            left = groups[i]
            kept = jnp.where(inside, 0.0, left)
            for s in range(8):
                weight = jnp.broadcast_to(left[:, base + s : base + s + 1], (8, size))
                kept = kept - weight * rows[s]
            groups[i] = kept
    return jnp.concatenate(done)


def inverse_factor_kernel(gram_ref, out_ref, work_ref):
    size = gram_ref.shape[0]
    block = 128
    count = size // block
    work_ref[...] = gram_ref[...]
    lane = lax.broadcasted_iota(jnp.int32, (block, size), 1)

    def step(k, carry):
        base = pl.multiple_of(k * block, block)
        here = pl.ds(base, block)
        small = invert_block(work_ref[here, here])
        inside = (lane >= base) & (lane < base + block)
        eye = lax.broadcasted_iota(jnp.int32, (block, size), 0) == lane - base
        rows = jnp.where(inside, jnp.where(eye, 1.0, 0.0), work_ref[here, :])
        rows = jnp.dot(small, rows, precision=lax.Precision.HIGHEST, preferred_element_type=F32)
        out_ref[here, :] = jnp.where(lane < base + block, rows, 0.0)
        work_ref[here, :] = rows

        def update(i, carry):
            there = pl.ds(pl.multiple_of(i * block, block), block)
            left = work_ref[here, there]
            old = jnp.where(inside, 0.0, work_ref[there, :])
            work_ref[there, :] = old - lax.dot_general(
                left,
                rows,
                (((0,), (0,)), ((), ())),
                precision=lax.Precision.HIGHEST,
                preferred_element_type=F32,
            )
            return carry

        return lax.fori_loop(k + 1, count, update, carry)

    lax.fori_loop(0, count, step, 0)


def inverse_factor(gram):
    size = gram.shape[0]
    return pl.pallas_call(
        inverse_factor_kernel,
        out_shape=jax.ShapeDtypeStruct((size, size), F32),
        in_specs=[pl.BlockSpec(memory_space=pltpu.VMEM)],
        out_specs=pl.BlockSpec(memory_space=pltpu.VMEM),
        scratch_shapes=[pltpu.VMEM((size, size), F32)],
        compiler_params=pltpu.CompilerParams(vmem_limit_bytes=32 << 20),
        cost_estimate=pl.CostEstimate(
            flops=40 * size**3, bytes_accessed=8 * size * size, transcendentals=size
        ),
        name="inverse_factor",
    )(gram)


LIMIT = 56 << 20


def dot(left, right, dims=((1,), (0,))):
    return lax.dot_general(left, right, (dims, ((), ())), preferred_element_type=F32)


NT = ((1,), (1,))


def put(value, send_ref, keep_ref):
    step, half = pl.program_id(0), pl.num_programs(0) // 2

    @pl.when(step < half)
    def _():
        send_ref[0] = value.astype(send_ref.dtype)

    @pl.when(step >= half)
    def _():
        keep_ref[0] = value.astype(keep_ref.dtype)


def halves_out(size, shape, send_type):
    half = size // 2
    dims = (half,) + shape
    shapes = (jax.ShapeDtypeStruct(dims, send_type), jax.ShapeDtypeStruct(dims, F32))
    specs = (
        pl.BlockSpec((1,) + shape, lambda i, *_: (jnp.minimum(i, half - 1), 0, 0)),
        pl.BlockSpec((1,) + shape, lambda i, *_: (jnp.maximum(i - half, 0), 0, 0)),
    )
    return shapes, specs


def join(order_ref, halves, whole_ref, width):
    @pl.when(pl.program_id(0) == 0)
    def _():
        count = halves[0].shape[0]
        for v in range(2 * count):
            block = order_ref[(v + count) % (2 * count)]
            there = pl.ds(pl.multiple_of(block * width, 128), width)
            whole_ref[:, there] = halves[v // count][v % count]


def rows_plain_kernel(rows_ref, weight_ref, right_ref, send_ref, keep_ref):
    put(dot(weight_ref[...], right_ref[...]), send_ref, keep_ref)


def rows_times(weight, right, part, width, rows):
    height, depth = weight.shape
    block = height // rows.size
    shapes, specs = halves_out(rows.size, (block, width), F32)
    return pl.pallas_call(
        rows_plain_kernel,
        out_shape=shapes,
        grid_spec=pltpu.PrefetchScalarGridSpec(
            num_scalar_prefetch=1,
            grid=(rows.size,),
            in_specs=[
                pl.BlockSpec((block, depth), lambda i, order: (order[i], 0)),
                pl.BlockSpec((depth, width), lambda i, order: (0, part)),
            ],
            out_specs=specs,
        ),
        compiler_params=pltpu.CompilerParams(vmem_limit_bytes=LIMIT),
        cost_estimate=pl.CostEstimate(
            flops=2 * height * depth * width,
            bytes_accessed=2 * (height + width) * depth,
            transcendentals=0,
        ),
        name="rows_times",
    )(rows.sending_first(), weight, right)


def rows_joined_kernel(rows_ref, cols_ref, weight_ref, first_ref, second_ref, send_ref, keep_ref, whole_ref):
    join(cols_ref, (first_ref, second_ref), whole_ref, first_ref.shape[2])
    put(dot(weight_ref[...], whole_ref[...], NT), send_ref, keep_ref)


def rows_times_joined(weight, halves, rows, cols):
    height, depth = weight.shape
    block = height // rows.size
    width, own = halves[0].shape[1:]
    if own % 128:
        right = cols.in_order(halves, 1)
        return rows_times(weight, right.T, 0, width, rows)
    shapes, specs = halves_out(rows.size, (block, width), F32)
    fixed = pl.BlockSpec(halves[0].shape, lambda i, *_: (0, 0, 0))
    return pl.pallas_call(
        rows_joined_kernel,
        out_shape=shapes,
        grid_spec=pltpu.PrefetchScalarGridSpec(
            num_scalar_prefetch=2,
            grid=(rows.size,),
            in_specs=[pl.BlockSpec((block, depth), lambda i, order, _: (order[i], 0)), fixed, fixed],
            out_specs=specs,
            scratch_shapes=[pltpu.VMEM((width, depth), BF16)],
        ),
        compiler_params=pltpu.CompilerParams(vmem_limit_bytes=LIMIT),
        cost_estimate=pl.CostEstimate(
            flops=2 * height * depth * width,
            bytes_accessed=2 * (height + width) * depth,
            transcendentals=0,
        ),
        name="rows_times_joined",
    )(rows.sending_first(), cols.sending_first(), weight, *halves)


def cols_kernel(cols_ref, rows_ref, weight_ref, first_ref, second_ref, send_ref, keep_ref, whole_ref):
    join(rows_ref, (first_ref, second_ref), whole_ref, first_ref.shape[2])
    put(dot(whole_ref[...], weight_ref[...]), send_ref, keep_ref)


def cols_times_joined(weight, halves, rows, cols):
    height, depth = weight.shape
    block = depth // cols.size
    width, own = halves[0].shape[1:]
    if own % 128 or block % 128:
        full = dot(rows.in_order(halves, 1), weight).reshape(width, cols.size, block)
        order = cols.sending_first()
        full = jnp.stack([full[:, order[i]] for i in range(cols.size)])
        return full[: cols.size // 2].astype(BF16), full[cols.size // 2 :]
    shapes, specs = halves_out(cols.size, (width, block), BF16)
    fixed = pl.BlockSpec(halves[0].shape, lambda i, *_: (0, 0, 0))
    return pl.pallas_call(
        cols_kernel,
        out_shape=shapes,
        grid_spec=pltpu.PrefetchScalarGridSpec(
            num_scalar_prefetch=2,
            grid=(cols.size,),
            in_specs=[pl.BlockSpec((height, block), lambda i, order, _: (0, order[i])), fixed, fixed],
            out_specs=specs,
            scratch_shapes=[pltpu.VMEM((width, height), BF16)],
        ),
        compiler_params=pltpu.CompilerParams(vmem_limit_bytes=LIMIT),
        cost_estimate=pl.CostEstimate(
            flops=2 * height * depth * width,
            bytes_accessed=2 * (height + width) * depth,
            transcendentals=0,
        ),
        name="cols_times_joined",
    )(cols.sending_first(), rows.sending_first(), weight, *halves)


def rank_kernel(rank_ref, rows_ref, weight_ref, basis_ref, out_ref, whole_ref):
    count, _, own = basis_ref.shape
    block = whole_ref.shape[0] // rank_ref.shape[0]

    @pl.when(pl.program_id(0) == 0)
    def _():
        for v in range(count):
            there = pl.ds(pl.multiple_of(rows_ref[(v + count // 2) % count] * own, 128), own)
            for i in range(rank_ref.shape[0]):
                here = pl.ds(pl.multiple_of(rank_ref[i] * block, block), block)
                whole_ref[pl.ds(i * block, block), there] = basis_ref[v, here, :]

    out_ref[...] = dot(whole_ref[...], weight_ref[...]).astype(out_ref.dtype)


def rank_times(weight, basis, ranks, block, rows, out_type):
    height, depth = weight.shape
    count, rank, own = basis.shape
    width = ranks.shape[0] * block
    if own % 128:
        left = rows.in_order((basis[: count // 2], basis[count // 2 :]), 1)
        left = left.reshape(rank // block, block, height)
        left = jnp.concatenate([left[ranks[i]] for i in range(ranks.shape[0])])
        return dot(left, weight).astype(out_type).reshape(ranks.shape[0], block, depth)
    tile = math.gcd(depth, 512)
    out = pl.pallas_call(
        rank_kernel,
        out_shape=jax.ShapeDtypeStruct((width, depth), out_type),
        grid_spec=pltpu.PrefetchScalarGridSpec(
            num_scalar_prefetch=2,
            grid=(depth // tile,),
            in_specs=[
                pl.BlockSpec((height, tile), lambda i, *_: (0, i)),
                pl.BlockSpec(basis.shape, lambda i, *_: (0, 0, 0)),
            ],
            out_specs=pl.BlockSpec((width, tile), lambda i, *_: (0, i)),
            scratch_shapes=[pltpu.VMEM((width, height), BF16)],
        ),
        compiler_params=pltpu.CompilerParams(vmem_limit_bytes=LIMIT),
        cost_estimate=pl.CostEstimate(
            flops=2 * height * depth * width,
            bytes_accessed=2 * (height + width) * depth,
            transcendentals=0,
        ),
        name="rank_times",
    )(ranks, rows.sending_first(), weight, basis)
    return out.reshape(ranks.shape[0], block, depth)


def whiten_kernel(scale_ref, left_ref, right_ref, high_ref, low_ref, out_ref):
    half = left_ref.shape[2]
    total = jnp.zeros(out_ref.shape[1:], F32)
    for part in (high_ref, low_ref):
        total = total + dot(part[:, :half], left_ref[0], NT)
        total = total + dot(part[:, half:], right_ref[0], NT)
    out_ref[0] = (total * scale_ref[0]).astype(BF16)


def whiten(scale, left, right, high, low):
    count, own, half = left.shape
    rank = high.shape[0]
    one = lambda v: (v, 0, 0)
    fixed = lambda v: (0, 0)
    return pl.pallas_call(
        whiten_kernel,
        out_shape=jax.ShapeDtypeStruct((count, rank, own), BF16),
        grid=(count,),
        in_specs=[
            pl.BlockSpec((1, 1, own), one),
            pl.BlockSpec((1, own, half), one),
            pl.BlockSpec((1, own, half), one),
            pl.BlockSpec((rank, rank), fixed),
            pl.BlockSpec((rank, rank), fixed),
        ],
        out_specs=pl.BlockSpec((1, rank, own), one),
        compiler_params=pltpu.CompilerParams(vmem_limit_bytes=LIMIT),
        cost_estimate=pl.CostEstimate(
            flops=4 * rank * rank * count * own,
            bytes_accessed=4 * count * own * rank,
            transcendentals=0,
        ),
        name="whiten",
    )(scale[:, None], left, right, high, low)


def split(value):
    high = lax.reduce_precision(value, 8, 7)
    return high.astype(BF16), (value - high).astype(BF16)


def local(activations, out_grads, valid_len, weight, sketch):
    width = activations.shape[2]
    rows_here, cols_here = weight.shape
    rank = sketch.shape[1]
    half = rank // 2
    row_count, col_count = lax.axis_size("row"), lax.axis_size("col")
    row, col = lax.axis_index("row"), lax.axis_index("col")
    own_rows = rows_here // col_count
    over_col, over_row = Halving("col"), Halving("row")

    mass = local_mass(activations, out_grads, valid_len)
    fisher = sum_everywhere(mass.reshape(-1, 128)).reshape(width)
    mean = jnp.sum(fisher) / width + 1e-06
    square_scale = lax.dynamic_slice_in_dim(fisher, row * rows_here, rows_here) / mean
    square_scale = square_scale.reshape(col_count, own_rows)
    own_square = lax.dynamic_index_in_dim(square_scale, col, 0, keepdims=False)

    def second_of(part):
        raw = over_col.scatter_sum(*rows_times(weight, sketch, part, half, over_col))
        first = (own_square[:, None] * raw).astype(BF16).T
        parts = cols_times_joined(weight, over_col.gather(first), over_col, over_row)
        projected = over_row.gather(over_row.scatter_sum(*parts).astype(BF16))
        parts = rows_times_joined(weight, projected, over_col, over_row)
        return over_col.gather(over_col.scatter_sum(*parts).astype(BF16))

    left, right = (jnp.concatenate(second_of(part)) for part in range(2))
    scale = jnp.stack([square_scale[over_col.block(v)] for v in range(col_count)])

    even = (col & 1) == 0
    mine = jnp.where(even, left, right).astype(F32) * scale[:, :, None]
    pair = ((0, 1), (0, 1))
    gram = [
        sum(dot(term, side, pair) for term in split(mine)) for side in (left, right)
    ]
    gram = sum_everywhere(jnp.concatenate(gram, 1), col=False)
    other = swap(gram, lambda parity: 0, lambda parity: 1)
    gram = jnp.concatenate([jnp.where(even, gram, other), jnp.where(even, other, gram)])

    high, low = split(inverse_factor(gram))
    basis = whiten(scale, left, right, high, low)
    ranks = over_row.sending_first()
    block = rank // row_count
    send = rank_times(weight, basis, ranks[: row_count // 2], block, over_col, BF16)
    keep = rank_times(weight, basis, ranks[row_count // 2 :], block, over_col, F32)
    coeffs = over_row.scatter_sum(send, keep)

    own = lambda side, part: dot(side[0], part, NT)
    basis = sum(own(left, part[:, :half]) + own(right, part[:, half:]) for part in (high, low))
    basis = basis * (jnp.sqrt(own_square)[:, None] * math.sqrt(width))
    return basis, coeffs * math.sqrt(cols_here * col_count)


def solution(mesh):
    placed = (
        P("row", None, None),
        P("row", None, "col"),
        P("row"),
        P("row", "col"),
        P("col", None),
    )
    return jax.shard_map(
        local,
        mesh=mesh,
        in_specs=placed,
        out_specs=(P(("row", "col"), None), P("row", "col")),
        check_vma=False,
    )
```

```python
import functools
import math

import jax
import jax.numpy as jnp
from jax import lax
from jax.experimental import pallas as pl
from jax.experimental.pallas import tpu as pltpu
from jax.sharding import PartitionSpec as P

AXES = ("row", "col")
F32 = jnp.float32
BF16 = jnp.bfloat16


def swap(block, row_bit, col_bit):
    rows, cols = lax.axis_size("row"), lax.axis_size("col")
    pairs = []
    for row in range(rows):
        for col in range(cols):
            other = (row ^ row_bit(col & 1)) * cols + (col ^ col_bit(col & 1))
            pairs.append((row * cols + col, other))
    return lax.ppermute(block, AXES, pairs)


class Halving:
    def __init__(self, axis):
        self.axis = axis
        self.size = lax.axis_size(axis)
        bits = list(range(self.size.bit_length() - 1))
        if axis == "col":
            self.orders = (bits, bits[:1] + bits[:0:-1])
        else:
            self.orders = (bits, bits[::-1])
        self.me = lax.axis_index(axis)
        self.odd = lax.axis_index("col") & 1
        steps = len(bits)
        self.masks = tuple(
            [
                sum(1 << order[t] for t in range(steps) if v >> (steps - 1 - t) & 1)
                for v in range(self.size)
            ]
            for order in self.orders
        )
        if axis == "col":
            half = self.size // 2
            even, odd = (masks[:half] for masks in self.masks)
            self.masks = (even + [1 ^ mask for mask in odd], odd + [1 ^ mask for mask in even])

    def block(self, v):
        even, odd = (masks[v] for masks in self.masks)
        return self.me ^ (even if even == odd else jnp.where(self.odd == 0, even, odd))

    def step(self, t, block):
        even, odd = (1 << order[t] for order in self.orders)
        pick = lambda parity: odd if parity else even
        none = lambda parity: 0
        return swap(block, *((none, pick) if self.axis == "col" else (pick, none)))

    def sending_first(self):
        half = self.size // 2
        places = [*range(half, self.size), *range(half)]
        return jnp.stack([self.block(v) for v in places]).astype(jnp.int32)

    def scatter_sum(self, send, keep):
        for t in range(len(self.orders[0])):
            now = keep.astype(F32) + self.step(t, send).astype(F32)
            half = now.shape[0] // 2
            send, keep = now[half:].astype(BF16), now[:half]
        return keep[0] if keep.shape[0] else now[0]

    def gather(self, own):
        now = own[None]
        for t in reversed(range(len(self.orders[0]))):
            came = self.step(t, now)
            if t:
                now = jnp.concatenate([now, came])
        return now, came

    def in_order(self, halves, axis):
        virtual = jnp.concatenate(halves)
        places = []
        for masks in self.masks:
            inverse = [0] * self.size
            for v, mask in enumerate(masks):
                inverse[mask] = v
            places.append(jnp.array(inverse, jnp.int32))
        place = jnp.where(self.odd == 0, places[0], places[1])
        take = lambda j: lax.dynamic_index_in_dim(
            virtual, place[self.me ^ j], 0, keepdims=False
        )
        return jnp.concatenate([take(j) for j in range(self.size)], axis)


def sum_everywhere(value, row=True, col=True):
    none = lambda parity: 0
    if col:
        for bit in range(lax.axis_size("col").bit_length() - 1):
            value = value + swap(value, none, lambda parity: 1 << bit)
    if row:
        steps = lax.axis_size("row").bit_length() - 1
        for t in range(steps):
            pick = lambda parity: 1 << (steps - 1 - t if parity else t)
            value = value + swap(value, pick, none)
    return value


def token_gram_kernel(valid_ref, grads_ref, gram_ref, scale_ref):
    seq = pl.program_id(0)
    length = grads_ref.shape[1]
    tokens = lax.broadcasted_iota(jnp.int32, (length, 1), 0)
    grads = grads_ref[0].astype(F32)
    grads = jnp.where(tokens < valid_ref[seq], grads, 0.0)
    largest = jnp.max(jnp.abs(grads), axis=1, keepdims=True)
    scale = jnp.ones_like(largest)
    shrink = jnp.ones_like(largest)
    for power in (16, 48, 80):
        step = 2.0 ** (power + 16)
        high, low = largest >= 2.0**power, largest < 2.0**-power
        scale = jnp.where(high, step, jnp.where(low, 1.0 / step, scale))
        shrink = jnp.where(high, 1.0 / step, jnp.where(low, step, shrink))
    near = (grads * shrink).astype(BF16)
    gram = lax.dot_general(near, near, (((1,), (1,)), ((), ())), preferred_element_type=F32)
    high = gram.astype(BF16)
    gram_ref[0, :length] = high
    gram_ref[0, length:] = (gram - high.astype(F32)).astype(BF16)
    scale_ref[0] = jnp.broadcast_to(scale, (length, 128))


def row_mass_kernel(acts_ref, gram_ref, scale_ref, mass_ref):
    length = acts_ref.shape[1]
    total = jnp.zeros((1, acts_ref.shape[2]), F32)
    for seq in range(acts_ref.shape[0]):
        acts = acts_ref[seq].astype(F32) * scale_ref[seq][:, :1]
        spread = jnp.dot(gram_ref[seq], acts.astype(BF16), preferred_element_type=F32)
        spread = spread[:length] + spread[length:]
        total = total + jnp.sum(spread * acts, axis=0, keepdims=True)
    mass_ref[...] = total


def local_mass(activations, out_grads, valid_len):
    seqs, length, width = activations.shape
    cols = out_grads.shape[2]
    whole = lambda seq, valid: (seq, 0, 0)
    gram, scale = pl.pallas_call(
        token_gram_kernel,
        out_shape=(
            jax.ShapeDtypeStruct((seqs, 2 * length, length), BF16),
            jax.ShapeDtypeStruct((seqs, length, 128), F32),
        ),
        grid_spec=pltpu.PrefetchScalarGridSpec(
            num_scalar_prefetch=1,
            grid=(seqs,),
            in_specs=[pl.BlockSpec((1, length, cols), whole)],
            out_specs=(
                pl.BlockSpec((1, 2 * length, length), whole),
                pl.BlockSpec((1, length, 128), whole),
            ),
        ),
        compiler_params=pltpu.CompilerParams(vmem_limit_bytes=48 << 20),
        cost_estimate=pl.CostEstimate(
            flops=2 * seqs * length * length * cols,
            bytes_accessed=2 * out_grads.size,
            transcendentals=0,
        ),
        name="token_gram",
    )(valid_len, out_grads)
    tile = math.gcd(width, 1024)
    fixed = lambda i: (0, 0, 0)
    mass = pl.pallas_call(
        row_mass_kernel,
        out_shape=jax.ShapeDtypeStruct((1, width), F32),
        grid=(width // tile,),
        in_specs=[
            pl.BlockSpec((seqs, length, tile), lambda i: (0, 0, i)),
            pl.BlockSpec((seqs, 2 * length, length), fixed),
            pl.BlockSpec((seqs, length, 128), fixed),
        ],
        out_specs=pl.BlockSpec((1, tile), lambda i: (0, i)),
        compiler_params=pltpu.CompilerParams(vmem_limit_bytes=48 << 20),
        cost_estimate=pl.CostEstimate(
            flops=4 * seqs * length * length * width,
            bytes_accessed=2 * activations.size,
            transcendentals=0,
        ),
        name="row_mass",
    )(activations, gram, scale)
    return mass.reshape(width)


def invert_block(tile):
    size = tile.shape[0]
    groups = [tile[i : i + 8] for i in range(0, size, 8)]
    lane = lax.broadcasted_iota(jnp.int32, (8, size), 1)
    sub = lax.broadcasted_iota(jnp.int32, (8, size), 0)
    done = []
    for g in range(size // 8):
        base = 8 * g
        inside = (lane >= base) & (lane < base + 8)
        now = groups[g]
        column = [jnp.broadcast_to(now[:, base + j : base + j + 1], (8, size)) for j in range(8)]
        now = jnp.where(inside, jnp.where(lane - base == sub, 1.0, 0.0), now)
        out = jnp.zeros((8, size), F32)
        for k in range(8):
            here = sub == k
            pivot = jnp.broadcast_to(column[k][k : k + 1], (8, size))
            row = jnp.broadcast_to(now[k : k + 1], (8, size))
            out = jnp.where(here, row * lax.rsqrt(pivot), out)
            inverse = 1.0 / pivot
            row = row * inverse
            now = jnp.where(here, row, now - column[k] * row)
            for j in range(k + 1, 8):
                part = jnp.broadcast_to(column[j][k : k + 1], (8, size)) * inverse
                column[j] = jnp.where(here, part, column[j] - column[k] * part)
        done.append(jnp.where(lane < base + 8, out, 0.0))
        rows = [jnp.broadcast_to(now[s : s + 1], (8, size)) for s in range(8)]
        for i in range(g + 1, size // 8):
            left = groups[i]
            kept = jnp.where(inside, 0.0, left)
            for s in range(8):
                weight = jnp.broadcast_to(left[:, base + s : base + s + 1], (8, size))
                kept = kept - weight * rows[s]
            groups[i] = kept
    return jnp.concatenate(done)


def inverse_factor_kernel(gram_ref, out_ref, work_ref):
    size = gram_ref.shape[0]
    block = 128
    count = size // block
    work_ref[...] = gram_ref[...]
    lane = lax.broadcasted_iota(jnp.int32, (block, size), 1)

    def step(k, carry):
        base = pl.multiple_of(k * block, block)
        here = pl.ds(base, block)
        small = invert_block(work_ref[here, here])
        inside = (lane >= base) & (lane < base + block)
        eye = lax.broadcasted_iota(jnp.int32, (block, size), 0) == lane - base
        rows = jnp.where(inside, jnp.where(eye, 1.0, 0.0), work_ref[here, :])
        rows = jnp.dot(small, rows, precision=lax.Precision.HIGHEST, preferred_element_type=F32)
        out_ref[here, :] = jnp.where(lane < base + block, rows, 0.0)
        work_ref[here, :] = rows

        def update(i, carry):
            there = pl.ds(pl.multiple_of(i * block, block), block)
            left = work_ref[here, there]
            old = jnp.where(inside, 0.0, work_ref[there, :])
            work_ref[there, :] = old - lax.dot_general(
                left,
                rows,
                (((0,), (0,)), ((), ())),
                precision=lax.Precision.HIGHEST,
                preferred_element_type=F32,
            )
            return carry

        return lax.fori_loop(k + 1, count, update, carry)

    lax.fori_loop(0, count, step, 0)


def inverse_factor(gram):
    size = gram.shape[0]
    return pl.pallas_call(
        inverse_factor_kernel,
        out_shape=jax.ShapeDtypeStruct((size, size), F32),
        in_specs=[pl.BlockSpec(memory_space=pltpu.VMEM)],
        out_specs=pl.BlockSpec(memory_space=pltpu.VMEM),
        scratch_shapes=[pltpu.VMEM((size, size), F32)],
        compiler_params=pltpu.CompilerParams(vmem_limit_bytes=32 << 20),
        cost_estimate=pl.CostEstimate(
            flops=40 * size**3, bytes_accessed=8 * size * size, transcendentals=size
        ),
        name="inverse_factor",
    )(gram)


LIMIT = 56 << 20


def dot(left, right, dims=((1,), (0,))):
    return lax.dot_general(left, right, (dims, ((), ())), preferred_element_type=F32)


NT = ((1,), (1,))


def gather_rows(order_ref, sum_ref, send_ref, keep_ref, turned):
    half = send_ref.shape[0]
    block = sum_ref.shape[0] // (2 * half)
    for i in range(2 * half):
        here = pl.ds(pl.multiple_of(order_ref[i] * block, block), block)
        value = sum_ref[here, :]
        target = send_ref if i < half else keep_ref
        target[i % half] = value.T if turned else value


def add_up(step, term, sum_ref):
    @pl.when(step == 0)
    def _():
        sum_ref[...] = term

    @pl.when(step > 0)
    def _():
        sum_ref[...] += term


def rows_plain_kernel(turned, order_ref, weight_ref, right_ref, send_ref, keep_ref, sum_ref):
    step = pl.program_id(0)
    add_up(step, dot(weight_ref[...], right_ref[...]), sum_ref)

    @pl.when(step == pl.num_programs(0) - 1)
    def _():
        gather_rows(order_ref, sum_ref, send_ref, keep_ref, turned)


def two_halves(size, shape, send_type):
    dims = (size // 2,) + shape
    shapes = (jax.ShapeDtypeStruct(dims, send_type), jax.ShapeDtypeStruct(dims, F32))
    return shapes, (pl.BlockSpec(dims, lambda *_: (0, 0, 0)),) * 2


def rows_times(weight, right, part, width, rows, turned):
    height, depth = weight.shape
    block = height // rows.size
    chunk = 512 if depth % 512 == 0 else depth
    shapes, specs = two_halves(rows.size, (width, block) if turned else (block, width), F32)
    return pl.pallas_call(
        functools.partial(rows_plain_kernel, turned),
        out_shape=shapes,
        grid_spec=pltpu.PrefetchScalarGridSpec(
            num_scalar_prefetch=1,
            grid=(depth // chunk,),
            in_specs=[
                pl.BlockSpec((height, chunk), lambda i, order: (0, i)),
                pl.BlockSpec((chunk, width), lambda i, order: (i, part)),
            ],
            out_specs=specs,
            scratch_shapes=[pltpu.VMEM((height, width), F32)],
        ),
        compiler_params=pltpu.CompilerParams(vmem_limit_bytes=LIMIT),
        cost_estimate=pl.CostEstimate(
            flops=2 * height * depth * width,
            bytes_accessed=2 * (height + width) * depth,
            transcendentals=0,
        ),
        name="rows_times",
    )(rows.sending_first(), weight, right)


def rows_joined_kernel(rows_ref, cols_ref, weight_ref, first_ref, second_ref, send_ref, keep_ref, sum_ref):
    step, steps = pl.program_id(0), pl.num_programs(0)
    right = jnp.where(step < steps // 2, first_ref[0], second_ref[0])
    add_up(step, dot(weight_ref[...], right, NT), sum_ref)

    @pl.when(step == steps - 1)
    def _():
        gather_rows(rows_ref, sum_ref, send_ref, keep_ref, False)


def rows_times_joined(weight, halves, rows, cols):
    height, depth = weight.shape
    block = height // rows.size
    half, width, own = halves[0].shape
    if own % 128:
        return rows_times(weight, cols.in_order(halves, 1).T, 0, width, rows, False)
    shapes, specs = two_halves(rows.size, (block, width), F32)
    return pl.pallas_call(
        rows_joined_kernel,
        out_shape=shapes,
        grid_spec=pltpu.PrefetchScalarGridSpec(
            num_scalar_prefetch=2,
            grid=(cols.size,),
            in_specs=[
                pl.BlockSpec(
                    (height, own), lambda i, _, order: (0, order[(i + half) % (2 * half)])
                ),
                pl.BlockSpec((1, width, own), lambda i, *_: (jnp.minimum(i, half - 1), 0, 0)),
                pl.BlockSpec((1, width, own), lambda i, *_: (jnp.maximum(i - half, 0), 0, 0)),
            ],
            out_specs=specs,
            scratch_shapes=[pltpu.VMEM((height, width), F32)],
        ),
        compiler_params=pltpu.CompilerParams(vmem_limit_bytes=LIMIT),
        cost_estimate=pl.CostEstimate(
            flops=2 * height * depth * width,
            bytes_accessed=2 * (height + width) * depth,
            transcendentals=0,
        ),
        name="rows_times_joined",
    )(rows.sending_first(), cols.sending_first(), weight, *halves)


def put(value, send_ref, keep_ref):
    step, half = pl.program_id(0), pl.num_programs(0) // 2

    @pl.when(step < half)
    def _():
        send_ref[0] = value.astype(send_ref.dtype)

    @pl.when(step >= half)
    def _():
        keep_ref[0] = value.astype(keep_ref.dtype)


def halves_out(size, shape, send_type):
    half = size // 2
    dims = (half,) + shape
    shapes = (jax.ShapeDtypeStruct(dims, send_type), jax.ShapeDtypeStruct(dims, F32))
    specs = (
        pl.BlockSpec((1,) + shape, lambda i, *_: (jnp.minimum(i, half - 1), 0, 0)),
        pl.BlockSpec((1,) + shape, lambda i, *_: (jnp.maximum(i - half, 0), 0, 0)),
    )
    return shapes, specs


def join(order_ref, halves, whole_ref, width):
    @pl.when(pl.program_id(0) == 0)
    def _():
        count = halves[0].shape[0]
        for v in range(2 * count):
            block = order_ref[(v + count) % (2 * count)]
            there = pl.ds(pl.multiple_of(block * width, 128), width)
            whole_ref[:, there] = halves[v // count][v % count]


def cols_kernel(cols_ref, rows_ref, weight_ref, first_ref, second_ref, send_ref, keep_ref, whole_ref):
    join(rows_ref, (first_ref, second_ref), whole_ref, first_ref.shape[2])
    put(dot(whole_ref[...], weight_ref[...]), send_ref, keep_ref)


def cols_times_joined(weight, halves, rows, cols):
    height, depth = weight.shape
    block = depth // cols.size
    width, own = halves[0].shape[1:]
    if own % 128 or block % 128:
        full = dot(rows.in_order(halves, 1), weight).reshape(width, cols.size, block)
        order = cols.sending_first()
        full = jnp.stack([full[:, order[i]] for i in range(cols.size)])
        return full[: cols.size // 2].astype(BF16), full[cols.size // 2 :]
    shapes, specs = halves_out(cols.size, (width, block), BF16)
    fixed = pl.BlockSpec(halves[0].shape, lambda i, *_: (0, 0, 0))
    return pl.pallas_call(
        cols_kernel,
        out_shape=shapes,
        grid_spec=pltpu.PrefetchScalarGridSpec(
            num_scalar_prefetch=2,
            grid=(cols.size,),
            in_specs=[pl.BlockSpec((height, block), lambda i, order, _: (0, order[i])), fixed, fixed],
            out_specs=specs,
            scratch_shapes=[pltpu.VMEM((width, height), BF16)],
        ),
        compiler_params=pltpu.CompilerParams(vmem_limit_bytes=LIMIT),
        cost_estimate=pl.CostEstimate(
            flops=2 * height * depth * width,
            bytes_accessed=2 * (height + width) * depth,
            transcendentals=0,
        ),
        name="cols_times_joined",
    )(cols.sending_first(), rows.sending_first(), weight, *halves)


def settle_kernel(order_ref, *refs):
    out_ref = refs[-1]
    count, block, half = refs[0].shape
    for v in range(2 * count):
        at = order_ref[(v + count) % (2 * count)] * block
        there = pl.ds(pl.multiple_of(at, block), block)
        for part in range(2):
            out_ref[there, part * half : (part + 1) * half] = refs[2 * part + v // count][v % count]


def settle(left, right, rows):
    count, block, half = left[0].shape
    if half % 128 or block % 16:
        return jnp.concatenate([rows.in_order(side, 0) for side in (left, right)], 1)
    vmem = pl.BlockSpec(memory_space=pltpu.VMEM)
    return pl.pallas_call(
        settle_kernel,
        out_shape=jax.ShapeDtypeStruct((2 * count * block, 2 * half), BF16),
        in_specs=[pl.BlockSpec(memory_space=pltpu.SMEM)] + [vmem] * 4,
        out_specs=vmem,
        compiler_params=pltpu.CompilerParams(vmem_limit_bytes=LIMIT),
        cost_estimate=pl.CostEstimate(
            flops=0, bytes_accessed=16 * count * block * half, transcendentals=0
        ),
        name="settle",
    )(rows.sending_first(), *left, *right)


def split(value):
    high = lax.reduce_precision(value, 8, 7)
    return high.astype(BF16), (value - high).astype(BF16)


def local(activations, out_grads, valid_len, weight, sketch):
    width = activations.shape[2]
    rows_here, cols_here = weight.shape
    rank = sketch.shape[1]
    half = rank // 2
    row_count, col_count = lax.axis_size("row"), lax.axis_size("col")
    row, col = lax.axis_index("row"), lax.axis_index("col")
    own_rows = rows_here // col_count
    over_col, over_row = Halving("col"), Halving("row")

    mass = local_mass(activations, out_grads, valid_len)
    mass, sketch = lax.optimization_barrier((mass, sketch))
    fisher = sum_everywhere(mass.reshape(-1, 128)).reshape(width)
    mean = jnp.sum(fisher) / width + 1e-06
    square_scale = lax.dynamic_slice_in_dim(fisher, row * rows_here, rows_here) / mean
    own_square = lax.dynamic_slice_in_dim(square_scale, col * own_rows, own_rows)

    def second_of(part):
        raw = over_col.scatter_sum(*rows_times(weight, sketch, part, half, over_col, True))
        first = (own_square * raw).astype(BF16)
        parts = cols_times_joined(weight, over_col.gather(first), over_col, over_row)
        projected = over_row.gather(over_row.scatter_sum(*parts).astype(BF16))
        parts = rows_times_joined(weight, projected, over_col, over_row)
        return over_col.gather(over_col.scatter_sum(*parts).astype(BF16))

    second = settle(second_of(0), second_of(1), over_col)

    even = (col & 1) == 0
    mine = lax.dynamic_slice_in_dim(second, (col & 1) * half, half, 1).astype(F32)
    rows_of = ((0,), (0,))
    gram = sum(dot(term, second, rows_of) for term in split(square_scale[:, None] * mine))
    gram = sum_everywhere(gram, col=False)
    other = swap(gram, lambda parity: 0, lambda parity: 1)
    gram = jnp.concatenate([jnp.where(even, gram, other), jnp.where(even, other, gram)])

    high, low = split(inverse_factor(gram))
    basis = dot(second, high, NT) + dot(second, low, NT)
    parts = dot((square_scale[:, None] * basis).astype(BF16), weight, rows_of).astype(BF16)
    parts = parts.reshape(row_count, rank // row_count, cols_here)
    order = over_row.sending_first()
    take = lambda places: jnp.stack(
        [lax.dynamic_index_in_dim(parts, order[i], 0, keepdims=False) for i in places]
    )
    coeffs = over_row.scatter_sum(
        take(range(row_count // 2)), take(range(row_count // 2, row_count))
    )

    basis = lax.dynamic_slice_in_dim(basis, col * own_rows, own_rows)
    basis = basis * (jnp.sqrt(own_square)[:, None] * math.sqrt(width))
    return basis, coeffs * math.sqrt(cols_here * col_count)


def solution(mesh):
    placed = (
        P("row", None, None),
        P("row", None, "col"),
        P("row"),
        P("row", "col"),
        P("col", None),
    )
    return jax.shard_map(
        local,
        mesh=mesh,
        in_specs=placed,
        out_specs=(P(("row", "col"), None), P("row", "col")),
        check_vma=False,
    )
```

```python
import functools
import math

import jax
import jax.numpy as jnp
from jax import lax
from jax.experimental import pallas as pl
from jax.experimental.pallas import tpu as pltpu
from jax.sharding import PartitionSpec as P

AXES = ("row", "col")
F32 = jnp.float32
BF16 = jnp.bfloat16


def swap(block, row_bit, col_bit):
    rows, cols = lax.axis_size("row"), lax.axis_size("col")
    pairs = []
    for row in range(rows):
        for col in range(cols):
            other = (row ^ row_bit(col & 1)) * cols + (col ^ col_bit(col & 1))
            pairs.append((row * cols + col, other))
    return lax.ppermute(block, AXES, pairs)


class Halving:
    def __init__(self, axis):
        self.axis = axis
        self.size = lax.axis_size(axis)
        bits = list(range(self.size.bit_length() - 1))
        if axis == "col":
            self.orders = (bits, bits[:1] + bits[:0:-1])
        else:
            self.orders = (bits, bits[::-1])
        self.me = lax.axis_index(axis)
        self.odd = lax.axis_index("col") & 1
        steps = len(bits)
        self.masks = tuple(
            [
                sum(1 << order[t] for t in range(steps) if v >> (steps - 1 - t) & 1)
                for v in range(self.size)
            ]
            for order in self.orders
        )
        if axis == "col":
            half = self.size // 2
            even, odd = (masks[:half] for masks in self.masks)
            self.masks = (even + [1 ^ mask for mask in odd], odd + [1 ^ mask for mask in even])

    def block(self, v):
        even, odd = (masks[v] for masks in self.masks)
        return self.me ^ (even if even == odd else jnp.where(self.odd == 0, even, odd))

    def step(self, t, block):
        even, odd = (1 << order[t] for order in self.orders)
        pick = lambda parity: odd if parity else even
        none = lambda parity: 0
        return swap(block, *((none, pick) if self.axis == "col" else (pick, none)))

    def sending_first(self):
        half = self.size // 2
        places = [*range(half, self.size), *range(half)]
        return jnp.stack([self.block(v) for v in places]).astype(jnp.int32)

    def scatter_sum(self, send, keep):
        for t in range(len(self.orders[0])):
            now = keep.astype(F32) + self.step(t, send).astype(F32)
            half = now.shape[0] // 2
            send, keep = now[half:].astype(BF16), now[:half]
        return keep[0] if keep.shape[0] else now[0]

    def gather(self, own):
        now = own[None]
        for t in reversed(range(len(self.orders[0]))):
            came = self.step(t, now)
            if t:
                now = jnp.concatenate([now, came])
        return now, came

    def in_order(self, halves, axis):
        virtual = jnp.concatenate(halves)
        places = []
        for masks in self.masks:
            inverse = [0] * self.size
            for v, mask in enumerate(masks):
                inverse[mask] = v
            places.append(jnp.array(inverse, jnp.int32))
        place = jnp.where(self.odd == 0, places[0], places[1])
        take = lambda j: lax.dynamic_index_in_dim(
            virtual, place[self.me ^ j], 0, keepdims=False
        )
        return jnp.concatenate([take(j) for j in range(self.size)], axis)


def sum_everywhere(value, row=True, col=True):
    none = lambda parity: 0
    if col:
        for bit in range(lax.axis_size("col").bit_length() - 1):
            value = value + swap(value, none, lambda parity: 1 << bit)
    if row:
        steps = lax.axis_size("row").bit_length() - 1
        for t in range(steps):
            pick = lambda parity: 1 << (steps - 1 - t if parity else t)
            value = value + swap(value, pick, none)
    return value


def token_gram_kernel(valid_ref, grads_ref, gram_ref, scale_ref):
    seq = pl.program_id(0)
    length = grads_ref.shape[1]
    tokens = lax.broadcasted_iota(jnp.int32, (length, 1), 0)
    grads = grads_ref[0].astype(F32)
    grads = jnp.where(tokens < valid_ref[seq], grads, 0.0)
    largest = jnp.max(jnp.abs(grads), axis=1, keepdims=True)
    scale = jnp.ones_like(largest)
    shrink = jnp.ones_like(largest)
    for power in (16, 48, 80):
        step = 2.0 ** (power + 16)
        high, low = largest >= 2.0**power, largest < 2.0**-power
        scale = jnp.where(high, step, jnp.where(low, 1.0 / step, scale))
        shrink = jnp.where(high, 1.0 / step, jnp.where(low, step, shrink))
    near = (grads * shrink).astype(BF16)
    gram = lax.dot_general(near, near, (((1,), (1,)), ((), ())), preferred_element_type=F32)
    high = gram.astype(BF16)
    gram_ref[0, :length] = high
    gram_ref[0, length:] = (gram - high.astype(F32)).astype(BF16)
    scale_ref[0] = jnp.broadcast_to(scale, (length, 128))


def row_mass_kernel(acts_ref, gram_ref, scale_ref, mass_ref):
    length = acts_ref.shape[1]
    total = jnp.zeros((1, acts_ref.shape[2]), F32)
    for seq in range(acts_ref.shape[0]):
        acts = acts_ref[seq].astype(F32) * scale_ref[seq][:, :1]
        spread = jnp.dot(gram_ref[seq], acts.astype(BF16), preferred_element_type=F32)
        spread = spread[:length] + spread[length:]
        total = total + jnp.sum(spread * acts, axis=0, keepdims=True)
    mass_ref[...] = total


def local_mass(activations, out_grads, valid_len):
    seqs, length, width = activations.shape
    cols = out_grads.shape[2]
    whole = lambda seq, valid: (seq, 0, 0)
    gram, scale = pl.pallas_call(
        token_gram_kernel,
        out_shape=(
            jax.ShapeDtypeStruct((seqs, 2 * length, length), BF16),
            jax.ShapeDtypeStruct((seqs, length, 128), F32),
        ),
        grid_spec=pltpu.PrefetchScalarGridSpec(
            num_scalar_prefetch=1,
            grid=(seqs,),
            in_specs=[pl.BlockSpec((1, length, cols), whole)],
            out_specs=(
                pl.BlockSpec((1, 2 * length, length), whole),
                pl.BlockSpec((1, length, 128), whole),
            ),
        ),
        compiler_params=pltpu.CompilerParams(vmem_limit_bytes=LIMIT),
        cost_estimate=pl.CostEstimate(
            flops=2 * seqs * length * length * cols,
            bytes_accessed=2 * out_grads.size,
            transcendentals=0,
        ),
        name="token_gram",
    )(valid_len, out_grads)
    tile = math.gcd(width, 1024)
    fixed = lambda i: (0, 0, 0)
    mass = pl.pallas_call(
        row_mass_kernel,
        out_shape=jax.ShapeDtypeStruct((1, width), F32),
        grid=(width // tile,),
        in_specs=[
            pl.BlockSpec((seqs, length, tile), lambda i: (0, 0, i)),
            pl.BlockSpec((seqs, 2 * length, length), fixed),
            pl.BlockSpec((seqs, length, 128), fixed),
        ],
        out_specs=pl.BlockSpec((1, tile), lambda i: (0, i)),
        compiler_params=pltpu.CompilerParams(vmem_limit_bytes=LIMIT),
        cost_estimate=pl.CostEstimate(
            flops=4 * seqs * length * length * width,
            bytes_accessed=2 * activations.size,
            transcendentals=0,
        ),
        name="row_mass",
    )(activations, gram, scale)
    return mass.reshape(width)


def invert_block(tile):
    size = tile.shape[0]
    groups = [tile[i : i + 8] for i in range(0, size, 8)]
    lane = lax.broadcasted_iota(jnp.int32, (8, size), 1)
    sub = lax.broadcasted_iota(jnp.int32, (8, size), 0)
    done = []
    for g in range(size // 8):
        base = 8 * g
        inside = (lane >= base) & (lane < base + 8)
        now = groups[g]
        column = [jnp.broadcast_to(now[:, base + j : base + j + 1], (8, size)) for j in range(8)]
        now = jnp.where(inside, jnp.where(lane - base == sub, 1.0, 0.0), now)
        out = jnp.zeros((8, size), F32)
        for k in range(8):
            here = sub == k
            pivot = jnp.broadcast_to(column[k][k : k + 1], (8, size))
            row = jnp.broadcast_to(now[k : k + 1], (8, size))
            out = jnp.where(here, row * lax.rsqrt(pivot), out)
            inverse = 1.0 / pivot
            row = row * inverse
            now = jnp.where(here, row, now - column[k] * row)
            for j in range(k + 1, 8):
                part = jnp.broadcast_to(column[j][k : k + 1], (8, size)) * inverse
                column[j] = jnp.where(here, part, column[j] - column[k] * part)
        done.append(jnp.where(lane < base + 8, out, 0.0))
        rows = [jnp.broadcast_to(now[s : s + 1], (8, size)) for s in range(8)]
        for i in range(g + 1, size // 8):
            left = groups[i]
            kept = jnp.where(inside, 0.0, left)
            for s in range(8):
                weight = jnp.broadcast_to(left[:, base + s : base + s + 1], (8, size))
                kept = kept - weight * rows[s]
            groups[i] = kept
    return jnp.concatenate(done)


def inverse_factor_kernel(gram_ref, out_ref, work_ref):
    size = gram_ref.shape[0]
    block = 128
    count = size // block
    work_ref[...] = gram_ref[...]
    lane = lax.broadcasted_iota(jnp.int32, (block, size), 1)

    def step(k, carry):
        base = pl.multiple_of(k * block, block)
        here = pl.ds(base, block)
        small = invert_block(work_ref[here, here])
        inside = (lane >= base) & (lane < base + block)
        eye = lax.broadcasted_iota(jnp.int32, (block, size), 0) == lane - base
        rows = jnp.where(inside, jnp.where(eye, 1.0, 0.0), work_ref[here, :])
        rows = jnp.dot(small, rows, precision=lax.Precision.HIGHEST, preferred_element_type=F32)
        out_ref[here, :] = jnp.where(lane < base + block, rows, 0.0)
        work_ref[here, :] = rows

        def update(i, carry):
            there = pl.ds(pl.multiple_of(i * block, block), block)
            left = work_ref[here, there]
            old = jnp.where(inside, 0.0, work_ref[there, :])
            work_ref[there, :] = old - lax.dot_general(
                left,
                rows,
                (((0,), (0,)), ((), ())),
                precision=lax.Precision.HIGHEST,
                preferred_element_type=F32,
            )
            return carry

        return lax.fori_loop(k + 1, count, update, carry)

    lax.fori_loop(0, count, step, 0)


def inverse_factor(gram):
    size = gram.shape[0]
    return pl.pallas_call(
        inverse_factor_kernel,
        out_shape=jax.ShapeDtypeStruct((size, size), F32),
        in_specs=[pl.BlockSpec(memory_space=pltpu.VMEM)],
        out_specs=pl.BlockSpec(memory_space=pltpu.VMEM),
        scratch_shapes=[pltpu.VMEM((size, size), F32)],
        compiler_params=pltpu.CompilerParams(vmem_limit_bytes=LIMIT),
        cost_estimate=pl.CostEstimate(
            flops=40 * size**3, bytes_accessed=8 * size * size, transcendentals=size
        ),
        name="inverse_factor",
    )(gram)


LIMIT = 24 << 20


def dot(left, right, dims=((1,), (0,))):
    return lax.dot_general(left, right, (dims, ((), ())), preferred_element_type=F32)


NT = ((1,), (1,))


def gather_rows(order_ref, sum_ref, send_ref, keep_ref, turned):
    half = send_ref.shape[0]
    block = sum_ref.shape[0] // (2 * half)
    for i in range(2 * half):
        here = pl.ds(pl.multiple_of(order_ref[i] * block, block), block)
        value = sum_ref[here, :]
        target = send_ref if i < half else keep_ref
        target[i % half] = value.T if turned else value


def add_up(step, term, sum_ref):
    @pl.when(step == 0)
    def _():
        sum_ref[...] = term

    @pl.when(step > 0)
    def _():
        sum_ref[...] += term


def rows_plain_kernel(turned, order_ref, weight_ref, right_ref, send_ref, keep_ref, sum_ref):
    step = pl.program_id(0)
    add_up(step, dot(weight_ref[...], right_ref[...]), sum_ref)

    @pl.when(step == pl.num_programs(0) - 1)
    def _():
        gather_rows(order_ref, sum_ref, send_ref, keep_ref, turned)


def two_halves(size, shape, send_type):
    dims = (size // 2,) + shape
    shapes = (jax.ShapeDtypeStruct(dims, send_type), jax.ShapeDtypeStruct(dims, F32))
    return shapes, (pl.BlockSpec(dims, lambda *_: (0, 0, 0)),) * 2


def rows_times(weight, right, part, width, rows, turned):
    height, depth = weight.shape
    block = height // rows.size
    chunk = 512 if depth % 512 == 0 else depth
    shapes, specs = two_halves(rows.size, (width, block) if turned else (block, width), F32)
    return pl.pallas_call(
        functools.partial(rows_plain_kernel, turned),
        out_shape=shapes,
        grid_spec=pltpu.PrefetchScalarGridSpec(
            num_scalar_prefetch=1,
            grid=(depth // chunk,),
            in_specs=[
                pl.BlockSpec((height, chunk), lambda i, order: (0, i)),
                pl.BlockSpec((chunk, width), lambda i, order: (i, part)),
            ],
            out_specs=specs,
            scratch_shapes=[pltpu.VMEM((height, width), F32)],
        ),
        compiler_params=pltpu.CompilerParams(vmem_limit_bytes=LIMIT),
        cost_estimate=pl.CostEstimate(
            flops=2 * height * depth * width,
            bytes_accessed=2 * (height + width) * depth,
            transcendentals=0,
        ),
        name="rows_times",
    )(rows.sending_first(), weight, right)


def rows_joined_kernel(rows_ref, cols_ref, weight_ref, first_ref, second_ref, send_ref, keep_ref, sum_ref):
    step, steps = pl.program_id(0), pl.num_programs(0)
    right = jnp.where(step < steps // 2, first_ref[0], second_ref[0])
    add_up(step, dot(weight_ref[...], right, NT), sum_ref)

    @pl.when(step == steps - 1)
    def _():
        gather_rows(rows_ref, sum_ref, send_ref, keep_ref, False)


def rows_times_joined(weight, halves, rows, cols):
    height, depth = weight.shape
    block = height // rows.size
    half, width, own = halves[0].shape
    if own % 128:
        return rows_times(weight, cols.in_order(halves, 1).T, 0, width, rows, False)
    shapes, specs = two_halves(rows.size, (block, width), F32)
    return pl.pallas_call(
        rows_joined_kernel,
        out_shape=shapes,
        grid_spec=pltpu.PrefetchScalarGridSpec(
            num_scalar_prefetch=2,
            grid=(cols.size,),
            in_specs=[
                pl.BlockSpec(
                    (height, own), lambda i, _, order: (0, order[(i + half) % (2 * half)])
                ),
                pl.BlockSpec((1, width, own), lambda i, *_: (jnp.minimum(i, half - 1), 0, 0)),
                pl.BlockSpec((1, width, own), lambda i, *_: (jnp.maximum(i - half, 0), 0, 0)),
            ],
            out_specs=specs,
            scratch_shapes=[pltpu.VMEM((height, width), F32)],
        ),
        compiler_params=pltpu.CompilerParams(vmem_limit_bytes=LIMIT),
        cost_estimate=pl.CostEstimate(
            flops=2 * height * depth * width,
            bytes_accessed=2 * (height + width) * depth,
            transcendentals=0,
        ),
        name="rows_times_joined",
    )(rows.sending_first(), cols.sending_first(), weight, *halves)


def put(value, send_ref, keep_ref):
    step, half = pl.program_id(0), pl.num_programs(0) // 2

    @pl.when(step < half)
    def _():
        send_ref[0] = value.astype(send_ref.dtype)

    @pl.when(step >= half)
    def _():
        keep_ref[0] = value.astype(keep_ref.dtype)


def halves_out(size, shape, send_type):
    half = size // 2
    dims = (half,) + shape
    shapes = (jax.ShapeDtypeStruct(dims, send_type), jax.ShapeDtypeStruct(dims, F32))
    specs = (
        pl.BlockSpec((1,) + shape, lambda i, *_: (jnp.minimum(i, half - 1), 0, 0)),
        pl.BlockSpec((1,) + shape, lambda i, *_: (jnp.maximum(i - half, 0), 0, 0)),
    )
    return shapes, specs


def join(order_ref, halves, whole_ref, width):
    @pl.when(pl.program_id(0) == 0)
    def _():
        count = halves[0].shape[0]
        for v in range(2 * count):
            block = order_ref[(v + count) % (2 * count)]
            there = pl.ds(pl.multiple_of(block * width, 128), width)
            whole_ref[:, there] = halves[v // count][v % count]


def cols_kernel(cols_ref, rows_ref, weight_ref, first_ref, second_ref, send_ref, keep_ref, whole_ref):
    join(rows_ref, (first_ref, second_ref), whole_ref, first_ref.shape[2])
    put(dot(whole_ref[...], weight_ref[...]), send_ref, keep_ref)


def cols_times_joined(weight, halves, rows, cols):
    height, depth = weight.shape
    block = depth // cols.size
    width, own = halves[0].shape[1:]
    if own % 128 or block % 128:
        full = dot(rows.in_order(halves, 1), weight).reshape(width, cols.size, block)
        order = cols.sending_first()
        full = jnp.stack([full[:, order[i]] for i in range(cols.size)])
        return full[: cols.size // 2].astype(BF16), full[cols.size // 2 :]
    shapes, specs = halves_out(cols.size, (width, block), BF16)
    fixed = pl.BlockSpec(halves[0].shape, lambda i, *_: (0, 0, 0))
    return pl.pallas_call(
        cols_kernel,
        out_shape=shapes,
        grid_spec=pltpu.PrefetchScalarGridSpec(
            num_scalar_prefetch=2,
            grid=(cols.size,),
            in_specs=[pl.BlockSpec((height, block), lambda i, order, _: (0, order[i])), fixed, fixed],
            out_specs=specs,
            scratch_shapes=[pltpu.VMEM((width, height), BF16)],
        ),
        compiler_params=pltpu.CompilerParams(vmem_limit_bytes=LIMIT),
        cost_estimate=pl.CostEstimate(
            flops=2 * height * depth * width,
            bytes_accessed=2 * (height + width) * depth,
            transcendentals=0,
        ),
        name="cols_times_joined",
    )(cols.sending_first(), rows.sending_first(), weight, *halves)


def settle_kernel(order_ref, *refs):
    out_ref = refs[-1]
    count, block, half = refs[0].shape
    for v in range(2 * count):
        at = order_ref[(v + count) % (2 * count)] * block
        there = pl.ds(pl.multiple_of(at, block), block)
        for part in range(2):
            out_ref[there, part * half : (part + 1) * half] = refs[2 * part + v // count][v % count]


def settle(left, right, rows):
    count, block, half = left[0].shape
    if half % 128 or block % 16:
        return jnp.concatenate([rows.in_order(side, 0) for side in (left, right)], 1)
    vmem = pl.BlockSpec(memory_space=pltpu.VMEM)
    return pl.pallas_call(
        settle_kernel,
        out_shape=jax.ShapeDtypeStruct((2 * count * block, 2 * half), BF16),
        in_specs=[pl.BlockSpec(memory_space=pltpu.SMEM)] + [vmem] * 4,
        out_specs=vmem,
        compiler_params=pltpu.CompilerParams(vmem_limit_bytes=LIMIT),
        cost_estimate=pl.CostEstimate(
            flops=0, bytes_accessed=16 * count * block * half, transcendentals=0
        ),
        name="settle",
    )(rows.sending_first(), *left, *right)


def split(value):
    high = lax.reduce_precision(value, 8, 7)
    return high.astype(BF16), (value - high).astype(BF16)


def local(activations, out_grads, valid_len, weight, sketch):
    width = activations.shape[2]
    rows_here, cols_here = weight.shape
    rank = sketch.shape[1]
    half = rank // 2
    row_count, col_count = lax.axis_size("row"), lax.axis_size("col")
    row, col = lax.axis_index("row"), lax.axis_index("col")
    own_rows = rows_here // col_count
    over_col, over_row = Halving("col"), Halving("row")

    mass = local_mass(activations, out_grads, valid_len)
    mass, sketch = lax.optimization_barrier((mass, sketch))
    fisher = sum_everywhere(mass.reshape(-1, 128)).reshape(width)
    mean = jnp.sum(fisher) / width + 1e-06
    square_scale = lax.dynamic_slice_in_dim(fisher, row * rows_here, rows_here) / mean
    own_square = lax.dynamic_slice_in_dim(square_scale, col * own_rows, own_rows)

    def second_of(part):
        raw = over_col.scatter_sum(*rows_times(weight, sketch, part, half, over_col, True))
        first = (own_square * raw).astype(BF16)
        parts = cols_times_joined(weight, over_col.gather(first), over_col, over_row)
        projected = over_row.gather(over_row.scatter_sum(*parts).astype(BF16))
        parts = rows_times_joined(weight, projected, over_col, over_row)
        return over_col.gather(over_col.scatter_sum(*parts).astype(BF16))

    second = settle(second_of(0), second_of(1), over_col)

    even = (col & 1) == 0
    mine = lax.dynamic_slice_in_dim(second, (col & 1) * half, half, 1).astype(F32)
    rows_of = ((0,), (0,))
    gram = sum(dot(term, second, rows_of) for term in split(square_scale[:, None] * mine))
    gram = sum_everywhere(gram, col=False)
    other = swap(gram, lambda parity: 0, lambda parity: 1)
    gram = jnp.concatenate([jnp.where(even, gram, other), jnp.where(even, other, gram)])

    high, low = split(inverse_factor(gram))
    basis = dot(second, high, NT) + dot(second, low, NT)
    parts = dot((square_scale[:, None] * basis).astype(BF16), weight, rows_of).astype(BF16)
    parts = parts.reshape(row_count, rank // row_count, cols_here)
    order = over_row.sending_first()
    take = lambda places: jnp.stack(
        [lax.dynamic_index_in_dim(parts, order[i], 0, keepdims=False) for i in places]
    )
    coeffs = over_row.scatter_sum(
        take(range(row_count // 2)), take(range(row_count // 2, row_count))
    )

    basis = lax.dynamic_slice_in_dim(basis, col * own_rows, own_rows)
    basis = basis * (jnp.sqrt(own_square)[:, None] * math.sqrt(width))
    return basis, coeffs * math.sqrt(cols_here * col_count)


def solution(mesh):
    placed = (
        P("row", None, None),
        P("row", None, "col"),
        P("row"),
        P("row", "col"),
        P("col", None),
    )
    return jax.shard_map(
        local,
        mesh=mesh,
        in_specs=placed,
        out_specs=(P(("row", "col"), None), P("row", "col")),
        check_vma=False,
    )
```

```python
import functools
import math

import jax
import jax.numpy as jnp
from jax import lax
from jax.experimental import pallas as pl
from jax.experimental.pallas import tpu as pltpu
from jax.sharding import PartitionSpec as P

AXES = ("row", "col")
F32 = jnp.float32
BF16 = jnp.bfloat16


def swap(block, row_bit, col_bit):
    rows, cols = lax.axis_size("row"), lax.axis_size("col")
    pairs = []
    for row in range(rows):
        for col in range(cols):
            other = (row ^ row_bit(col & 1)) * cols + (col ^ col_bit(col & 1))
            pairs.append((row * cols + col, other))
    return lax.ppermute(block, AXES, pairs)


class Halving:
    def __init__(self, axis):
        self.axis = axis
        self.size = lax.axis_size(axis)
        bits = list(range(self.size.bit_length() - 1))
        if axis == "col":
            self.orders = (bits, bits[:1] + bits[:0:-1])
        else:
            self.orders = (bits, bits[::-1])
        self.me = lax.axis_index(axis)
        self.odd = lax.axis_index("col") & 1
        steps = len(bits)
        self.masks = tuple(
            [
                sum(1 << order[t] for t in range(steps) if v >> (steps - 1 - t) & 1)
                for v in range(self.size)
            ]
            for order in self.orders
        )
        if axis == "col":
            half = self.size // 2
            even, odd = (masks[:half] for masks in self.masks)
            self.masks = (even + [1 ^ mask for mask in odd], odd + [1 ^ mask for mask in even])

    def block(self, v):
        even, odd = (masks[v] for masks in self.masks)
        return self.me ^ (even if even == odd else jnp.where(self.odd == 0, even, odd))

    def step(self, t, block):
        even, odd = (1 << order[t] for order in self.orders)
        pick = lambda parity: odd if parity else even
        none = lambda parity: 0
        return swap(block, *((none, pick) if self.axis == "col" else (pick, none)))

    def sending_first(self):
        half = self.size // 2
        places = [*range(half, self.size), *range(half)]
        return jnp.stack([self.block(v) for v in places]).astype(jnp.int32)

    def scatter_sum(self, send, keep):
        for t in range(len(self.orders[0])):
            now = keep.astype(F32) + self.step(t, send).astype(F32)
            half = now.shape[0] // 2
            send, keep = now[half:].astype(BF16), now[:half]
        return keep[0] if keep.shape[0] else now[0]

    def gather(self, own):
        now = own[None]
        for t in reversed(range(len(self.orders[0]))):
            came = self.step(t, now)
            if t:
                now = jnp.concatenate([now, came])
        return now, came

    def in_order(self, halves, axis):
        virtual = jnp.concatenate(halves)
        places = []
        for masks in self.masks:
            inverse = [0] * self.size
            for v, mask in enumerate(masks):
                inverse[mask] = v
            places.append(jnp.array(inverse, jnp.int32))
        place = jnp.where(self.odd == 0, places[0], places[1])
        take = lambda j: lax.dynamic_index_in_dim(
            virtual, place[self.me ^ j], 0, keepdims=False
        )
        return jnp.concatenate([take(j) for j in range(self.size)], axis)


def sum_everywhere(value, row=True, col=True):
    none = lambda parity: 0
    if col:
        for bit in range(lax.axis_size("col").bit_length() - 1):
            value = value + swap(value, none, lambda parity: 1 << bit)
    if row:
        steps = lax.axis_size("row").bit_length() - 1
        for t in range(steps):
            pick = lambda parity: 1 << (steps - 1 - t if parity else t)
            value = value + swap(value, pick, none)
    return value


def token_gram_kernel(valid_ref, grads_ref, gram_ref, scale_ref):
    seq = pl.program_id(0)
    length = grads_ref.shape[1]
    tokens = lax.broadcasted_iota(jnp.int32, (length, 1), 0)
    grads = grads_ref[0].astype(F32)
    grads = jnp.where(tokens < valid_ref[seq], grads, 0.0)
    largest = jnp.max(jnp.abs(grads), axis=1, keepdims=True)
    scale = jnp.ones_like(largest)
    shrink = jnp.ones_like(largest)
    for power in (16, 48, 80):
        step = 2.0 ** (power + 16)
        high, low = largest >= 2.0**power, largest < 2.0**-power
        scale = jnp.where(high, step, jnp.where(low, 1.0 / step, scale))
        shrink = jnp.where(high, 1.0 / step, jnp.where(low, step, shrink))
    near = (grads * shrink).astype(BF16)
    gram = lax.dot_general(near, near, (((1,), (1,)), ((), ())), preferred_element_type=F32)
    high = gram.astype(BF16)
    gram_ref[0, :length] = high
    gram_ref[0, length:] = (gram - high.astype(F32)).astype(BF16)
    scale_ref[0] = jnp.broadcast_to(scale, (length, 128))


def row_mass_kernel(acts_ref, gram_ref, scale_ref, mass_ref):
    length = acts_ref.shape[1]
    total = jnp.zeros((1, acts_ref.shape[2]), F32)
    for seq in range(acts_ref.shape[0]):
        acts = acts_ref[seq].astype(F32) * scale_ref[seq][:, :1]
        spread = jnp.dot(gram_ref[seq], acts.astype(BF16), preferred_element_type=F32)
        spread = spread[:length] + spread[length:]
        total = total + jnp.sum(spread * acts, axis=0, keepdims=True)
    mass_ref[...] = total


def local_mass(activations, out_grads, valid_len):
    seqs, length, width = activations.shape
    cols = out_grads.shape[2]
    whole = lambda seq, valid: (seq, 0, 0)
    gram, scale = pl.pallas_call(
        token_gram_kernel,
        out_shape=(
            jax.ShapeDtypeStruct((seqs, 2 * length, length), BF16),
            jax.ShapeDtypeStruct((seqs, length, 128), F32),
        ),
        grid_spec=pltpu.PrefetchScalarGridSpec(
            num_scalar_prefetch=1,
            grid=(seqs,),
            in_specs=[pl.BlockSpec((1, length, cols), whole)],
            out_specs=(
                pl.BlockSpec((1, 2 * length, length), whole),
                pl.BlockSpec((1, length, 128), whole),
            ),
        ),
        compiler_params=pltpu.CompilerParams(vmem_limit_bytes=LIMIT),
        cost_estimate=pl.CostEstimate(
            flops=2 * seqs * length * length * cols,
            bytes_accessed=2 * out_grads.size,
            transcendentals=0,
        ),
        name="token_gram",
    )(valid_len, out_grads)
    tile = math.gcd(width, 1024)
    fixed = lambda i: (0, 0, 0)
    mass = pl.pallas_call(
        row_mass_kernel,
        out_shape=jax.ShapeDtypeStruct((1, width), F32),
        grid=(width // tile,),
        in_specs=[
            pl.BlockSpec((seqs, length, tile), lambda i: (0, 0, i)),
            pl.BlockSpec((seqs, 2 * length, length), fixed),
            pl.BlockSpec((seqs, length, 128), fixed),
        ],
        out_specs=pl.BlockSpec((1, tile), lambda i: (0, i)),
        compiler_params=pltpu.CompilerParams(vmem_limit_bytes=LIMIT),
        cost_estimate=pl.CostEstimate(
            flops=4 * seqs * length * length * width,
            bytes_accessed=2 * activations.size,
            transcendentals=0,
        ),
        name="row_mass",
    )(activations, gram, scale)
    return mass.reshape(width)


def invert_block(tile):
    size = tile.shape[0]
    groups = [tile[i : i + 8] for i in range(0, size, 8)]
    lane = lax.broadcasted_iota(jnp.int32, (8, size), 1)
    sub = lax.broadcasted_iota(jnp.int32, (8, size), 0)
    done = []
    for g in range(size // 8):
        base = 8 * g
        inside = (lane >= base) & (lane < base + 8)
        now = groups[g]
        column = [jnp.broadcast_to(now[:, base + j : base + j + 1], (8, size)) for j in range(8)]
        now = jnp.where(inside, jnp.where(lane - base == sub, 1.0, 0.0), now)
        out = jnp.zeros((8, size), F32)
        for k in range(8):
            here = sub == k
            pivot = jnp.broadcast_to(column[k][k : k + 1], (8, size))
            row = jnp.broadcast_to(now[k : k + 1], (8, size))
            out = jnp.where(here, row * lax.rsqrt(pivot), out)
            inverse = 1.0 / pivot
            row = row * inverse
            now = jnp.where(here, row, now - column[k] * row)
            for j in range(k + 1, 8):
                part = jnp.broadcast_to(column[j][k : k + 1], (8, size)) * inverse
                column[j] = jnp.where(here, part, column[j] - column[k] * part)
        done.append(jnp.where(lane < base + 8, out, 0.0))
        rows = [jnp.broadcast_to(now[s : s + 1], (8, size)) for s in range(8)]
        for i in range(g + 1, size // 8):
            left = groups[i]
            kept = jnp.where(inside, 0.0, left)
            for s in range(8):
                weight = jnp.broadcast_to(left[:, base + s : base + s + 1], (8, size))
                kept = kept - weight * rows[s]
            groups[i] = kept
    return jnp.concatenate(done)


def inverse_factor_kernel(gram_ref, out_ref, work_ref):
    size = gram_ref.shape[0]
    block = 128
    count = size // block
    work_ref[...] = gram_ref[...]
    lane = lax.broadcasted_iota(jnp.int32, (block, size), 1)

    def step(k, carry):
        base = pl.multiple_of(k * block, block)
        here = pl.ds(base, block)
        small = invert_block(work_ref[here, here])
        inside = (lane >= base) & (lane < base + block)
        eye = lax.broadcasted_iota(jnp.int32, (block, size), 0) == lane - base
        rows = jnp.where(inside, jnp.where(eye, 1.0, 0.0), work_ref[here, :])
        rows = jnp.dot(small, rows, precision=lax.Precision.HIGHEST, preferred_element_type=F32)
        out_ref[here, :] = jnp.where(lane < base + block, rows, 0.0)
        work_ref[here, :] = rows

        def update(i, carry):
            there = pl.ds(pl.multiple_of(i * block, block), block)
            left = work_ref[here, there]
            old = jnp.where(inside, 0.0, work_ref[there, :])
            work_ref[there, :] = old - lax.dot_general(
                left,
                rows,
                (((0,), (0,)), ((), ())),
                precision=lax.Precision.HIGHEST,
                preferred_element_type=F32,
            )
            return carry

        return lax.fori_loop(k + 1, count, update, carry)

    lax.fori_loop(0, count, step, 0)


def inverse_factor(gram):
    size = gram.shape[0]
    return pl.pallas_call(
        inverse_factor_kernel,
        out_shape=jax.ShapeDtypeStruct((size, size), F32),
        in_specs=[pl.BlockSpec(memory_space=pltpu.VMEM)],
        out_specs=pl.BlockSpec(memory_space=pltpu.VMEM),
        scratch_shapes=[pltpu.VMEM((size, size), F32)],
        compiler_params=pltpu.CompilerParams(vmem_limit_bytes=LIMIT),
        cost_estimate=pl.CostEstimate(
            flops=40 * size**3, bytes_accessed=8 * size * size, transcendentals=size
        ),
        name="inverse_factor",
    )(gram)


LIMIT = 24 << 20


def dot(left, right, dims=((1,), (0,))):
    return lax.dot_general(left, right, (dims, ((), ())), preferred_element_type=F32)


NT = ((1,), (1,))


def gather_rows(order_ref, sum_ref, send_ref, keep_ref, turned):
    half = send_ref.shape[0]
    block = sum_ref.shape[0] // (2 * half)
    for i in range(2 * half):
        here = pl.ds(pl.multiple_of(order_ref[i] * block, block), block)
        value = sum_ref[here, :]
        target = send_ref if i < half else keep_ref
        target[i % half] = value.T if turned else value


def add_up(step, term, sum_ref):
    @pl.when(step == 0)
    def _():
        sum_ref[...] = term

    @pl.when(step > 0)
    def _():
        sum_ref[...] += term


def two_halves(size, shape, send_type):
    dims = (size // 2,) + shape
    return (jax.ShapeDtypeStruct(dims, send_type), jax.ShapeDtypeStruct(dims, F32))


def product_call(kernel, name, out_shape, scratch, weight, width, indices, arrays):
    height, depth = weight.shape
    smem, vmem = (pl.BlockSpec(memory_space=space) for space in (pltpu.SMEM, pltpu.VMEM))
    return pl.pallas_call(
        kernel,
        out_shape=out_shape,
        in_specs=[smem] * len(indices) + [vmem] * (1 + len(arrays)),
        out_specs=(vmem, vmem),
        scratch_shapes=[scratch],
        compiler_params=pltpu.CompilerParams(vmem_limit_bytes=LIMIT),
        cost_estimate=pl.CostEstimate(
            flops=2 * height * depth * width,
            bytes_accessed=2 * (height + width) * depth,
            transcendentals=0,
        ),
        name=name,
    )(*indices, weight, *arrays)


def rows_plain_kernel(part, width, turned, order_ref, weight_ref, right_ref, send_ref, keep_ref, sum_ref):
    depth = weight_ref.shape[1]
    chunk = 512 if depth % 512 == 0 else depth

    @pl.loop(0, depth // chunk)
    def _(i):
        here = pl.ds(pl.multiple_of(i * chunk, chunk), chunk)
        right = right_ref[here, part * width : (part + 1) * width]
        add_up(i, dot(weight_ref[:, here], right), sum_ref)

    gather_rows(order_ref, sum_ref, send_ref, keep_ref, turned)


def rows_times(weight, right, part, width, rows, turned):
    height = weight.shape[0]
    block = height // rows.size
    shapes = two_halves(rows.size, (width, block) if turned else (block, width), F32)
    return product_call(
        functools.partial(rows_plain_kernel, part, width, turned),
        "rows_times",
        shapes,
        pltpu.VMEM((height, width), F32),
        weight,
        width,
        (rows.sending_first(),),
        (right,),
    )


def rows_joined_kernel(rows_ref, cols_ref, weight_ref, first_ref, second_ref, send_ref, keep_ref, sum_ref):
    half, _, own = first_ref.shape
    for part, right_ref in enumerate((first_ref, second_ref)):

        @pl.loop(0, half)
        def _(i):
            block = cols_ref[i + half * (1 - part)]
            here = pl.ds(pl.multiple_of(block * own, 128), own)
            term = dot(weight_ref[:, here], right_ref[i], NT)
            add_up(i + half * part, term, sum_ref)

    gather_rows(rows_ref, sum_ref, send_ref, keep_ref, False)


def rows_times_joined(weight, halves, rows, cols):
    height = weight.shape[0]
    width, own = halves[0].shape[1:]
    if own % 128:
        return rows_times(weight, cols.in_order(halves, 1).T, 0, width, rows, False)
    return product_call(
        rows_joined_kernel,
        "rows_times_joined",
        two_halves(rows.size, (height // rows.size, width), F32),
        pltpu.VMEM((height, width), F32),
        weight,
        width,
        (rows.sending_first(), cols.sending_first()),
        halves,
    )


def cols_kernel(
    cols_ref, rows_ref, weight_ref, scale_ref, first_ref, second_ref, send_ref, keep_ref, whole_ref
):
    count, _, own = first_ref.shape
    for v in range(2 * count):
        block = rows_ref[(v + count) % (2 * count)]
        there = pl.ds(pl.multiple_of(block * own, 128), own)
        value = (first_ref, second_ref)[v // count][v % count]
        whole_ref[:, there] = (value.astype(F32) * scale_ref[:, there]).astype(BF16)

    half, _, block = send_ref.shape
    for part, out_ref in enumerate((send_ref, keep_ref)):

        @pl.loop(0, half)
        def _(i):
            here = pl.ds(pl.multiple_of(cols_ref[i + half * part] * block, 128), block)
            out_ref[i] = dot(whole_ref[...], weight_ref[:, here]).astype(out_ref.dtype)


def cols_times_joined(weight, scale, halves, rows, cols):
    height, depth = weight.shape
    block = depth // cols.size
    width, own = halves[0].shape[1:]
    if own % 128 or block % 128:
        left = (scale * rows.in_order(halves, 1)).astype(BF16)
        full = dot(left, weight).reshape(width, cols.size, block)
        order = cols.sending_first()
        full = jnp.stack([full[:, order[i]] for i in range(cols.size)])
        return full[: cols.size // 2].astype(BF16), full[cols.size // 2 :]
    return product_call(
        cols_kernel,
        "cols_times_joined",
        two_halves(cols.size, (width, block), BF16),
        pltpu.VMEM((width, height), BF16),
        weight,
        width,
        (cols.sending_first(), rows.sending_first()),
        (scale[None], *halves),
    )


def settle_kernel(order_ref, *refs):
    out_ref = refs[-1]
    count, block, half = refs[0].shape
    for v in range(2 * count):
        at = order_ref[(v + count) % (2 * count)] * block
        there = pl.ds(pl.multiple_of(at, block), block)
        for part in range(2):
            out_ref[there, part * half : (part + 1) * half] = refs[2 * part + v // count][v % count]


def settle(left, right, rows):
    count, block, half = left[0].shape
    if half % 128 or block % 16:
        return jnp.concatenate([rows.in_order(side, 0) for side in (left, right)], 1)
    vmem = pl.BlockSpec(memory_space=pltpu.VMEM)
    return pl.pallas_call(
        settle_kernel,
        out_shape=jax.ShapeDtypeStruct((2 * count * block, 2 * half), BF16),
        in_specs=[pl.BlockSpec(memory_space=pltpu.SMEM)] + [vmem] * 4,
        out_specs=vmem,
        compiler_params=pltpu.CompilerParams(vmem_limit_bytes=LIMIT),
        cost_estimate=pl.CostEstimate(
            flops=0, bytes_accessed=16 * count * block * half, transcendentals=0
        ),
        name="settle",
    )(rows.sending_first(), *left, *right)


def split(value):
    high = lax.reduce_precision(value, 8, 7)
    return high.astype(BF16), (value - high).astype(BF16)


def local(activations, out_grads, valid_len, weight, sketch):
    width = activations.shape[2]
    rows_here, cols_here = weight.shape
    rank = sketch.shape[1]
    half = rank // 2
    row_count, col_count = lax.axis_size("row"), lax.axis_size("col")
    row, col = lax.axis_index("row"), lax.axis_index("col")
    own_rows = rows_here // col_count
    over_col, over_row = Halving("col"), Halving("row")

    mass = local_mass(activations, out_grads, valid_len)
    fisher = sum_everywhere(mass.reshape(-1, 128)).reshape(width)
    mean = jnp.sum(fisher) / width + 1e-06
    square_scale = lax.dynamic_slice_in_dim(fisher, row * rows_here, rows_here) / mean
    own_square = lax.dynamic_slice_in_dim(square_scale, col * own_rows, own_rows)

    def second_of(part):
        raw = over_col.scatter_sum(*rows_times(weight, sketch, part, half, over_col, True))
        first = over_col.gather(raw.astype(BF16))
        parts = cols_times_joined(weight, square_scale, first, over_col, over_row)
        projected = over_row.gather(over_row.scatter_sum(*parts).astype(BF16))
        parts = rows_times_joined(weight, projected, over_col, over_row)
        return over_col.gather(over_col.scatter_sum(*parts).astype(BF16))

    second = settle(second_of(0), second_of(1), over_col)

    even = (col & 1) == 0
    mine = lax.dynamic_slice_in_dim(second, (col & 1) * half, half, 1).astype(F32)
    rows_of = ((0,), (0,))
    gram = sum(dot(term, second, rows_of) for term in split(square_scale[:, None] * mine))
    gram = sum_everywhere(gram, col=False)
    other = swap(gram, lambda parity: 0, lambda parity: 1)
    gram = jnp.concatenate([jnp.where(even, gram, other), jnp.where(even, other, gram)])

    inverse = inverse_factor(gram)
    order = over_row.sending_first()
    blocks = inverse.reshape(row_count, rank // row_count, rank)

    def coeffs_of(places):
        part = [lax.dynamic_index_in_dim(blocks, order[i], 0, keepdims=False) for i in places]
        high, low = split(jnp.concatenate(part))
        basis = dot(second, high, NT) + dot(second, low, NT)
        parts = dot((square_scale[:, None] * basis).astype(BF16), weight, rows_of)
        return parts.astype(BF16).reshape(len(part), -1, cols_here)

    coeffs = over_row.scatter_sum(
        coeffs_of(range(row_count // 2)), coeffs_of(range(row_count // 2, row_count))
    )

    own = lax.dynamic_slice_in_dim(second, col * own_rows, own_rows)
    basis = sum(dot(own, term, NT) for term in split(inverse))
    basis = basis * (jnp.sqrt(own_square)[:, None] * math.sqrt(width))
    return basis, coeffs * math.sqrt(cols_here * col_count)


def solution(mesh):
    placed = (
        P("row", None, None),
        P("row", None, "col"),
        P("row"),
        P("row", "col"),
        P("col", None),
    )
    return jax.shard_map(
        local,
        mesh=mesh,
        in_specs=placed,
        out_specs=(P(("row", "col"), None), P("row", "col")),
        check_vma=False,
    )
```

```python
import functools
import math

import jax
import jax.numpy as jnp
from jax import lax
from jax.experimental import pallas as pl
from jax.experimental.pallas import tpu as pltpu
from jax.sharding import PartitionSpec as P

AXES = ("row", "col")
F32 = jnp.float32
BF16 = jnp.bfloat16


def swap(block, row_bit, col_bit):
    rows, cols = lax.axis_size("row"), lax.axis_size("col")
    pairs = []
    for row in range(rows):
        for col in range(cols):
            other = (row ^ row_bit(col & 1)) * cols + (col ^ col_bit(col & 1))
            pairs.append((row * cols + col, other))
    return lax.ppermute(block, AXES, pairs)


class Halving:
    def __init__(self, axis):
        self.axis = axis
        self.size = lax.axis_size(axis)
        bits = list(range(self.size.bit_length() - 1))
        if axis == "col":
            self.orders = (bits, bits[:1] + bits[:0:-1])
        else:
            self.orders = (bits, bits[::-1])
        self.me = lax.axis_index(axis)
        self.odd = lax.axis_index("col") & 1
        steps = len(bits)
        self.masks = tuple(
            [
                sum(1 << order[t] for t in range(steps) if v >> (steps - 1 - t) & 1)
                for v in range(self.size)
            ]
            for order in self.orders
        )
        if axis == "col":
            half = self.size // 2
            even, odd = (masks[:half] for masks in self.masks)
            self.masks = (even + [1 ^ mask for mask in odd], odd + [1 ^ mask for mask in even])

    def block(self, v):
        even, odd = (masks[v] for masks in self.masks)
        return self.me ^ (even if even == odd else jnp.where(self.odd == 0, even, odd))

    def step(self, t, block):
        even, odd = (1 << order[t] for order in self.orders)
        pick = lambda parity: odd if parity else even
        none = lambda parity: 0
        return swap(block, *((none, pick) if self.axis == "col" else (pick, none)))

    def sending_first(self):
        half = self.size // 2
        places = [*range(half, self.size), *range(half)]
        return jnp.stack([self.block(v) for v in places]).astype(jnp.int32)

    def scatter_sum(self, send, keep):
        for t in range(len(self.orders[0])):
            now = keep.astype(F32) + self.step(t, send).astype(F32)
            half = now.shape[0] // 2
            send, keep = now[half:].astype(BF16), now[:half]
        return keep[0] if keep.shape[0] else now[0]

    def gather(self, own):
        now = own[None]
        for t in reversed(range(len(self.orders[0]))):
            came = self.step(t, now)
            if t:
                now = jnp.concatenate([now, came])
        return now, came

    def in_order(self, halves, axis):
        virtual = jnp.concatenate(halves)
        places = []
        for masks in self.masks:
            inverse = [0] * self.size
            for v, mask in enumerate(masks):
                inverse[mask] = v
            places.append(jnp.array(inverse, jnp.int32))
        place = jnp.where(self.odd == 0, places[0], places[1])
        take = lambda j: lax.dynamic_index_in_dim(
            virtual, place[self.me ^ j], 0, keepdims=False
        )
        return jnp.concatenate([take(j) for j in range(self.size)], axis)


def sum_everywhere(value, row=True, col=True):
    none = lambda parity: 0
    if col:
        for bit in range(lax.axis_size("col").bit_length() - 1):
            value = value + swap(value, none, lambda parity: 1 << bit)
    if row:
        steps = lax.axis_size("row").bit_length() - 1
        for t in range(steps):
            pick = lambda parity: 1 << (steps - 1 - t if parity else t)
            value = value + swap(value, pick, none)
    return value


def token_gram_kernel(valid_ref, grads_ref, after_ref, weight_ref, gram_ref, scale_ref):
    seq = pl.program_id(0)
    length = grads_ref.shape[1]
    tokens = lax.broadcasted_iota(jnp.int32, (length, 1), 0)
    grads = grads_ref[0].astype(F32)
    grads = jnp.where(tokens < valid_ref[seq], grads, 0.0)
    largest = jnp.max(jnp.abs(grads), axis=1, keepdims=True)
    scale = jnp.ones_like(largest)
    shrink = jnp.ones_like(largest)
    for power in (16, 48, 80):
        step = 2.0 ** (power + 16)
        high, low = largest >= 2.0**power, largest < 2.0**-power
        scale = jnp.where(high, step, jnp.where(low, 1.0 / step, scale))
        shrink = jnp.where(high, 1.0 / step, jnp.where(low, step, shrink))
    near = (grads * shrink).astype(BF16)
    gram = lax.dot_general(near, near, (((1,), (1,)), ((), ())), preferred_element_type=F32)
    high = gram.astype(BF16)
    gram_ref[0, :length] = high
    gram_ref[0, length:] = (gram - high.astype(F32)).astype(BF16)
    scale_ref[0] = jnp.broadcast_to(scale, (length, 128))


def row_mass_kernel(acts_ref, gram_ref, scale_ref, weight_ref, mass_ref):
    length = acts_ref.shape[1]
    total = jnp.zeros((1, acts_ref.shape[2]), F32)
    for seq in range(acts_ref.shape[0]):
        acts = acts_ref[seq].astype(F32) * scale_ref[seq][:, :1]
        spread = jnp.dot(gram_ref[seq], acts.astype(BF16), preferred_element_type=F32)
        spread = spread[:length] + spread[length:]
        total = total + jnp.sum(spread * acts, axis=0, keepdims=True)
    mass_ref[...] = total


def local_mass(activations, out_grads, valid_len, after, weight):
    seqs, length, width = activations.shape
    cols = out_grads.shape[2]
    whole = lambda seq, valid: (seq, 0, 0)
    gram, scale = pl.pallas_call(
        token_gram_kernel,
        out_shape=(
            jax.ShapeDtypeStruct((seqs, 2 * length, length), BF16),
            jax.ShapeDtypeStruct((seqs, length, 128), F32),
        ),
        grid_spec=pltpu.PrefetchScalarGridSpec(
            num_scalar_prefetch=1,
            grid=(seqs,),
            in_specs=[
                pl.BlockSpec((1, length, cols), whole),
                pl.BlockSpec(memory_space=pl.ANY),
                pl.BlockSpec(memory_space=pltpu.VMEM),
            ],
            out_specs=(
                pl.BlockSpec((1, 2 * length, length), whole),
                pl.BlockSpec((1, length, 128), whole),
            ),
        ),
        compiler_params=pltpu.CompilerParams(vmem_limit_bytes=LIMIT),
        cost_estimate=pl.CostEstimate(
            flops=2 * seqs * length * length * cols,
            bytes_accessed=2 * out_grads.size,
            transcendentals=0,
        ),
        name="token_gram",
    )(valid_len, out_grads, after, weight)
    tile = math.gcd(width, 1024)
    fixed = lambda i: (0, 0, 0)
    mass = pl.pallas_call(
        row_mass_kernel,
        out_shape=jax.ShapeDtypeStruct((1, width), F32),
        grid=(width // tile,),
        in_specs=[
            pl.BlockSpec((seqs, length, tile), lambda i: (0, 0, i)),
            pl.BlockSpec((seqs, 2 * length, length), fixed),
            pl.BlockSpec((seqs, length, 128), fixed),
            pl.BlockSpec(memory_space=pltpu.VMEM),
        ],
        out_specs=pl.BlockSpec((1, tile), lambda i: (0, i)),
        compiler_params=pltpu.CompilerParams(vmem_limit_bytes=LIMIT),
        cost_estimate=pl.CostEstimate(
            flops=4 * seqs * length * length * width,
            bytes_accessed=2 * activations.size,
            transcendentals=0,
        ),
        name="row_mass",
    )(activations, gram, scale, weight)
    return mass.reshape(width)


def invert_block(tile):
    size = tile.shape[0]
    groups = [tile[i : i + 8] for i in range(0, size, 8)]
    lane = lax.broadcasted_iota(jnp.int32, (8, size), 1)
    sub = lax.broadcasted_iota(jnp.int32, (8, size), 0)
    done = []
    for g in range(size // 8):
        base = 8 * g
        inside = (lane >= base) & (lane < base + 8)
        now = groups[g]
        column = [jnp.broadcast_to(now[:, base + j : base + j + 1], (8, size)) for j in range(8)]
        now = jnp.where(inside, jnp.where(lane - base == sub, 1.0, 0.0), now)
        out = jnp.zeros((8, size), F32)
        for k in range(8):
            here = sub == k
            pivot = jnp.broadcast_to(column[k][k : k + 1], (8, size))
            row = jnp.broadcast_to(now[k : k + 1], (8, size))
            out = jnp.where(here, row * lax.rsqrt(pivot), out)
            inverse = pl.reciprocal(pivot, approx=True)
            inverse = inverse * (2.0 - pivot * inverse)
            row = row * inverse
            now = jnp.where(here, row, now - column[k] * row)
            for j in range(k + 1, 8):
                part = jnp.broadcast_to(column[j][k : k + 1], (8, size))
                product = column[k] * part
                column[j] = jnp.where(here, part * inverse, column[j] - product * inverse)
        done.append(jnp.where(lane < base + 8, out, 0.0))
        rows = [jnp.broadcast_to(now[s : s + 1], (8, size)) for s in range(8)]
        for i in range(g + 1, size // 8):
            left = groups[i]
            kept = jnp.where(inside, 0.0, left)
            for s in range(8):
                weight = jnp.broadcast_to(left[:, base + s : base + s + 1], (8, size))
                kept = kept - weight * rows[s]
            groups[i] = kept
    return jnp.concatenate(done)


def inverse_factor_kernel(gram_ref, out_ref, work_ref):
    size = gram_ref.shape[0]
    block = 128
    count = size // block
    work_ref[...] = gram_ref[...]
    lane = lax.broadcasted_iota(jnp.int32, (block, size), 1)

    def step(k, carry):
        base = pl.multiple_of(k * block, block)
        here = pl.ds(base, block)
        small = invert_block(work_ref[here, here])
        inside = (lane >= base) & (lane < base + block)
        eye = lax.broadcasted_iota(jnp.int32, (block, size), 0) == lane - base
        rows = jnp.where(inside, jnp.where(eye, 1.0, 0.0), work_ref[here, :])
        rows = jnp.dot(small, rows, precision=lax.Precision.HIGHEST, preferred_element_type=F32)
        out_ref[here, :] = jnp.where(lane < base + block, rows, 0.0)
        work_ref[here, :] = rows

        def update(i, carry):
            there = pl.ds(pl.multiple_of(i * block, block), block)
            left = work_ref[here, there]
            old = jnp.where(inside, 0.0, work_ref[there, :])
            work_ref[there, :] = old - lax.dot_general(
                left,
                rows,
                (((0,), (0,)), ((), ())),
                precision=lax.Precision.HIGHEST,
                preferred_element_type=F32,
            )
            return carry

        return lax.fori_loop(k + 1, count, update, carry)

    lax.fori_loop(0, count, step, 0)


def inverse_factor(gram):
    size = gram.shape[0]
    return pl.pallas_call(
        inverse_factor_kernel,
        out_shape=jax.ShapeDtypeStruct((size, size), F32),
        in_specs=[pl.BlockSpec(memory_space=pltpu.VMEM)],
        out_specs=pl.BlockSpec(memory_space=pltpu.VMEM),
        scratch_shapes=[pltpu.VMEM((size, size), F32)],
        compiler_params=pltpu.CompilerParams(vmem_limit_bytes=LIMIT),
        cost_estimate=pl.CostEstimate(
            flops=40 * size**3, bytes_accessed=8 * size * size, transcendentals=size
        ),
        name="inverse_factor",
    )(gram)


LIMIT = 16 << 20


def dot(left, right, dims=((1,), (0,))):
    return lax.dot_general(left, right, (dims, ((), ())), preferred_element_type=F32)


NT = ((1,), (1,))


def gather_rows(order_ref, sum_ref, send_ref, keep_ref, turned):
    half = send_ref.shape[0]
    block = sum_ref.shape[0] // (2 * half)
    for i in range(2 * half):
        here = pl.ds(pl.multiple_of(order_ref[i] * block, block), block)
        value = sum_ref[here, :]
        target = send_ref if i < half else keep_ref
        target[i % half] = value.T if turned else value


def two_halves(size, shape, send_type):
    dims = (size // 2,) + shape
    return (jax.ShapeDtypeStruct(dims, send_type), jax.ShapeDtypeStruct(dims, F32))


def product_call(kernel, name, out_shape, scratch, weight, width, indices, arrays, after=()):
    height, depth = weight.shape
    smem, vmem = (pl.BlockSpec(memory_space=space) for space in (pltpu.SMEM, pltpu.VMEM))
    return pl.pallas_call(
        lambda *refs: kernel(*refs[len(after) :]),
        out_shape=out_shape,
        in_specs=[pl.BlockSpec(memory_space=pl.ANY)] * len(after)
        + [smem] * len(indices)
        + [vmem] * (1 + len(arrays)),
        out_specs=(vmem, vmem),
        scratch_shapes=[scratch],
        compiler_params=pltpu.CompilerParams(vmem_limit_bytes=LIMIT),
        cost_estimate=pl.CostEstimate(
            flops=2 * height * depth * width,
            bytes_accessed=2 * (height + width) * depth,
            transcendentals=0,
        ),
        name=name,
    )(*after, *indices, weight, *arrays)


def rows_plain_kernel(part, width, turned, order_ref, weight_ref, right_ref, send_ref, keep_ref, sum_ref):
    depth = weight_ref.shape[1]
    chunk = 512 if depth % 512 == 0 else depth

    def term(start):
        here = pl.ds(start, chunk)
        return dot(weight_ref[:, here], right_ref[here, part * width : (part + 1) * width])

    sum_ref[...] = term(0)

    @pl.loop(1, depth // chunk)
    def _(i):
        sum_ref[...] += term(pl.multiple_of(i * chunk, chunk))

    gather_rows(order_ref, sum_ref, send_ref, keep_ref, turned)


def rows_times(weight, right, part, width, rows, turned, after=()):
    height = weight.shape[0]
    block = height // rows.size
    shapes = two_halves(rows.size, (width, block) if turned else (block, width), F32)
    return product_call(
        functools.partial(rows_plain_kernel, part, width, turned),
        "rows_times",
        shapes,
        pltpu.VMEM((height, width), F32),
        weight,
        width,
        (rows.sending_first(),),
        (right,),
        after,
    )


def rows_joined_kernel(rows_ref, cols_ref, weight_ref, first_ref, second_ref, send_ref, keep_ref, sum_ref):
    half, _, own = first_ref.shape

    def term(part, i):
        block = cols_ref[i + half * (1 - part)]
        here = pl.ds(pl.multiple_of(block * own, 128), own)
        return dot(weight_ref[:, here], (first_ref, second_ref)[part][i], NT)

    sum_ref[...] = term(0, 0)
    for part in range(2):

        @pl.loop(1 - part, half)
        def _(i):
            sum_ref[...] += term(part, i)

    gather_rows(rows_ref, sum_ref, send_ref, keep_ref, False)


def rows_times_joined(weight, halves, rows, cols):
    height = weight.shape[0]
    width, own = halves[0].shape[1:]
    if own % 128:
        return rows_times(weight, cols.in_order(halves, 1).T, 0, width, rows, False)
    return product_call(
        rows_joined_kernel,
        "rows_times_joined",
        two_halves(rows.size, (height // rows.size, width), F32),
        pltpu.VMEM((height, width), F32),
        weight,
        width,
        (rows.sending_first(), cols.sending_first()),
        halves,
    )


def cols_kernel(
    cols_ref, rows_ref, weight_ref, scale_ref, first_ref, second_ref, send_ref, keep_ref, whole_ref
):
    count, _, own = first_ref.shape
    for v in range(2 * count):
        block = rows_ref[(v + count) % (2 * count)]
        there = pl.ds(pl.multiple_of(block * own, 128), own)
        value = (first_ref, second_ref)[v // count][v % count]
        whole_ref[:, there] = (value.astype(F32) * scale_ref[:, there]).astype(BF16)

    half, _, block = send_ref.shape
    for part, out_ref in enumerate((send_ref, keep_ref)):

        @pl.loop(0, half)
        def _(i):
            here = pl.ds(pl.multiple_of(cols_ref[i + half * part] * block, 128), block)
            out_ref[i] = dot(whole_ref[...], weight_ref[:, here]).astype(out_ref.dtype)


def cols_times_joined(weight, scale, halves, rows, cols):
    height, depth = weight.shape
    block = depth // cols.size
    width, own = halves[0].shape[1:]
    if own % 128 or block % 128:
        left = (scale * rows.in_order(halves, 1)).astype(BF16)
        full = dot(left, weight).reshape(width, cols.size, block)
        order = cols.sending_first()
        full = jnp.stack([full[:, order[i]] for i in range(cols.size)])
        return full[: cols.size // 2].astype(BF16), full[cols.size // 2 :]
    return product_call(
        cols_kernel,
        "cols_times_joined",
        two_halves(cols.size, (width, block), BF16),
        pltpu.VMEM((width, height), BF16),
        weight,
        width,
        (cols.sending_first(), rows.sending_first()),
        (scale[None], *halves),
    )


def rank_kernel(weight_ref, basis_ref, out_ref):
    depth = weight_ref.shape[1]
    tile = math.gcd(depth, 512)

    @pl.loop(0, depth // tile)
    def _(i):
        here = pl.ds(pl.multiple_of(i * tile, tile), tile)
        out_ref[:, here] = dot(basis_ref[...], weight_ref[:, here]).astype(BF16)


def rank_times(weight, basis):
    height, depth = weight.shape
    if depth % 512:
        return dot(basis, weight).astype(BF16)
    vmem = pl.BlockSpec(memory_space=pltpu.VMEM)
    return pl.pallas_call(
        rank_kernel,
        out_shape=jax.ShapeDtypeStruct((basis.shape[0], depth), BF16),
        in_specs=[vmem, vmem],
        out_specs=vmem,
        compiler_params=pltpu.CompilerParams(vmem_limit_bytes=LIMIT),
        cost_estimate=pl.CostEstimate(
            flops=2 * height * depth * basis.shape[0],
            bytes_accessed=2 * (height + basis.shape[0]) * depth,
            transcendentals=0,
        ),
        name="rank_times",
    )(weight, basis)


def settle_kernel(order_ref, *refs):
    out_ref = refs[-1]
    count, block, half = refs[0].shape
    for v in range(2 * count):
        at = order_ref[(v + count) % (2 * count)] * block
        there = pl.ds(pl.multiple_of(at, block), block)
        for part in range(2):
            out_ref[there, part * half : (part + 1) * half] = refs[2 * part + v // count][v % count]


def settle(left, right, rows):
    count, block, half = left[0].shape
    if half % 128 or block % 16:
        return jnp.concatenate([rows.in_order(side, 0) for side in (left, right)], 1)
    vmem = pl.BlockSpec(memory_space=pltpu.VMEM)
    return pl.pallas_call(
        settle_kernel,
        out_shape=jax.ShapeDtypeStruct((2 * count * block, 2 * half), BF16),
        in_specs=[pl.BlockSpec(memory_space=pltpu.SMEM)] + [vmem] * 4,
        out_specs=vmem,
        compiler_params=pltpu.CompilerParams(vmem_limit_bytes=LIMIT),
        cost_estimate=pl.CostEstimate(
            flops=0, bytes_accessed=16 * count * block * half, transcendentals=0
        ),
        name="settle",
    )(rows.sending_first(), *left, *right)


def split(value):
    high = lax.reduce_precision(value, 8, 7)
    return high.astype(BF16), (value - high).astype(BF16)


def local(activations, out_grads, valid_len, weight, sketch):
    width = activations.shape[2]
    rows_here, cols_here = weight.shape
    rank = sketch.shape[1]
    half = rank // 2
    row_count, col_count = lax.axis_size("row"), lax.axis_size("col")
    row, col = lax.axis_index("row"), lax.axis_index("col")
    own_rows = rows_here // col_count
    over_col, over_row = Halving("col"), Halving("row")

    raw = [rows_times(weight, sketch, 0, half, over_col, True)]
    mass = local_mass(activations, out_grads, valid_len, raw[0][1], weight)
    raw.append(rows_times(weight, sketch, 1, half, over_col, True, (mass,)))
    fisher = sum_everywhere(mass.reshape(-1, 128)).reshape(width)
    mean = jnp.sum(fisher) / width + 1e-06
    square_scale = lax.dynamic_slice_in_dim(fisher, row * rows_here, rows_here) / mean
    own_square = lax.dynamic_slice_in_dim(square_scale, col * own_rows, own_rows)

    def second_of(parts):
        raw = over_col.scatter_sum(*parts)
        first = over_col.gather(raw.astype(BF16))
        parts = cols_times_joined(weight, square_scale, first, over_col, over_row)
        projected = over_row.gather(over_row.scatter_sum(*parts).astype(BF16))
        parts = rows_times_joined(weight, projected, over_col, over_row)
        return over_col.gather(over_col.scatter_sum(*parts).astype(BF16))

    second = settle(second_of(raw[0]), second_of(raw[1]), over_col)

    even = (col & 1) == 0
    mine = lax.dynamic_slice_in_dim(second, (col & 1) * half, half, 1).astype(F32)
    rows_of = ((0,), (0,))
    gram = sum(dot(term, second, rows_of) for term in split(square_scale[:, None] * mine))
    gram = sum_everywhere(gram, col=False)
    other = swap(gram, lambda parity: 0, lambda parity: 1)
    gram = jnp.concatenate([jnp.where(even, gram, other), jnp.where(even, other, gram)])

    inverse = inverse_factor(gram)
    order = over_row.sending_first()
    blocks = inverse.reshape(row_count, rank // row_count, rank)

    def coeffs_of(places):
        part = [lax.dynamic_index_in_dim(blocks, order[i], 0, keepdims=False) for i in places]
        high, low = split(jnp.concatenate(part))
        basis = (dot(high, second, NT) + dot(low, second, NT)) * square_scale
        return rank_times(weight, basis.astype(BF16)).reshape(len(part), -1, cols_here)

    coeffs = over_row.scatter_sum(
        coeffs_of(range(row_count // 2)), coeffs_of(range(row_count // 2, row_count))
    )

    own = lax.dynamic_slice_in_dim(second, col * own_rows, own_rows)
    basis = sum(dot(own, term, NT) for term in split(inverse))
    basis = basis * (jnp.sqrt(own_square)[:, None] * math.sqrt(width))
    return basis, coeffs * math.sqrt(cols_here * col_count)


def solution(mesh):
    placed = (
        P("row", None, None),
        P("row", None, "col"),
        P("row"),
        P("row", "col"),
        P("col", None),
    )
    return jax.shard_map(
        local,
        mesh=mesh,
        in_specs=placed,
        out_specs=(P(("row", "col"), None), P("row", "col")),
        check_vma=False,
    )
```

```python
import functools
import math

import jax
import jax.numpy as jnp
from jax import lax
from jax.experimental import pallas as pl
from jax.experimental.pallas import tpu as pltpu
from jax.sharding import PartitionSpec as P

AXES = ("row", "col")
F32 = jnp.float32
BF16 = jnp.bfloat16


def swap(block, row_bit, col_bit):
    rows, cols = lax.axis_size("row"), lax.axis_size("col")
    pairs = []
    for row in range(rows):
        for col in range(cols):
            other = (row ^ row_bit(col & 1)) * cols + (col ^ col_bit(col & 1))
            pairs.append((row * cols + col, other))
    return lax.ppermute(block, AXES, pairs)


class Halving:
    def __init__(self, axis):
        self.axis = axis
        self.size = lax.axis_size(axis)
        bits = list(range(self.size.bit_length() - 1))
        if axis == "col":
            self.orders = (bits, bits[:1] + bits[:0:-1])
        else:
            self.orders = (bits, bits[::-1])
        self.me = lax.axis_index(axis)
        self.odd = lax.axis_index("col") & 1
        steps = len(bits)
        self.masks = tuple(
            [
                sum(1 << order[t] for t in range(steps) if v >> (steps - 1 - t) & 1)
                for v in range(self.size)
            ]
            for order in self.orders
        )
        if axis == "col":
            half = self.size // 2
            even, odd = (masks[:half] for masks in self.masks)
            self.masks = (even + [1 ^ mask for mask in odd], odd + [1 ^ mask for mask in even])

    def block(self, v):
        even, odd = (masks[v] for masks in self.masks)
        return self.me ^ (even if even == odd else jnp.where(self.odd == 0, even, odd))

    def step(self, t, block):
        even, odd = (1 << order[t] for order in self.orders)
        pick = lambda parity: odd if parity else even
        none = lambda parity: 0
        return swap(block, *((none, pick) if self.axis == "col" else (pick, none)))

    def sending_first(self):
        half = self.size // 2
        places = [*range(half, self.size), *range(half)]
        return jnp.stack([self.block(v) for v in places]).astype(jnp.int32)

    def scatter_sum(self, send, keep):
        terms = [keep]
        for t in range(len(self.orders[0])):
            terms.append(self.step(t, send))
            half = terms[0].shape[0] // 2
            add = lambda part: sum(term[part].astype(F32) for term in terms)
            if half:
                send = add(slice(half, None)).astype(BF16)
                terms = [term[:half] for term in terms]
        return add(0)

    def gather(self, own):
        now = own[None]
        for t in reversed(range(len(self.orders[0]))):
            came = self.step(t, now)
            if t:
                now = jnp.concatenate([now, came])
        return now, came

    def in_order(self, halves, axis):
        virtual = jnp.concatenate(halves)
        places = []
        for masks in self.masks:
            inverse = [0] * self.size
            for v, mask in enumerate(masks):
                inverse[mask] = v
            places.append(jnp.array(inverse, jnp.int32))
        place = jnp.where(self.odd == 0, places[0], places[1])
        take = lambda j: lax.dynamic_index_in_dim(
            virtual, place[self.me ^ j], 0, keepdims=False
        )
        return jnp.concatenate([take(j) for j in range(self.size)], axis)


def sum_everywhere(value, row=True, col=True):
    none = lambda parity: 0
    if col:
        for bit in range(lax.axis_size("col").bit_length() - 1):
            value = value + swap(value, none, lambda parity: 1 << bit)
    if row:
        steps = lax.axis_size("row").bit_length() - 1
        for t in range(steps):
            pick = lambda parity: 1 << (steps - 1 - t if parity else t)
            value = value + swap(value, pick, none)
    return value


def token_gram_kernel(valid_ref, grads_ref, after_ref, weight_ref, gram_ref, scale_ref):
    seq = pl.program_id(0)
    length = grads_ref.shape[1]
    tokens = lax.broadcasted_iota(jnp.int32, (length, 1), 0)
    grads = grads_ref[0].astype(F32)
    grads = jnp.where(tokens < valid_ref[seq], grads, 0.0)
    largest = jnp.max(jnp.abs(grads), axis=1, keepdims=True)
    scale = jnp.ones_like(largest)
    shrink = jnp.ones_like(largest)
    for power in (16, 48, 80):
        step = 2.0 ** (power + 16)
        high, low = largest >= 2.0**power, largest < 2.0**-power
        scale = jnp.where(high, step, jnp.where(low, 1.0 / step, scale))
        shrink = jnp.where(high, 1.0 / step, jnp.where(low, step, shrink))
    near = (grads * shrink).astype(BF16)
    gram = lax.dot_general(near, near, (((1,), (1,)), ((), ())), preferred_element_type=F32)
    high = gram.astype(BF16)
    gram_ref[0, :length] = high
    gram_ref[0, length:] = (gram - high.astype(F32)).astype(BF16)
    scale_ref[0] = jnp.broadcast_to(scale, (length, 128))


def row_mass_kernel(acts_ref, gram_ref, scale_ref, weight_ref, mass_ref):
    length = acts_ref.shape[1]
    total = jnp.zeros((1, acts_ref.shape[2]), F32)
    for seq in range(acts_ref.shape[0]):
        acts = acts_ref[seq].astype(F32) * scale_ref[seq][:, :1]
        spread = jnp.dot(gram_ref[seq], acts.astype(BF16), preferred_element_type=F32)
        spread = spread[:length] + spread[length:]
        total = total + jnp.sum(spread * acts, axis=0, keepdims=True)
    mass_ref[...] = total


def local_mass(activations, out_grads, valid_len, after, weight):
    seqs, length, width = activations.shape
    cols = out_grads.shape[2]
    whole = lambda seq, valid: (seq, 0, 0)
    gram, scale = pl.pallas_call(
        token_gram_kernel,
        out_shape=(
            jax.ShapeDtypeStruct((seqs, 2 * length, length), BF16),
            jax.ShapeDtypeStruct((seqs, length, 128), F32),
        ),
        grid_spec=pltpu.PrefetchScalarGridSpec(
            num_scalar_prefetch=1,
            grid=(seqs,),
            in_specs=[
                pl.BlockSpec((1, length, cols), whole),
                pl.BlockSpec(memory_space=pl.ANY),
                pl.BlockSpec(memory_space=pltpu.VMEM),
            ],
            out_specs=(
                pl.BlockSpec((1, 2 * length, length), whole),
                pl.BlockSpec((1, length, 128), whole),
            ),
        ),
        compiler_params=pltpu.CompilerParams(vmem_limit_bytes=LIMIT),
        cost_estimate=pl.CostEstimate(
            flops=2 * seqs * length * length * cols,
            bytes_accessed=2 * out_grads.size,
            transcendentals=0,
        ),
        name="token_gram",
    )(valid_len, out_grads, after, weight)
    tile = math.gcd(width, 1024)
    fixed = lambda i: (0, 0, 0)
    mass = pl.pallas_call(
        row_mass_kernel,
        out_shape=jax.ShapeDtypeStruct((1, width), F32),
        grid=(width // tile,),
        in_specs=[
            pl.BlockSpec((seqs, length, tile), lambda i: (0, 0, i)),
            pl.BlockSpec((seqs, 2 * length, length), fixed),
            pl.BlockSpec((seqs, length, 128), fixed),
            pl.BlockSpec(memory_space=pltpu.VMEM),
        ],
        out_specs=pl.BlockSpec((1, tile), lambda i: (0, i)),
        compiler_params=pltpu.CompilerParams(vmem_limit_bytes=LIMIT),
        cost_estimate=pl.CostEstimate(
            flops=4 * seqs * length * length * width,
            bytes_accessed=2 * activations.size,
            transcendentals=0,
        ),
        name="row_mass",
    )(activations, gram, scale, weight)
    return mass.reshape(width)


def invert_block(tile):
    size = tile.shape[0]
    groups = [tile[i : i + 8] for i in range(0, size, 8)]
    lane = lax.broadcasted_iota(jnp.int32, (8, size), 1)
    sub = lax.broadcasted_iota(jnp.int32, (8, size), 0)
    done = []
    for g in range(size // 8):
        base = 8 * g
        inside = (lane >= base) & (lane < base + 8)
        now = groups[g]
        column = [jnp.broadcast_to(now[:, base + j : base + j + 1], (8, size)) for j in range(8)]
        now = jnp.where(inside, jnp.where(lane - base == sub, 1.0, 0.0), now)
        out, pivots, inverses = (jnp.ones((8, size), F32) for _ in range(3))
        for k in range(8):
            here = sub == k
            pivot = jnp.broadcast_to(column[k][k : k + 1], (8, size))
            inverse = pl.reciprocal(pivot, approx=True)
            inverse = inverse * (2.0 - pivot * inverse)
            out, pivots = jnp.where(here, now, out), jnp.where(here, pivot, pivots)
            inverses = jnp.where(here, inverse, inverses)
            factor = jnp.where(here, 0.0, column[k]) * inverse
            now = now - factor * jnp.broadcast_to(now[k : k + 1], (8, size))
            for j in range(k + 1, 8):
                across = jnp.broadcast_to(column[j][k : k + 1], (8, size))
                column[j] = column[j] - factor * across
        now = now * inverses
        done.append(jnp.where(lane < base + 8, out * lax.rsqrt(pivots), 0.0))
        rows = [jnp.broadcast_to(now[s : s + 1], (8, size)) for s in range(8)]
        for i in range(g + 1, size // 8):
            left = groups[i]
            kept = jnp.where(inside, 0.0, left)
            for s in range(8):
                weight = jnp.broadcast_to(left[:, base + s : base + s + 1], (8, size))
                kept = kept - weight * rows[s]
            groups[i] = kept
    return jnp.concatenate(done)


def inverse_factor_kernel(gram_ref, out_ref, work_ref):
    size = gram_ref.shape[0]
    block = 128
    count = size // block
    work_ref[...] = gram_ref[...]
    lane = lax.broadcasted_iota(jnp.int32, (block, size), 1)

    def step(k, carry):
        base = pl.multiple_of(k * block, block)
        here = pl.ds(base, block)
        small = invert_block(work_ref[here, here])
        inside = (lane >= base) & (lane < base + block)
        eye = lax.broadcasted_iota(jnp.int32, (block, size), 0) == lane - base
        rows = jnp.where(inside, jnp.where(eye, 1.0, 0.0), work_ref[here, :])
        rows = jnp.dot(small, rows, precision=lax.Precision.HIGHEST, preferred_element_type=F32)
        out_ref[here, :] = jnp.where(lane < base + block, rows, 0.0)
        work_ref[here, :] = rows

        def update(i, carry):
            there = pl.ds(pl.multiple_of(i * block, block), block)
            left = work_ref[here, there]
            old = jnp.where(inside, 0.0, work_ref[there, :])
            work_ref[there, :] = old - lax.dot_general(
                left,
                rows,
                (((0,), (0,)), ((), ())),
                precision=lax.Precision.HIGHEST,
                preferred_element_type=F32,
            )
            return carry

        return lax.fori_loop(k + 1, count, update, carry)

    lax.fori_loop(0, count, step, 0)


def inverse_factor(gram):
    size = gram.shape[0]
    return pl.pallas_call(
        inverse_factor_kernel,
        out_shape=jax.ShapeDtypeStruct((size, size), F32),
        in_specs=[pl.BlockSpec(memory_space=pltpu.VMEM)],
        out_specs=pl.BlockSpec(memory_space=pltpu.VMEM),
        scratch_shapes=[pltpu.VMEM((size, size), F32)],
        compiler_params=pltpu.CompilerParams(vmem_limit_bytes=LIMIT),
        cost_estimate=pl.CostEstimate(
            flops=40 * size**3, bytes_accessed=8 * size * size, transcendentals=size
        ),
        name="inverse_factor",
    )(gram)


LIMIT = 16 << 20


def dot(left, right, dims=((1,), (0,))):
    return lax.dot_general(left, right, (dims, ((), ())), preferred_element_type=F32)


NT = ((1,), (1,))


def gather_rows(order_ref, sum_ref, send_ref, keep_ref, turned):
    half = send_ref.shape[0]
    block = sum_ref.shape[0] // (2 * half)
    for i in range(2 * half):
        here = pl.ds(pl.multiple_of(order_ref[i] * block, block), block)
        value = sum_ref[here, :]
        target = send_ref if i < half else keep_ref
        target[i % half] = (value.T if turned else value).astype(target.dtype)


def two_halves(size, shape, send_type):
    dims = (size // 2,) + shape
    return (jax.ShapeDtypeStruct(dims, send_type), jax.ShapeDtypeStruct(dims, F32))


def product_call(kernel, name, out_shape, scratch, weight, width, indices, arrays, after=()):
    height, depth = weight.shape
    smem, vmem = (pl.BlockSpec(memory_space=space) for space in (pltpu.SMEM, pltpu.VMEM))
    return pl.pallas_call(
        lambda *refs: kernel(*refs[len(after) :]),
        out_shape=out_shape,
        in_specs=[pl.BlockSpec(memory_space=pl.ANY)] * len(after)
        + [smem] * len(indices)
        + [vmem] * (1 + len(arrays)),
        out_specs=(vmem, vmem),
        scratch_shapes=[scratch],
        compiler_params=pltpu.CompilerParams(vmem_limit_bytes=LIMIT),
        cost_estimate=pl.CostEstimate(
            flops=2 * height * depth * width,
            bytes_accessed=2 * (height + width) * depth,
            transcendentals=0,
        ),
        name=name,
    )(*after, *indices, weight, *arrays)


def rows_plain_kernel(part, width, turned, order_ref, weight_ref, right_ref, send_ref, keep_ref, sum_ref):
    depth = weight_ref.shape[1]
    chunk = 512 if depth % 512 == 0 else depth

    def term(start):
        here = pl.ds(start, chunk)
        return dot(weight_ref[:, here], right_ref[here, part * width : (part + 1) * width])

    sum_ref[...] = term(0)

    @pl.loop(1, depth // chunk)
    def _(i):
        sum_ref[...] += term(pl.multiple_of(i * chunk, chunk))

    gather_rows(order_ref, sum_ref, send_ref, keep_ref, turned)


def rows_times(weight, right, part, width, rows, turned, after=()):
    height = weight.shape[0]
    block = height // rows.size
    shapes = two_halves(rows.size, (width, block) if turned else (block, width), F32)
    return product_call(
        functools.partial(rows_plain_kernel, part, width, turned),
        "rows_times",
        shapes,
        pltpu.VMEM((height, width), F32),
        weight,
        width,
        (rows.sending_first(),),
        (right,),
        after,
    )


def rows_joined_kernel(rows_ref, cols_ref, weight_ref, first_ref, second_ref, send_ref, keep_ref, sum_ref):
    half, _, own = first_ref.shape

    def term(part, i):
        block = cols_ref[i + half * (1 - part)]
        here = pl.ds(pl.multiple_of(block * own, 128), own)
        return dot(weight_ref[:, here], (first_ref, second_ref)[part][i], NT)

    sum_ref[...] = term(0, 0)
    for part in range(2):

        @pl.loop(1 - part, half)
        def _(i):
            sum_ref[...] += term(part, i)

    gather_rows(rows_ref, sum_ref, send_ref, keep_ref, False)


def rows_times_joined(weight, halves, rows, cols):
    height = weight.shape[0]
    width, own = halves[0].shape[1:]
    if own % 128:
        return rows_times(weight, cols.in_order(halves, 1).T, 0, width, rows, False)
    return product_call(
        rows_joined_kernel,
        "rows_times_joined",
        two_halves(rows.size, (height // rows.size, width), BF16),
        pltpu.VMEM((height, width), F32),
        weight,
        width,
        (rows.sending_first(), cols.sending_first()),
        halves,
    )


def cols_kernel(
    cols_ref, rows_ref, weight_ref, scale_ref, first_ref, second_ref, send_ref, keep_ref, whole_ref
):
    count, _, own = first_ref.shape
    for v in range(2 * count):
        block = rows_ref[(v + count) % (2 * count)]
        there = pl.ds(pl.multiple_of(block * own, 128), own)
        value = (first_ref, second_ref)[v // count][v % count]
        whole_ref[:, there] = (value.astype(F32) * scale_ref[:, there]).astype(BF16)

    half, _, block = send_ref.shape
    for part, out_ref in enumerate((send_ref, keep_ref)):

        @pl.loop(0, half)
        def _(i):
            here = pl.ds(pl.multiple_of(cols_ref[i + half * part] * block, 128), block)
            out_ref[i] = dot(whole_ref[...], weight_ref[:, here]).astype(out_ref.dtype)


def cols_times_joined(weight, scale, halves, rows, cols):
    height, depth = weight.shape
    block = depth // cols.size
    width, own = halves[0].shape[1:]
    if own % 128 or block % 128:
        left = (scale * rows.in_order(halves, 1)).astype(BF16)
        full = dot(left, weight).reshape(width, cols.size, block)
        order = cols.sending_first()
        full = jnp.stack([full[:, order[i]] for i in range(cols.size)])
        return full[: cols.size // 2].astype(BF16), full[cols.size // 2 :]
    return product_call(
        cols_kernel,
        "cols_times_joined",
        two_halves(cols.size, (width, block), BF16),
        pltpu.VMEM((width, height), BF16),
        weight,
        width,
        (cols.sending_first(), rows.sending_first()),
        (scale[None], *halves),
    )


def rank_kernel(weight_ref, basis_ref, out_ref):
    depth = weight_ref.shape[1]
    tile = math.gcd(depth, 512)

    @pl.loop(0, depth // tile)
    def _(i):
        here = pl.ds(pl.multiple_of(i * tile, tile), tile)
        out_ref[:, here] = dot(basis_ref[...], weight_ref[:, here]).astype(BF16)


def rank_times(weight, basis):
    height, depth = weight.shape
    if depth % 512:
        return dot(basis, weight).astype(BF16)
    vmem = pl.BlockSpec(memory_space=pltpu.VMEM)
    return pl.pallas_call(
        rank_kernel,
        out_shape=jax.ShapeDtypeStruct((basis.shape[0], depth), BF16),
        in_specs=[vmem, vmem],
        out_specs=vmem,
        compiler_params=pltpu.CompilerParams(vmem_limit_bytes=LIMIT),
        cost_estimate=pl.CostEstimate(
            flops=2 * height * depth * basis.shape[0],
            bytes_accessed=2 * (height + basis.shape[0]) * depth,
            transcendentals=0,
        ),
        name="rank_times",
    )(weight, basis)


def settle_kernel(order_ref, *refs):
    out_ref = refs[-1]
    count, block, half = refs[0].shape
    for v in range(2 * count):
        at = order_ref[(v + count) % (2 * count)] * block
        there = pl.ds(pl.multiple_of(at, block), block)
        for part in range(2):
            out_ref[there, part * half : (part + 1) * half] = refs[2 * part + v // count][v % count]


def settle(left, right, rows):
    count, block, half = left[0].shape
    if half % 128 or block % 16:
        return jnp.concatenate([rows.in_order(side, 0) for side in (left, right)], 1)
    vmem = pl.BlockSpec(memory_space=pltpu.VMEM)
    return pl.pallas_call(
        settle_kernel,
        out_shape=jax.ShapeDtypeStruct((2 * count * block, 2 * half), BF16),
        in_specs=[pl.BlockSpec(memory_space=pltpu.SMEM)] + [vmem] * 4,
        out_specs=vmem,
        compiler_params=pltpu.CompilerParams(vmem_limit_bytes=LIMIT),
        cost_estimate=pl.CostEstimate(
            flops=0, bytes_accessed=16 * count * block * half, transcendentals=0
        ),
        name="settle",
    )(rows.sending_first(), *left, *right)


def split(value):
    high = lax.reduce_precision(value, 8, 7)
    return high.astype(BF16), (value - high).astype(BF16)


def local(activations, out_grads, valid_len, weight, sketch):
    width = activations.shape[2]
    rows_here, cols_here = weight.shape
    rank = sketch.shape[1]
    half = rank // 2
    row_count, col_count = lax.axis_size("row"), lax.axis_size("col")
    row, col = lax.axis_index("row"), lax.axis_index("col")
    own_rows = rows_here // col_count
    over_col, over_row = Halving("col"), Halving("row")

    raw = [rows_times(weight, sketch, 0, half, over_col, True)]
    mass = local_mass(activations, out_grads, valid_len, raw[0][1], weight)
    raw.append(rows_times(weight, sketch, 1, half, over_col, True, (mass,)))
    fisher = sum_everywhere(mass.reshape(-1, 128)).reshape(width)
    mean = jnp.sum(fisher) / width + 1e-06
    square_scale = lax.dynamic_slice_in_dim(fisher, row * rows_here, rows_here) / mean
    own_square = lax.dynamic_slice_in_dim(square_scale, col * own_rows, own_rows)

    def second_of(part):
        first, scale = over_col.scatter_sum(*raw[part]), square_scale
        if part:
            first, scale = first * own_square, jnp.ones_like(square_scale)
        first = over_col.gather(first.astype(BF16))
        parts = cols_times_joined(weight, scale, first, over_col, over_row)
        projected = over_row.gather(over_row.scatter_sum(*parts).astype(BF16))
        parts = rows_times_joined(weight, projected, over_col, over_row)
        return over_col.gather(over_col.scatter_sum(*parts).astype(BF16))

    second = settle(second_of(0), second_of(1), over_col)

    even = (col & 1) == 0
    mine = lax.dynamic_slice_in_dim(second, (col & 1) * half, half, 1).astype(F32)
    rows_of = ((0,), (0,))
    gram = sum(dot(term, second, rows_of) for term in split(square_scale[:, None] * mine))
    gram = sum_everywhere(gram, col=False)
    other = swap(gram, lambda parity: 0, lambda parity: 1)
    gram = jnp.concatenate([jnp.where(even, gram, other), jnp.where(even, other, gram)])

    inverse = inverse_factor(gram)
    order = over_row.sending_first()
    blocks = inverse.reshape(row_count, rank // row_count, rank)

    def coeffs_of(places):
        part = [lax.dynamic_index_in_dim(blocks, order[i], 0, keepdims=False) for i in places]
        high, low = split(jnp.concatenate(part))
        basis = (dot(high, second, NT) + dot(low, second, NT)) * square_scale
        return rank_times(weight, basis.astype(BF16)).reshape(len(part), -1, cols_here)

    coeffs = over_row.scatter_sum(
        coeffs_of(range(row_count // 2)), coeffs_of(range(row_count // 2, row_count))
    )

    own = lax.dynamic_slice_in_dim(second, col * own_rows, own_rows)
    basis = sum(dot(own, term, NT) for term in split(inverse))
    basis = basis * (jnp.sqrt(own_square)[:, None] * math.sqrt(width))
    return basis, coeffs * math.sqrt(cols_here * col_count)


def solution(mesh):
    placed = (
        P("row", None, None),
        P("row", None, "col"),
        P("row"),
        P("row", "col"),
        P("col", None),
    )
    return jax.shard_map(
        local,
        mesh=mesh,
        in_specs=placed,
        out_specs=(P(("row", "col"), None), P("row", "col")),
        check_vma=False,
    )
```

```python
import functools
import math

import jax
import jax.numpy as jnp
from jax import lax
from jax.experimental import pallas as pl
from jax.experimental.pallas import tpu as pltpu
from jax.sharding import PartitionSpec as P

AXES = ("row", "col")
F32 = jnp.float32
BF16 = jnp.bfloat16


def swap(block, row_bit, col_bit):
    rows, cols = lax.axis_size("row"), lax.axis_size("col")
    pairs = []
    for row in range(rows):
        for col in range(cols):
            other = (row ^ row_bit(col & 1)) * cols + (col ^ col_bit(col & 1))
            pairs.append((row * cols + col, other))
    return lax.ppermute(block, AXES, pairs)


def split(value):
    high = lax.reduce_precision(value, 8, 7)
    return high.astype(BF16), (value - high).astype(BF16)


class Halving:
    def __init__(self, axis):
        self.axis = axis
        self.size = lax.axis_size(axis)
        bits = list(range(self.size.bit_length() - 1))
        if axis == "col":
            self.orders = (bits, bits[:1] + bits[:0:-1])
        else:
            self.orders = (bits, bits[::-1])
        self.me = lax.axis_index(axis)
        self.odd = lax.axis_index("col") & 1
        steps = len(bits)
        self.masks = tuple(
            [
                sum(1 << order[t] for t in range(steps) if v >> (steps - 1 - t) & 1)
                for v in range(self.size)
            ]
            for order in self.orders
        )
        if axis == "col":
            half = self.size // 2
            even, odd = (masks[:half] for masks in self.masks)
            self.masks = (even + [1 ^ mask for mask in odd], odd + [1 ^ mask for mask in even])

    def block(self, v):
        even, odd = (masks[v] for masks in self.masks)
        return self.me ^ (even if even == odd else jnp.where(self.odd == 0, even, odd))

    def step(self, t, block):
        even, odd = (1 << order[t] for order in self.orders)
        pick = lambda parity: odd if parity else even
        none = lambda parity: 0
        return swap(block, *((none, pick) if self.axis == "col" else (pick, none)))

    def sending_first(self):
        half = self.size // 2
        places = [*range(half, self.size), *range(half)]
        return jnp.stack([self.block(v) for v in places]).astype(jnp.int32)

    def scatter_sum(self, send, keep, rider=None):
        terms = [keep]
        for t in range(len(self.orders[0])):
            came = self.step(t, send)
            if rider is not None:
                height = rider.shape[0]
                *parts, blocks = jnp.split(came, [height] if t == 0 else [height, 2 * height])
                rider = rider + sum(part.astype(F32) for part in parts)
                came = blocks.reshape(terms[0].shape)
            terms.append(came)
            half = terms[0].shape[0] // 2
            add = lambda part: sum(term[part].astype(F32) for term in terms)
            if half:
                send = add(slice(half, None)).astype(BF16)
                terms = [term[:half] for term in terms]
                if rider is not None:
                    parts = split(rider)
                    rider = sum(part.astype(F32) for part in parts)
                    send = jnp.concatenate([*parts, send.reshape(-1, send.shape[-1])])
        return add(0) if rider is None else (add(0), rider)

    def gather(self, own):
        now = own[None]
        for t in reversed(range(len(self.orders[0]))):
            came = self.step(t, now)
            if t:
                now = jnp.concatenate([now, came])
        return now, came

    def in_order(self, halves, axis):
        virtual = jnp.concatenate(halves)
        places = []
        for masks in self.masks:
            inverse = [0] * self.size
            for v, mask in enumerate(masks):
                inverse[mask] = v
            places.append(jnp.array(inverse, jnp.int32))
        place = jnp.where(self.odd == 0, places[0], places[1])
        take = lambda j: lax.dynamic_index_in_dim(
            virtual, place[self.me ^ j], 0, keepdims=False
        )
        return jnp.concatenate([take(j) for j in range(self.size)], axis)


def sum_everywhere(value, row=True, col=True):
    none = lambda parity: 0
    if col:
        for bit in range(lax.axis_size("col").bit_length() - 1):
            value = value + swap(value, none, lambda parity: 1 << bit)
    if row:
        steps = lax.axis_size("row").bit_length() - 1
        for t in range(steps):
            pick = lambda parity: 1 << (steps - 1 - t if parity else t)
            value = value + swap(value, pick, none)
    return value


def token_gram_kernel(valid_ref, grads_ref, after_ref, weight_ref, gram_ref, scale_ref):
    seq = pl.program_id(0)
    length = grads_ref.shape[1]
    tokens = lax.broadcasted_iota(jnp.int32, (length, 1), 0)
    grads = grads_ref[0].astype(F32)
    grads = jnp.where(tokens < valid_ref[seq], grads, 0.0)
    largest = jnp.max(jnp.abs(grads), axis=1, keepdims=True)
    scale = jnp.ones_like(largest)
    shrink = jnp.ones_like(largest)
    for power in (16, 48, 80):
        step = 2.0 ** (power + 16)
        high, low = largest >= 2.0**power, largest < 2.0**-power
        scale = jnp.where(high, step, jnp.where(low, 1.0 / step, scale))
        shrink = jnp.where(high, 1.0 / step, jnp.where(low, step, shrink))
    near = (grads * shrink).astype(BF16)
    gram = lax.dot_general(near, near, (((1,), (1,)), ((), ())), preferred_element_type=F32)
    high = gram.astype(BF16)
    gram_ref[0, :length] = high
    gram_ref[0, length:] = (gram - high.astype(F32)).astype(BF16)
    scale_ref[0] = jnp.broadcast_to(scale, (length, 128))


def row_mass_kernel(acts_ref, gram_ref, scale_ref, weight_ref, mass_ref):
    length = acts_ref.shape[1]
    total = jnp.zeros((1, acts_ref.shape[2]), F32)
    for seq in range(acts_ref.shape[0]):
        acts = acts_ref[seq].astype(F32) * scale_ref[seq][:, :1]
        spread = jnp.dot(gram_ref[seq], acts.astype(BF16), preferred_element_type=F32)
        spread = spread[:length] + spread[length:]
        total = total + jnp.sum(spread * acts, axis=0, keepdims=True)
    mass_ref[...] = total


def local_mass(activations, out_grads, valid_len, after, weight):
    seqs, length, width = activations.shape
    cols = out_grads.shape[2]
    whole = lambda seq, valid: (seq, 0, 0)
    gram, scale = pl.pallas_call(
        token_gram_kernel,
        out_shape=(
            jax.ShapeDtypeStruct((seqs, 2 * length, length), BF16),
            jax.ShapeDtypeStruct((seqs, length, 128), F32),
        ),
        grid_spec=pltpu.PrefetchScalarGridSpec(
            num_scalar_prefetch=1,
            grid=(seqs,),
            in_specs=[
                pl.BlockSpec((1, length, cols), whole),
                pl.BlockSpec(memory_space=pl.ANY),
                pl.BlockSpec(memory_space=pltpu.VMEM),
            ],
            out_specs=(
                pl.BlockSpec((1, 2 * length, length), whole),
                pl.BlockSpec((1, length, 128), whole),
            ),
        ),
        compiler_params=pltpu.CompilerParams(vmem_limit_bytes=LIMIT),
        cost_estimate=pl.CostEstimate(
            flops=2 * seqs * length * length * cols,
            bytes_accessed=2 * out_grads.size,
            transcendentals=0,
        ),
        name="token_gram",
    )(valid_len, out_grads, after, weight)
    tile = math.gcd(width, 1024)
    fixed = lambda i: (0, 0, 0)
    mass = pl.pallas_call(
        row_mass_kernel,
        out_shape=jax.ShapeDtypeStruct((1, width), F32),
        grid=(width // tile,),
        in_specs=[
            pl.BlockSpec((seqs, length, tile), lambda i: (0, 0, i)),
            pl.BlockSpec((seqs, 2 * length, length), fixed),
            pl.BlockSpec((seqs, length, 128), fixed),
            pl.BlockSpec(memory_space=pltpu.VMEM),
        ],
        out_specs=pl.BlockSpec((1, tile), lambda i: (0, i)),
        compiler_params=pltpu.CompilerParams(vmem_limit_bytes=LIMIT),
        cost_estimate=pl.CostEstimate(
            flops=4 * seqs * length * length * width,
            bytes_accessed=2 * activations.size,
            transcendentals=0,
        ),
        name="row_mass",
    )(activations, gram, scale, weight)
    return mass.reshape(width)


def invert_block(tile):
    size = tile.shape[0]
    groups = [tile[i : i + 8] for i in range(0, size, 8)]
    lane = lax.broadcasted_iota(jnp.int32, (8, size), 1)
    sub = lax.broadcasted_iota(jnp.int32, (8, size), 0)
    done = []
    for g in range(size // 8):
        base = 8 * g
        inside = (lane >= base) & (lane < base + 8)
        now = groups[g]
        column = [jnp.broadcast_to(now[:, base + j : base + j + 1], (8, size)) for j in range(8)]
        now = jnp.where(inside, jnp.where(lane - base == sub, 1.0, 0.0), now)
        out, pivots, inverses = (jnp.ones((8, size), F32) for _ in range(3))
        for k in range(8):
            here = sub == k
            pivot = jnp.broadcast_to(column[k][k : k + 1], (8, size))
            inverse = 1.0 / pivot
            out, pivots = jnp.where(here, now, out), jnp.where(here, pivot, pivots)
            inverses = jnp.where(here, inverse, inverses)
            factor = jnp.where(here, 0.0, column[k])
            now = now - factor * jnp.broadcast_to(now[k : k + 1], (8, size)) * inverse
            for j in range(k + 1, 8):
                across = jnp.broadcast_to(column[j][k : k + 1], (8, size))
                column[j] = column[j] - factor * across * inverse
        now = now * inverses
        done.append(jnp.where(lane < base + 8, out * lax.rsqrt(pivots), 0.0))
        rows = [jnp.broadcast_to(now[s : s + 1], (8, size)) for s in range(8)]
        for i in range(g + 1, size // 8):
            left = groups[i]
            kept = jnp.where(inside, 0.0, left)
            for s in range(8):
                weight = jnp.broadcast_to(left[:, base + s : base + s + 1], (8, size))
                kept = kept - weight * rows[s]
            groups[i] = kept
    return jnp.concatenate(done)


def inverse_factor_kernel(gram_ref, out_ref, work_ref):
    size = gram_ref.shape[0]
    block = 128
    count = size // block
    work_ref[...] = gram_ref[...]
    lane = lax.broadcasted_iota(jnp.int32, (block, size), 1)

    def step(k, carry):
        base = pl.multiple_of(k * block, block)
        here = pl.ds(base, block)
        small = invert_block(work_ref[here, here])
        inside = (lane >= base) & (lane < base + block)
        eye = lax.broadcasted_iota(jnp.int32, (block, size), 0) == lane - base
        rows = jnp.where(inside, jnp.where(eye, 1.0, 0.0), work_ref[here, :])
        rows = jnp.dot(small, rows, precision=lax.Precision.HIGHEST, preferred_element_type=F32)
        out_ref[here, :] = jnp.where(lane < base + block, rows, 0.0)
        work_ref[here, :] = rows

        def update(i, carry):
            there = pl.ds(pl.multiple_of(i * block, block), block)
            left = work_ref[here, there]
            old = jnp.where(inside, 0.0, work_ref[there, :])
            work_ref[there, :] = old - lax.dot_general(
                left,
                rows,
                (((0,), (0,)), ((), ())),
                precision=lax.Precision.HIGHEST,
                preferred_element_type=F32,
            )
            return carry

        return lax.fori_loop(k + 1, count, update, carry)

    lax.fori_loop(0, count, step, 0)


def inverse_factor(gram):
    size = gram.shape[0]
    return pl.pallas_call(
        inverse_factor_kernel,
        out_shape=jax.ShapeDtypeStruct((size, size), F32),
        in_specs=[pl.BlockSpec(memory_space=pltpu.VMEM)],
        out_specs=pl.BlockSpec(memory_space=pltpu.VMEM),
        scratch_shapes=[pltpu.VMEM((size, size), F32)],
        compiler_params=pltpu.CompilerParams(vmem_limit_bytes=LIMIT),
        cost_estimate=pl.CostEstimate(
            flops=40 * size**3, bytes_accessed=8 * size * size, transcendentals=size
        ),
        name="inverse_factor",
    )(gram)


LIMIT = 16 << 20


def dot(left, right, dims=((1,), (0,))):
    return lax.dot_general(left, right, (dims, ((), ())), preferred_element_type=F32)


NT = ((1,), (1,))


def gather_rows(order_ref, sum_ref, send_ref, keep_ref, turned):
    half, height = keep_ref.shape[:2]
    above = send_ref.shape[0] - half * height
    block = sum_ref.shape[0] // (2 * half)
    for i in range(2 * half):
        here = pl.ds(pl.multiple_of(order_ref[i] * block, block), block)
        value = sum_ref[here, :]
        value = value.T if turned else value
        if i >= half:
            keep_ref[i - half] = value
        elif len(send_ref.shape) == 3:
            send_ref[i] = value.astype(send_ref.dtype)
        else:
            start = above + i * height
            send_ref[start : start + height] = value


def two_halves(size, shape, send_type):
    dims = (size // 2,) + shape
    return (jax.ShapeDtypeStruct(dims, send_type), jax.ShapeDtypeStruct(dims, F32))


def product_call(kernel, name, out_shape, scratch, weight, width, indices, arrays):
    height, depth = weight.shape
    smem, vmem = (pl.BlockSpec(memory_space=space) for space in (pltpu.SMEM, pltpu.VMEM))
    return pl.pallas_call(
        kernel,
        out_shape=out_shape,
        in_specs=[smem] * len(indices) + [vmem] * (1 + len(arrays)),
        out_specs=(vmem, vmem),
        scratch_shapes=[scratch],
        compiler_params=pltpu.CompilerParams(vmem_limit_bytes=LIMIT),
        cost_estimate=pl.CostEstimate(
            flops=2 * height * depth * width,
            bytes_accessed=2 * (height + width) * depth,
            transcendentals=0,
        ),
        name=name,
    )(*indices, weight, *arrays)


def rows_plain_kernel(part, width, turned, order_ref, weight_ref, right_ref, *refs):
    *rider_ref, send_ref, keep_ref, sum_ref = refs
    depth = weight_ref.shape[1]
    chunk = 512 if depth % 512 == 0 else depth

    def term(start):
        here = pl.ds(start, chunk)
        return dot(weight_ref[:, here], right_ref[here, part * width : (part + 1) * width])

    sum_ref[...] = term(0)

    @pl.loop(1, depth // chunk)
    def _(i):
        sum_ref[...] += term(pl.multiple_of(i * chunk, chunk))

    if rider_ref:
        send_ref[: rider_ref[0].shape[0]] = rider_ref[0][...]
    gather_rows(order_ref, sum_ref, send_ref, keep_ref, turned)


def rows_times(weight, right, part, width, rows, turned, rider=()):
    height = weight.shape[0]
    block = height // rows.size
    shapes = two_halves(rows.size, (width, block) if turned else (block, width), F32)
    for load in rider:
        dims = (load.shape[0] + rows.size // 2 * width, block)
        shapes = (jax.ShapeDtypeStruct(dims, F32), shapes[1])
    return product_call(
        functools.partial(rows_plain_kernel, part, width, turned),
        "rows_times",
        shapes,
        pltpu.VMEM((height, width), F32),
        weight,
        width,
        (rows.sending_first(),),
        (right, *rider),
    )


def rows_joined_kernel(rows_ref, cols_ref, weight_ref, first_ref, second_ref, send_ref, keep_ref, sum_ref):
    half, _, own = first_ref.shape

    def term(part, i):
        block = cols_ref[i + half * (1 - part)]
        here = pl.ds(pl.multiple_of(block * own, 128), own)
        return dot(weight_ref[:, here], (first_ref, second_ref)[part][i], NT)

    sum_ref[...] = term(0, 0)
    for part in range(2):

        @pl.loop(1 - part, half)
        def _(i):
            sum_ref[...] += term(part, i)

    gather_rows(rows_ref, sum_ref, send_ref, keep_ref, False)


def rows_times_joined(weight, halves, rows, cols):
    height = weight.shape[0]
    width, own = halves[0].shape[1:]
    if own % 128:
        return rows_times(weight, cols.in_order(halves, 1).T, 0, width, rows, False)
    return product_call(
        rows_joined_kernel,
        "rows_times_joined",
        two_halves(rows.size, (height // rows.size, width), BF16),
        pltpu.VMEM((height, width), F32),
        weight,
        width,
        (rows.sending_first(), cols.sending_first()),
        halves,
    )


def cols_kernel(
    cols_ref, rows_ref, weight_ref, scale_ref, first_ref, second_ref, send_ref, keep_ref, whole_ref
):
    count, _, own = first_ref.shape
    for v in range(2 * count):
        block = rows_ref[(v + count) % (2 * count)]
        there = pl.ds(pl.multiple_of(block * own, 128), own)
        value = (first_ref, second_ref)[v // count][v % count]
        whole_ref[:, there] = (value.astype(F32) * scale_ref[:, there]).astype(BF16)

    half, _, block = send_ref.shape
    for part, out_ref in enumerate((send_ref, keep_ref)):

        @pl.loop(0, half)
        def _(i):
            here = pl.ds(pl.multiple_of(cols_ref[i + half * part] * block, 128), block)
            out_ref[i] = dot(whole_ref[...], weight_ref[:, here]).astype(out_ref.dtype)


def cols_times_joined(weight, scale, halves, rows, cols):
    height, depth = weight.shape
    block = depth // cols.size
    width, own = halves[0].shape[1:]
    if own % 128 or block % 128:
        left = (scale * rows.in_order(halves, 1)).astype(BF16)
        full = dot(left, weight).reshape(width, cols.size, block)
        order = cols.sending_first()
        full = jnp.stack([full[:, order[i]] for i in range(cols.size)])
        return full[: cols.size // 2].astype(BF16), full[cols.size // 2 :]
    return product_call(
        cols_kernel,
        "cols_times_joined",
        two_halves(cols.size, (width, block), BF16),
        pltpu.VMEM((width, height), BF16),
        weight,
        width,
        (cols.sending_first(), rows.sending_first()),
        (scale[None], *halves),
    )


def rank_kernel(weight_ref, basis_ref, out_ref):
    depth = weight_ref.shape[1]
    tile = math.gcd(depth, 512)

    @pl.loop(0, depth // tile)
    def _(i):
        here = pl.ds(pl.multiple_of(i * tile, tile), tile)
        out_ref[:, here] = dot(basis_ref[...], weight_ref[:, here]).astype(BF16)


def rank_times(weight, basis):
    height, depth = weight.shape
    if depth % 512:
        return dot(basis, weight).astype(BF16)
    vmem = pl.BlockSpec(memory_space=pltpu.VMEM)
    return pl.pallas_call(
        rank_kernel,
        out_shape=jax.ShapeDtypeStruct((basis.shape[0], depth), BF16),
        in_specs=[vmem, vmem],
        out_specs=vmem,
        compiler_params=pltpu.CompilerParams(vmem_limit_bytes=LIMIT),
        cost_estimate=pl.CostEstimate(
            flops=2 * height * depth * basis.shape[0],
            bytes_accessed=2 * (height + basis.shape[0]) * depth,
            transcendentals=0,
        ),
        name="rank_times",
    )(weight, basis)


def settle_kernel(order_ref, *refs):
    out_ref = refs[-1]
    count, block, half = refs[0].shape
    for v in range(2 * count):
        at = order_ref[(v + count) % (2 * count)] * block
        there = pl.ds(pl.multiple_of(at, block), block)
        for part in range(2):
            out_ref[there, part * half : (part + 1) * half] = refs[2 * part + v // count][v % count]


def settle(left, right, rows):
    count, block, half = left[0].shape
    if half % 128 or block % 16:
        return jnp.concatenate([rows.in_order(side, 0) for side in (left, right)], 1)
    vmem = pl.BlockSpec(memory_space=pltpu.VMEM)
    return pl.pallas_call(
        settle_kernel,
        out_shape=jax.ShapeDtypeStruct((2 * count * block, 2 * half), BF16),
        in_specs=[pl.BlockSpec(memory_space=pltpu.SMEM)] + [vmem] * 4,
        out_specs=vmem,
        compiler_params=pltpu.CompilerParams(vmem_limit_bytes=LIMIT),
        cost_estimate=pl.CostEstimate(
            flops=0, bytes_accessed=16 * count * block * half, transcendentals=0
        ),
        name="settle",
    )(rows.sending_first(), *left, *right)


def local(activations, out_grads, valid_len, weight, sketch):
    width = activations.shape[2]
    rows_here, cols_here = weight.shape
    rank = sketch.shape[1]
    half = rank // 2
    row_count, col_count = lax.axis_size("row"), lax.axis_size("col")
    row, col = lax.axis_index("row"), lax.axis_index("col")
    own_rows = rows_here // col_count
    over_col, over_row = Halving("col"), Halving("row")

    raw = rows_times(weight, sketch, 0, half, over_col, True)
    mass = local_mass(activations, out_grads, valid_len, raw[1], weight)
    mass = mass.reshape(-1, own_rows)
    later = rows_times(weight, sketch, 1, half, over_col, True, (mass,))
    raw = over_col.scatter_sum(*raw)
    later, fisher = over_col.scatter_sum(*later, mass)
    fisher = sum_everywhere(fisher, col=False).reshape(width)
    mean = jnp.sum(fisher) / width + 1e-06
    square_scale = lax.dynamic_slice_in_dim(fisher, row * rows_here, rows_here) / mean
    own_square = lax.dynamic_slice_in_dim(square_scale, col * own_rows, own_rows)

    def second_of(raw):
        first = over_col.gather(raw.astype(BF16))
        parts = cols_times_joined(weight, square_scale, first, over_col, over_row)
        projected = over_row.gather(over_row.scatter_sum(*parts).astype(BF16))
        parts = rows_times_joined(weight, projected, over_col, over_row)
        return over_col.gather(over_col.scatter_sum(*parts).astype(BF16))

    second = settle(second_of(raw), second_of(later), over_col)

    even = (col & 1) == 0
    mine = lax.dynamic_slice_in_dim(second, (col & 1) * half, half, 1).astype(F32)
    rows_of = ((0,), (0,))
    gram = sum(dot(term, second, rows_of) for term in split(square_scale[:, None] * mine))
    gram = sum_everywhere(gram, col=False)
    other = swap(gram, lambda parity: 0, lambda parity: 1)
    gram = jnp.concatenate([jnp.where(even, gram, other), jnp.where(even, other, gram)])

    inverse = inverse_factor(gram)
    order = over_row.sending_first()
    blocks = inverse.reshape(row_count, rank // row_count, rank)

    def coeffs_of(places):
        part = [lax.dynamic_index_in_dim(blocks, order[i], 0, keepdims=False) for i in places]
        high, low = split(jnp.concatenate(part))
        basis = (dot(high, second, NT) + dot(low, second, NT)) * square_scale
        return rank_times(weight, basis.astype(BF16)).reshape(len(part), -1, cols_here)

    coeffs = over_row.scatter_sum(
        coeffs_of(range(row_count // 2)), coeffs_of(range(row_count // 2, row_count))
    )

    own = lax.dynamic_slice_in_dim(second, col * own_rows, own_rows)
    basis = sum(dot(own, term, NT) for term in split(inverse))
    basis = basis * (jnp.sqrt(own_square)[:, None] * math.sqrt(width))
    return basis, coeffs * math.sqrt(cols_here * col_count)


def solution(mesh):
    placed = (
        P("row", None, None),
        P("row", None, "col"),
        P("row"),
        P("row", "col"),
        P("col", None),
    )
    return jax.shard_map(
        local,
        mesh=mesh,
        in_specs=placed,
        out_specs=(P(("row", "col"), None), P("row", "col")),
        check_vma=False,
    )
```

```python
import functools
import math

import jax
import jax.numpy as jnp
from jax import lax
from jax.experimental import pallas as pl
from jax.experimental.pallas import tpu as pltpu
from jax.sharding import PartitionSpec as P

AXES = ("row", "col")
F32 = jnp.float32
BF16 = jnp.bfloat16


def swap(block, row_bit, col_bit):
    rows, cols = lax.axis_size("row"), lax.axis_size("col")
    pairs = []
    for row in range(rows):
        for col in range(cols):
            other = (row ^ row_bit(col & 1)) * cols + (col ^ col_bit(col & 1))
            pairs.append((row * cols + col, other))
    return lax.ppermute(block, AXES, pairs)


def split(value):
    high = lax.reduce_precision(value, 8, 7)
    return high.astype(BF16), (value - high).astype(BF16)


class Halving:
    def __init__(self, axis):
        self.axis = axis
        self.size = lax.axis_size(axis)
        bits = list(range(self.size.bit_length() - 1))
        if axis == "col":
            self.orders = (bits, bits[:1] + bits[:0:-1])
        else:
            self.orders = (bits, bits[::-1])
        self.me = lax.axis_index(axis)
        self.odd = lax.axis_index("col") & 1
        steps = len(bits)
        self.masks = tuple(
            [
                sum(1 << order[t] for t in range(steps) if v >> (steps - 1 - t) & 1)
                for v in range(self.size)
            ]
            for order in self.orders
        )
        if axis == "col":
            half = self.size // 2
            even, odd = (masks[:half] for masks in self.masks)
            self.masks = (even + [1 ^ mask for mask in odd], odd + [1 ^ mask for mask in even])

    def block(self, v):
        even, odd = (masks[v] for masks in self.masks)
        return self.me ^ (even if even == odd else jnp.where(self.odd == 0, even, odd))

    def step(self, t, block):
        even, odd = (1 << order[t] for order in self.orders)
        pick = lambda parity: odd if parity else even
        none = lambda parity: 0
        return swap(block, *((none, pick) if self.axis == "col" else (pick, none)))

    def sending_first(self):
        half = self.size // 2
        places = [*range(half, self.size), *range(half)]
        return jnp.stack([self.block(v) for v in places]).astype(jnp.int32)

    def scatter_sum(self, send, keep, rider=None):
        terms = [keep]
        for t in range(len(self.orders[0])):
            came = self.step(t, send)
            if rider is not None:
                if t == 0:
                    rider = rider + self.step(t, rider)
                else:
                    height = rider.shape[0]
                    *parts, blocks = jnp.split(came, [height, 2 * height])
                    rider = rider + sum(part.astype(F32) for part in parts)
                    came = blocks.reshape(terms[0].shape)
            terms.append(came)
            half = terms[0].shape[0] // 2
            add = lambda part: sum(term[part].astype(F32) for term in terms)
            if half:
                send = add(slice(half, None)).astype(BF16)
                terms = [term[:half] for term in terms]
                if rider is not None:
                    parts = split(rider)
                    rider = sum(part.astype(F32) for part in parts)
                    send = jnp.concatenate([*parts, send.reshape(-1, send.shape[-1])])
        return add(0) if rider is None else (add(0), rider)

    def gather(self, own):
        now = own[None]
        for t in reversed(range(len(self.orders[0]))):
            came = self.step(t, now)
            if t:
                now = jnp.concatenate([now, came])
        return now, came

    def in_order(self, halves, axis):
        virtual = jnp.concatenate(halves)
        places = []
        for masks in self.masks:
            inverse = [0] * self.size
            for v, mask in enumerate(masks):
                inverse[mask] = v
            places.append(jnp.array(inverse, jnp.int32))
        place = jnp.where(self.odd == 0, places[0], places[1])
        take = lambda j: lax.dynamic_index_in_dim(
            virtual, place[self.me ^ j], 0, keepdims=False
        )
        return jnp.concatenate([take(j) for j in range(self.size)], axis)


def sum_everywhere(value, row=True, col=True):
    none = lambda parity: 0
    if col:
        for bit in range(lax.axis_size("col").bit_length() - 1):
            value = value + swap(value, none, lambda parity: 1 << bit)
    if row:
        steps = lax.axis_size("row").bit_length() - 1
        for t in range(steps):
            pick = lambda parity: 1 << (steps - 1 - t if parity else t)
            value = value + swap(value, pick, none)
    return value


def token_gram_kernel(valid_ref, grads_ref, after_ref, gram_ref, scale_ref):
    seq = pl.program_id(0)
    length = grads_ref.shape[1]
    tokens = lax.broadcasted_iota(jnp.int32, (length, 1), 0)
    grads = grads_ref[0].astype(F32)
    grads = jnp.where(tokens < valid_ref[seq], grads, 0.0)
    largest = jnp.max(jnp.abs(grads), axis=1, keepdims=True)
    scale = jnp.ones_like(largest)
    shrink = jnp.ones_like(largest)
    for power in (16, 48, 80):
        step = 2.0 ** (power + 16)
        high, low = largest >= 2.0**power, largest < 2.0**-power
        scale = jnp.where(high, step, jnp.where(low, 1.0 / step, scale))
        shrink = jnp.where(high, 1.0 / step, jnp.where(low, step, shrink))
    near = (grads * shrink).astype(BF16)
    gram = lax.dot_general(near, near, (((1,), (1,)), ((), ())), preferred_element_type=F32)
    high = gram.astype(BF16)
    gram_ref[0, :length] = high
    gram_ref[0, length:] = (gram - high.astype(F32)).astype(BF16)
    scale_ref[0] = jnp.broadcast_to(scale, (length, 128))


def row_mass_kernel(acts_ref, gram_ref, scale_ref, mass_ref):
    length = acts_ref.shape[1]
    total = jnp.zeros((1, acts_ref.shape[2]), F32)
    for seq in range(acts_ref.shape[0]):
        acts = acts_ref[seq].astype(F32) * scale_ref[seq][:, :1]
        spread = jnp.dot(gram_ref[seq], acts.astype(BF16), preferred_element_type=F32)
        spread = spread[:length] + spread[length:]
        total = total + jnp.sum(spread * acts, axis=0, keepdims=True)
    mass_ref[...] = total


def local_mass(activations, out_grads, valid_len, after):
    seqs, length, width = activations.shape
    cols = out_grads.shape[2]
    whole = lambda seq, valid: (seq, 0, 0)
    gram, scale = pl.pallas_call(
        token_gram_kernel,
        out_shape=(
            jax.ShapeDtypeStruct((seqs, 2 * length, length), BF16),
            jax.ShapeDtypeStruct((seqs, length, 128), F32),
        ),
        grid_spec=pltpu.PrefetchScalarGridSpec(
            num_scalar_prefetch=1,
            grid=(seqs,),
            in_specs=[
                pl.BlockSpec((1, length, cols), whole),
                pl.BlockSpec(memory_space=pl.ANY),
            ],
            out_specs=(
                pl.BlockSpec((1, 2 * length, length), whole),
                pl.BlockSpec((1, length, 128), whole),
            ),
        ),
        compiler_params=pltpu.CompilerParams(vmem_limit_bytes=LIMIT),
        cost_estimate=pl.CostEstimate(
            flops=2 * seqs * length * length * cols,
            bytes_accessed=2 * out_grads.size,
            transcendentals=0,
        ),
        name="token_gram",
    )(valid_len, out_grads, after)
    tile = math.gcd(width, 1024)
    fixed = lambda i: (0, 0, 0)
    mass = pl.pallas_call(
        row_mass_kernel,
        out_shape=jax.ShapeDtypeStruct((1, width), F32),
        grid=(width // tile,),
        in_specs=[
            pl.BlockSpec((seqs, length, tile), lambda i: (0, 0, i)),
            pl.BlockSpec((seqs, 2 * length, length), fixed),
            pl.BlockSpec((seqs, length, 128), fixed),
        ],
        out_specs=pl.BlockSpec((1, tile), lambda i: (0, i)),
        compiler_params=pltpu.CompilerParams(vmem_limit_bytes=LIMIT),
        cost_estimate=pl.CostEstimate(
            flops=4 * seqs * length * length * width,
            bytes_accessed=2 * activations.size,
            transcendentals=0,
        ),
        name="row_mass",
    )(activations, gram, scale)
    return mass.reshape(width)


def invert_block(tile):
    size = tile.shape[0]
    groups = [tile[i : i + 8] for i in range(0, size, 8)]
    lane = lax.broadcasted_iota(jnp.int32, (8, size), 1)
    sub = lax.broadcasted_iota(jnp.int32, (8, size), 0)
    done = []
    for g in range(size // 8):
        base = 8 * g
        inside = (lane >= base) & (lane < base + 8)
        now = groups[g]
        column = [jnp.broadcast_to(now[:, base + j : base + j + 1], (8, size)) for j in range(8)]
        now = jnp.where(inside, jnp.where(lane - base == sub, 1.0, 0.0), now)
        out, pivots, inverses = (jnp.ones((8, size), F32) for _ in range(3))
        for k in range(8):
            here = sub == k
            pivot = jnp.broadcast_to(column[k][k : k + 1], (8, size))
            inverse = 1.0 / pivot
            out, pivots = jnp.where(here, now, out), jnp.where(here, pivot, pivots)
            inverses = jnp.where(here, inverse, inverses)
            factor = jnp.where(here, 0.0, column[k])
            now = now - factor * jnp.broadcast_to(now[k : k + 1], (8, size)) * inverse
            for j in range(k + 1, 8):
                across = jnp.broadcast_to(column[j][k : k + 1], (8, size))
                column[j] = column[j] - factor * across * inverse
        now = now * inverses
        done.append(jnp.where(lane < base + 8, out * lax.rsqrt(pivots), 0.0))
        rows = [jnp.broadcast_to(now[s : s + 1], (8, size)) for s in range(8)]
        for i in range(g + 1, size // 8):
            left = groups[i]
            kept = jnp.where(inside, 0.0, left)
            for s in range(8):
                weight = jnp.broadcast_to(left[:, base + s : base + s + 1], (8, size))
                kept = kept - weight * rows[s]
            groups[i] = kept
    return jnp.concatenate(done)


def inverse_factor_kernel(gram_ref, out_ref, work_ref):
    size = gram_ref.shape[0]
    block = 128
    count = size // block
    work_ref[...] = gram_ref[...]
    lane = lax.broadcasted_iota(jnp.int32, (block, size), 1)

    def step(k, carry):
        base = pl.multiple_of(k * block, block)
        here = pl.ds(base, block)
        small = invert_block(work_ref[here, here])
        inside = (lane >= base) & (lane < base + block)
        eye = lax.broadcasted_iota(jnp.int32, (block, size), 0) == lane - base
        rows = jnp.where(inside, jnp.where(eye, 1.0, 0.0), work_ref[here, :])
        rows = jnp.dot(small, rows, precision=lax.Precision.HIGHEST, preferred_element_type=F32)
        out_ref[here, :] = jnp.where(lane < base + block, rows, 0.0)
        work_ref[here, :] = rows

        def update(i, carry):
            there = pl.ds(pl.multiple_of(i * block, block), block)
            left = work_ref[here, there]
            old = jnp.where(inside, 0.0, work_ref[there, :])
            work_ref[there, :] = old - lax.dot_general(
                left,
                rows,
                (((0,), (0,)), ((), ())),
                precision=lax.Precision.HIGHEST,
                preferred_element_type=F32,
            )
            return carry

        return lax.fori_loop(k + 1, count, update, carry)

    lax.fori_loop(0, count, step, 0)


def inverse_factor(gram):
    size = gram.shape[0]
    return pl.pallas_call(
        inverse_factor_kernel,
        out_shape=jax.ShapeDtypeStruct((size, size), F32),
        in_specs=[pl.BlockSpec(memory_space=pltpu.VMEM)],
        out_specs=pl.BlockSpec(memory_space=pltpu.VMEM),
        scratch_shapes=[pltpu.VMEM((size, size), F32)],
        compiler_params=pltpu.CompilerParams(vmem_limit_bytes=LIMIT),
        cost_estimate=pl.CostEstimate(
            flops=40 * size**3, bytes_accessed=8 * size * size, transcendentals=size
        ),
        name="inverse_factor",
    )(gram)


LIMIT = 16 << 20


def dot(left, right, dims=((1,), (0,))):
    return lax.dot_general(left, right, (dims, ((), ())), preferred_element_type=F32)


NT = ((1,), (1,))


def gather_rows(order_ref, sum_ref, send_ref, keep_ref, turned):
    half = send_ref.shape[0]
    block = sum_ref.shape[0] // (2 * half)
    for i in range(2 * half):
        here = pl.ds(pl.multiple_of(order_ref[i] * block, block), block)
        value = sum_ref[here, :]
        value = value.T if turned else value
        target = send_ref if i < half else keep_ref
        target[i % half] = value.astype(target.dtype)


def two_halves(size, shape, send_type):
    dims = (size // 2,) + shape
    return (jax.ShapeDtypeStruct(dims, send_type), jax.ShapeDtypeStruct(dims, F32))


def product_call(kernel, name, out_shape, scratch, weight, width, indices, arrays):
    height, depth = weight.shape
    smem, vmem = (pl.BlockSpec(memory_space=space) for space in (pltpu.SMEM, pltpu.VMEM))
    return pl.pallas_call(
        kernel,
        out_shape=out_shape,
        in_specs=[smem] * len(indices) + [vmem] * (1 + len(arrays)),
        out_specs=(vmem, vmem),
        scratch_shapes=[scratch],
        compiler_params=pltpu.CompilerParams(vmem_limit_bytes=LIMIT),
        cost_estimate=pl.CostEstimate(
            flops=2 * height * depth * width,
            bytes_accessed=2 * (height + width) * depth,
            transcendentals=0,
        ),
        name=name,
    )(*indices, weight, *arrays)


def rows_plain_kernel(
    part, width, turned, order_ref, weight_ref, right_ref, send_ref, keep_ref, sum_ref
):
    depth = weight_ref.shape[1]
    chunk = 512 if depth % 512 == 0 else depth

    def term(start):
        here = pl.ds(start, chunk)
        return dot(weight_ref[:, here], right_ref[here, part * width : (part + 1) * width])

    sum_ref[...] = term(0)

    @pl.loop(1, depth // chunk)
    def _(i):
        sum_ref[...] += term(pl.multiple_of(i * chunk, chunk))

    gather_rows(order_ref, sum_ref, send_ref, keep_ref, turned)


def rows_times(weight, right, part, width, rows, turned):
    height = weight.shape[0]
    block = height // rows.size
    shapes = two_halves(rows.size, (width, block) if turned else (block, width), F32)
    return product_call(
        functools.partial(rows_plain_kernel, part, width, turned),
        "rows_times",
        shapes,
        pltpu.VMEM((height, width), F32),
        weight,
        width,
        (rows.sending_first(),),
        (right,),
    )


def rows_joined_kernel(rows_ref, cols_ref, weight_ref, first_ref, second_ref, send_ref, keep_ref, sum_ref):
    half, _, own = first_ref.shape

    def term(part, i):
        block = cols_ref[i + half * (1 - part)]
        here = pl.ds(pl.multiple_of(block * own, 128), own)
        return dot(weight_ref[:, here], (first_ref, second_ref)[part][i], NT)

    sum_ref[...] = term(0, 0)
    for part in range(2):

        @pl.loop(1 - part, half)
        def _(i):
            sum_ref[...] += term(part, i)

    gather_rows(rows_ref, sum_ref, send_ref, keep_ref, False)


def rows_times_joined(weight, halves, rows, cols):
    height = weight.shape[0]
    width, own = halves[0].shape[1:]
    if own % 128:
        return rows_times(weight, cols.in_order(halves, 1).T, 0, width, rows, False)
    return product_call(
        rows_joined_kernel,
        "rows_times_joined",
        two_halves(rows.size, (height // rows.size, width), BF16),
        pltpu.VMEM((height, width), F32),
        weight,
        width,
        (rows.sending_first(), cols.sending_first()),
        halves,
    )


def cols_kernel(
    cols_ref, rows_ref, weight_ref, scale_ref, first_ref, second_ref, send_ref, keep_ref, whole_ref
):
    count, _, own = first_ref.shape
    for v in range(2 * count):
        block = rows_ref[(v + count) % (2 * count)]
        there = pl.ds(pl.multiple_of(block * own, 128), own)
        value = (first_ref, second_ref)[v // count][v % count]
        whole_ref[:, there] = (value.astype(F32) * scale_ref[:, there]).astype(BF16)

    half, _, block = send_ref.shape
    for part, out_ref in enumerate((send_ref, keep_ref)):

        @pl.loop(0, half)
        def _(i):
            here = pl.ds(pl.multiple_of(cols_ref[i + half * part] * block, 128), block)
            out_ref[i] = dot(whole_ref[...], weight_ref[:, here]).astype(out_ref.dtype)


def cols_times_joined(weight, scale, halves, rows, cols):
    height, depth = weight.shape
    block = depth // cols.size
    width, own = halves[0].shape[1:]
    if own % 128 or block % 128:
        left = (scale * rows.in_order(halves, 1)).astype(BF16)
        full = dot(left, weight).reshape(width, cols.size, block)
        order = cols.sending_first()
        full = jnp.stack([full[:, order[i]] for i in range(cols.size)])
        return full[: cols.size // 2].astype(BF16), full[cols.size // 2 :]
    return product_call(
        cols_kernel,
        "cols_times_joined",
        two_halves(cols.size, (width, block), BF16),
        pltpu.VMEM((width, height), BF16),
        weight,
        width,
        (cols.sending_first(), rows.sending_first()),
        (scale[None], *halves),
    )


def rank_kernel(weight_ref, basis_ref, out_ref):
    depth = weight_ref.shape[1]
    tile = math.gcd(depth, 512)

    @pl.loop(0, depth // tile)
    def _(i):
        here = pl.ds(pl.multiple_of(i * tile, tile), tile)
        out_ref[:, here] = dot(basis_ref[...], weight_ref[:, here]).astype(BF16)


def rank_times(weight, basis):
    height, depth = weight.shape
    if depth % 512:
        return dot(basis, weight).astype(BF16)
    vmem = pl.BlockSpec(memory_space=pltpu.VMEM)
    return pl.pallas_call(
        rank_kernel,
        out_shape=jax.ShapeDtypeStruct((basis.shape[0], depth), BF16),
        in_specs=[vmem, vmem],
        out_specs=vmem,
        compiler_params=pltpu.CompilerParams(vmem_limit_bytes=LIMIT),
        cost_estimate=pl.CostEstimate(
            flops=2 * height * depth * basis.shape[0],
            bytes_accessed=2 * (height + basis.shape[0]) * depth,
            transcendentals=0,
        ),
        name="rank_times",
    )(weight, basis)


def settle_kernel(order_ref, *refs):
    out_ref = refs[-1]
    count, block, half = refs[0].shape
    for v in range(2 * count):
        at = order_ref[(v + count) % (2 * count)] * block
        there = pl.ds(pl.multiple_of(at, block), block)
        for part in range(2):
            out_ref[there, part * half : (part + 1) * half] = refs[2 * part + v // count][v % count]


def settle(left, right, rows):
    count, block, half = left[0].shape
    if half % 128 or block % 16:
        return jnp.concatenate([rows.in_order(side, 0) for side in (left, right)], 1)
    vmem = pl.BlockSpec(memory_space=pltpu.VMEM)
    return pl.pallas_call(
        settle_kernel,
        out_shape=jax.ShapeDtypeStruct((2 * count * block, 2 * half), BF16),
        in_specs=[pl.BlockSpec(memory_space=pltpu.SMEM)] + [vmem] * 4,
        out_specs=vmem,
        compiler_params=pltpu.CompilerParams(vmem_limit_bytes=LIMIT),
        cost_estimate=pl.CostEstimate(
            flops=0, bytes_accessed=16 * count * block * half, transcendentals=0
        ),
        name="settle",
    )(rows.sending_first(), *left, *right)


def local(activations, out_grads, valid_len, weight, sketch):
    width = activations.shape[2]
    rows_here, cols_here = weight.shape
    rank = sketch.shape[1]
    half = rank // 2
    row_count, col_count = lax.axis_size("row"), lax.axis_size("col")
    row, col = lax.axis_index("row"), lax.axis_index("col")
    own_rows = rows_here // col_count
    over_col, over_row = Halving("col"), Halving("row")

    raw, later = (rows_times(weight, sketch, part, half, over_col, True) for part in range(2))
    mass = local_mass(activations, out_grads, valid_len, later[1])
    mass = mass.reshape(-1, own_rows)
    raw = over_col.scatter_sum(*raw)
    later, fisher = over_col.scatter_sum(*later, mass)
    fisher = sum_everywhere(fisher, col=False).reshape(width)
    mean = jnp.sum(fisher) / width + 1e-06
    square_scale = lax.dynamic_slice_in_dim(fisher, row * rows_here, rows_here) / mean
    own_square = lax.dynamic_slice_in_dim(square_scale, col * own_rows, own_rows)

    def second_of(raw):
        first = over_col.gather(raw.astype(BF16))
        parts = cols_times_joined(weight, square_scale, first, over_col, over_row)
        projected = over_row.gather(over_row.scatter_sum(*parts).astype(BF16))
        parts = rows_times_joined(weight, projected, over_col, over_row)
        return over_col.gather(over_col.scatter_sum(*parts).astype(BF16))

    second = settle(second_of(raw), second_of(later), over_col)

    even = (col & 1) == 0
    mine = lax.dynamic_slice_in_dim(second, (col & 1) * half, half, 1).astype(F32)
    rows_of = ((0,), (0,))
    gram = sum(dot(term, second, rows_of) for term in split(square_scale[:, None] * mine))
    gram = sum_everywhere(gram, col=False)
    other = swap(gram, lambda parity: 0, lambda parity: 1)
    gram = jnp.concatenate([jnp.where(even, gram, other), jnp.where(even, other, gram)])

    inverse = inverse_factor(gram)
    order = over_row.sending_first()
    blocks = inverse.reshape(row_count, rank // row_count, rank)

    def coeffs_of(places):
        part = [lax.dynamic_index_in_dim(blocks, order[i], 0, keepdims=False) for i in places]
        high, low = split(jnp.concatenate(part))
        basis = (dot(high, second, NT) + dot(low, second, NT)) * square_scale
        return rank_times(weight, basis.astype(BF16)).reshape(len(part), -1, cols_here)

    coeffs = over_row.scatter_sum(
        coeffs_of(range(row_count // 2)), coeffs_of(range(row_count // 2, row_count))
    )

    own = lax.dynamic_slice_in_dim(second, col * own_rows, own_rows)
    basis = sum(dot(own, term, NT) for term in split(inverse))
    basis = basis * (jnp.sqrt(own_square)[:, None] * math.sqrt(width))
    return basis, coeffs * math.sqrt(cols_here * col_count)


def solution(mesh):
    placed = (
        P("row", None, None),
        P("row", None, "col"),
        P("row"),
        P("row", "col"),
        P("col", None),
    )
    return jax.shard_map(
        local,
        mesh=mesh,
        in_specs=placed,
        out_specs=(P(("row", "col"), None), P("row", "col")),
        check_vma=False,
    )
```

```python
import functools
import math

import jax
import jax.numpy as jnp
from jax import lax
from jax.experimental import pallas as pl
from jax.experimental.pallas import tpu as pltpu
from jax.sharding import PartitionSpec as P

AXES = ("row", "col")
F32 = jnp.float32
BF16 = jnp.bfloat16


def swap(block, row_bit, col_bit):
    rows, cols = lax.axis_size("row"), lax.axis_size("col")
    pairs = []
    for row in range(rows):
        for col in range(cols):
            other = (row ^ row_bit(col & 1)) * cols + (col ^ col_bit(col & 1))
            pairs.append((row * cols + col, other))
    return lax.ppermute(block, AXES, pairs)


def split(value):
    high = lax.reduce_precision(value, 8, 7)
    return high.astype(BF16), (value - high).astype(BF16)


class Halving:
    def __init__(self, axis):
        self.axis = axis
        self.size = lax.axis_size(axis)
        bits = list(range(self.size.bit_length() - 1))
        if axis == "col":
            self.orders = (bits, bits[:1] + bits[:0:-1])
        else:
            self.orders = (bits, bits[::-1])
        self.me = lax.axis_index(axis)
        self.odd = lax.axis_index("col") & 1
        steps = len(bits)
        self.masks = tuple(
            [
                sum(1 << order[t] for t in range(steps) if v >> (steps - 1 - t) & 1)
                for v in range(self.size)
            ]
            for order in self.orders
        )
        if axis == "col":
            half = self.size // 2
            even, odd = (masks[:half] for masks in self.masks)
            self.masks = (even + [1 ^ mask for mask in odd], odd + [1 ^ mask for mask in even])

    def block(self, v):
        even, odd = (masks[v] for masks in self.masks)
        return self.me ^ (even if even == odd else jnp.where(self.odd == 0, even, odd))

    def step(self, t, block):
        even, odd = (1 << order[t] for order in self.orders)
        pick = lambda parity: odd if parity else even
        none = lambda parity: 0
        return swap(block, *((none, pick) if self.axis == "col" else (pick, none)))

    def sending_first(self):
        half = self.size // 2
        places = [*range(half, self.size), *range(half)]
        return jnp.stack([self.block(v) for v in places]).astype(jnp.int32)

    def scatter_sum(self, send, keep, rider=None):
        terms = [keep]
        for t in range(len(self.orders[0])):
            came = self.step(t, send)
            if rider is not None:
                if t == 0:
                    rider = rider + self.step(t, rider)
                else:
                    height = rider.shape[0]
                    *parts, blocks = jnp.split(came, [height, 2 * height])
                    rider = rider + sum(part.astype(F32) for part in parts)
                    came = blocks.reshape(terms[0].shape)
            terms.append(came)
            half = terms[0].shape[0] // 2
            add = lambda part: sum(term[part].astype(F32) for term in terms)
            if half:
                send = add(slice(half, None)).astype(BF16)
                terms = [term[:half] for term in terms]
                if rider is not None:
                    parts = split(rider)
                    rider = sum(part.astype(F32) for part in parts)
                    send = jnp.concatenate([*parts, send.reshape(-1, send.shape[-1])])
        return add(0) if rider is None else (add(0), rider)

    def gather(self, own):
        now = own[None]
        for t in reversed(range(len(self.orders[0]))):
            came = self.step(t, now)
            if t:
                now = jnp.concatenate([now, came])
        return now, came

    def in_order(self, halves, axis):
        virtual = jnp.concatenate(halves)
        places = []
        for masks in self.masks:
            inverse = [0] * self.size
            for v, mask in enumerate(masks):
                inverse[mask] = v
            places.append(jnp.array(inverse, jnp.int32))
        place = jnp.where(self.odd == 0, places[0], places[1])
        take = lambda j: lax.dynamic_index_in_dim(
            virtual, place[self.me ^ j], 0, keepdims=False
        )
        return jnp.concatenate([take(j) for j in range(self.size)], axis)


def sum_everywhere(value, row=True, col=True):
    none = lambda parity: 0
    if col:
        for bit in range(lax.axis_size("col").bit_length() - 1):
            value = value + swap(value, none, lambda parity: 1 << bit)
    if row:
        steps = lax.axis_size("row").bit_length() - 1
        for t in range(steps):
            pick = lambda parity: 1 << (steps - 1 - t if parity else t)
            value = value + swap(value, pick, none)
    return value


def token_gram_kernel(valid_ref, grads_ref, after_ref, gram_ref, scale_ref):
    seq = pl.program_id(0)
    length = grads_ref.shape[1]
    tokens = lax.broadcasted_iota(jnp.int32, (length, 1), 0)
    grads = grads_ref[0].astype(F32)
    grads = jnp.where(tokens < valid_ref[seq], grads, 0.0)
    largest = jnp.max(jnp.abs(grads), axis=1, keepdims=True)
    scale = jnp.ones_like(largest)
    shrink = jnp.ones_like(largest)
    for power in (16, 48, 80):
        step = 2.0 ** (power + 16)
        high, low = largest >= 2.0**power, largest < 2.0**-power
        scale = jnp.where(high, step, jnp.where(low, 1.0 / step, scale))
        shrink = jnp.where(high, 1.0 / step, jnp.where(low, step, shrink))
    near = (grads * shrink).astype(BF16)
    gram = lax.dot_general(near, near, (((1,), (1,)), ((), ())), preferred_element_type=F32)
    high = gram.astype(BF16)
    gram_ref[0, :length] = high
    gram_ref[0, length:] = (gram - high.astype(F32)).astype(BF16)
    scale_ref[0] = jnp.broadcast_to(scale, (length, 128))


def row_mass_kernel(acts_ref, gram_ref, scale_ref, mass_ref):
    length = acts_ref.shape[1]
    total = jnp.zeros((1, acts_ref.shape[2]), F32)
    for seq in range(acts_ref.shape[0]):
        acts = acts_ref[seq].astype(F32) * scale_ref[seq][:, :1]
        spread = jnp.dot(gram_ref[seq], acts.astype(BF16), preferred_element_type=F32)
        spread = spread[:length] + spread[length:]
        total = total + jnp.sum(spread * acts, axis=0, keepdims=True)
    mass_ref[...] = total


def local_mass(activations, out_grads, valid_len, after):
    seqs, length, width = activations.shape
    cols = out_grads.shape[2]
    whole = lambda seq, valid: (seq, 0, 0)
    gram, scale = pl.pallas_call(
        token_gram_kernel,
        out_shape=(
            jax.ShapeDtypeStruct((seqs, 2 * length, length), BF16),
            jax.ShapeDtypeStruct((seqs, length, 128), F32),
        ),
        grid_spec=pltpu.PrefetchScalarGridSpec(
            num_scalar_prefetch=1,
            grid=(seqs,),
            in_specs=[
                pl.BlockSpec((1, length, cols), whole),
                pl.BlockSpec(memory_space=pl.ANY),
            ],
            out_specs=(
                pl.BlockSpec((1, 2 * length, length), whole),
                pl.BlockSpec((1, length, 128), whole),
            ),
        ),
        compiler_params=pltpu.CompilerParams(vmem_limit_bytes=LIMIT),
        cost_estimate=pl.CostEstimate(
            flops=2 * seqs * length * length * cols,
            bytes_accessed=2 * out_grads.size,
            transcendentals=0,
        ),
        name="token_gram",
    )(valid_len, out_grads, after)
    tile = math.gcd(width, 1024)
    fixed = lambda i: (0, 0, 0)
    mass = pl.pallas_call(
        row_mass_kernel,
        out_shape=jax.ShapeDtypeStruct((1, width), F32),
        grid=(width // tile,),
        in_specs=[
            pl.BlockSpec((seqs, length, tile), lambda i: (0, 0, i)),
            pl.BlockSpec((seqs, 2 * length, length), fixed),
            pl.BlockSpec((seqs, length, 128), fixed),
        ],
        out_specs=pl.BlockSpec((1, tile), lambda i: (0, i)),
        compiler_params=pltpu.CompilerParams(vmem_limit_bytes=LIMIT),
        cost_estimate=pl.CostEstimate(
            flops=4 * seqs * length * length * width,
            bytes_accessed=2 * activations.size,
            transcendentals=0,
        ),
        name="row_mass",
    )(activations, gram, scale)
    return mass.reshape(width)


def invert_block(tile):
    size = tile.shape[0]
    groups = [tile[i : i + 8] for i in range(0, size, 8)]
    lane = lax.broadcasted_iota(jnp.int32, (8, size), 1)
    sub = lax.broadcasted_iota(jnp.int32, (8, size), 0)
    done = []
    for g in range(size // 8):
        base = 8 * g
        inside = (lane >= base) & (lane < base + 8)
        now = groups[g]
        column = [jnp.broadcast_to(now[:, base + j : base + j + 1], (8, size)) for j in range(8)]
        now = jnp.where(inside, jnp.where(lane - base == sub, 1.0, 0.0), now)
        out, pivots, inverses = (jnp.ones((8, size), F32) for _ in range(3))
        for k in range(8):
            here = sub == k
            pivot = jnp.broadcast_to(column[k][k : k + 1], (8, size))
            inverse = 1.0 / pivot
            out, pivots = jnp.where(here, now, out), jnp.where(here, pivot, pivots)
            inverses = jnp.where(here, inverse, inverses)
            factor = jnp.where(here, 0.0, column[k])
            now = now - factor * jnp.broadcast_to(now[k : k + 1], (8, size)) * inverse
            for j in range(k + 1, 8):
                across = jnp.broadcast_to(column[j][k : k + 1], (8, size))
                column[j] = column[j] - factor * across * inverse
        now = now * inverses
        done.append(jnp.where(lane < base + 8, out * lax.rsqrt(pivots), 0.0))
        rows = [jnp.broadcast_to(now[s : s + 1], (8, size)) for s in range(8)]
        for i in range(g + 1, size // 8):
            left = groups[i]
            kept = jnp.where(inside, 0.0, left)
            for s in range(8):
                weight = jnp.broadcast_to(left[:, base + s : base + s + 1], (8, size))
                kept = kept - weight * rows[s]
            groups[i] = kept
    return jnp.concatenate(done)


def inverse_factor_kernel(gram_ref, out_ref, work_ref):
    size = gram_ref.shape[0]
    block = 128
    count = size // block
    work_ref[...] = gram_ref[...]
    lane = lax.broadcasted_iota(jnp.int32, (block, size), 1)

    def step(k, carry):
        base = pl.multiple_of(k * block, block)
        here = pl.ds(base, block)
        small = invert_block(work_ref[here, here])
        inside = (lane >= base) & (lane < base + block)
        eye = lax.broadcasted_iota(jnp.int32, (block, size), 0) == lane - base
        rows = jnp.where(inside, jnp.where(eye, 1.0, 0.0), work_ref[here, :])
        rows = jnp.dot(small, rows, precision=lax.Precision.HIGHEST, preferred_element_type=F32)
        out_ref[here, :] = jnp.where(lane < base + block, rows, 0.0)
        work_ref[here, :] = rows

        def update(i, carry):
            there = pl.ds(pl.multiple_of(i * block, block), block)
            left = work_ref[here, there]
            old = jnp.where(inside, 0.0, work_ref[there, :])
            work_ref[there, :] = old - lax.dot_general(
                left,
                rows,
                (((0,), (0,)), ((), ())),
                precision=lax.Precision.HIGHEST,
                preferred_element_type=F32,
            )
            return carry

        return lax.fori_loop(k + 1, count, update, carry)

    lax.fori_loop(0, count, step, 0)


def inverse_factor(gram):
    size = gram.shape[0]
    return pl.pallas_call(
        inverse_factor_kernel,
        out_shape=jax.ShapeDtypeStruct((size, size), F32),
        in_specs=[pl.BlockSpec(memory_space=pltpu.VMEM)],
        out_specs=pl.BlockSpec(memory_space=pltpu.VMEM),
        scratch_shapes=[pltpu.VMEM((size, size), F32)],
        compiler_params=pltpu.CompilerParams(vmem_limit_bytes=LIMIT),
        cost_estimate=pl.CostEstimate(
            flops=40 * size**3, bytes_accessed=8 * size * size, transcendentals=size
        ),
        name="inverse_factor",
    )(gram)


LIMIT = 16 << 20


def dot(left, right, dims=((1,), (0,))):
    return lax.dot_general(left, right, (dims, ((), ())), preferred_element_type=F32)


NT = ((1,), (1,))


def gather_rows(order_ref, sum_ref, send_ref, keep_ref, turned):
    half = send_ref.shape[0]
    block = sum_ref.shape[0] // (2 * half)
    for i in range(2 * half):
        here = pl.ds(pl.multiple_of(order_ref[i] * block, block), block)
        value = sum_ref[here, :]
        value = value.T if turned else value
        target = send_ref if i < half else keep_ref
        target[i % half] = value.astype(target.dtype)


def two_halves(size, shape, send_type):
    dims = (size // 2,) + shape
    return (jax.ShapeDtypeStruct(dims, send_type), jax.ShapeDtypeStruct(dims, F32))


def product_call(kernel, name, out_shape, scratch, weight, width, indices, arrays):
    height, depth = weight.shape
    smem, vmem = (pl.BlockSpec(memory_space=space) for space in (pltpu.SMEM, pltpu.VMEM))
    return pl.pallas_call(
        kernel,
        out_shape=out_shape,
        in_specs=[smem] * len(indices) + [vmem] * (1 + len(arrays)),
        out_specs=(vmem, vmem),
        scratch_shapes=[scratch],
        compiler_params=pltpu.CompilerParams(vmem_limit_bytes=LIMIT),
        cost_estimate=pl.CostEstimate(
            flops=2 * height * depth * width,
            bytes_accessed=2 * (height + width) * depth,
            transcendentals=0,
        ),
        name=name,
    )(*indices, weight, *arrays)


def rows_plain_kernel(
    part, width, turned, order_ref, weight_ref, right_ref, send_ref, keep_ref, sum_ref
):
    depth = weight_ref.shape[1]
    chunk = 512 if depth % 512 == 0 else depth

    def term(start):
        here = pl.ds(start, chunk)
        return dot(weight_ref[:, here], right_ref[here, part * width : (part + 1) * width])

    sum_ref[...] = term(0)

    @pl.loop(1, depth // chunk)
    def _(i):
        sum_ref[...] += term(pl.multiple_of(i * chunk, chunk))

    gather_rows(order_ref, sum_ref, send_ref, keep_ref, turned)


def rows_times(weight, right, part, width, rows, turned):
    height = weight.shape[0]
    block = height // rows.size
    shapes = two_halves(rows.size, (width, block) if turned else (block, width), F32)
    return product_call(
        functools.partial(rows_plain_kernel, part, width, turned),
        "rows_times",
        shapes,
        pltpu.VMEM((height, width), F32),
        weight,
        width,
        (rows.sending_first(),),
        (right,),
    )


def rows_joined_kernel(rows_ref, cols_ref, weight_ref, first_ref, second_ref, send_ref, keep_ref, sum_ref):
    half, _, own = first_ref.shape

    def term(part, i):
        block = cols_ref[i + half * (1 - part)]
        here = pl.ds(pl.multiple_of(block * own, 128), own)
        return dot(weight_ref[:, here], (first_ref, second_ref)[part][i], NT)

    sum_ref[...] = term(0, 0)
    for part in range(2):

        @pl.loop(1 - part, half)
        def _(i):
            sum_ref[...] += term(part, i)

    gather_rows(rows_ref, sum_ref, send_ref, keep_ref, False)


def rows_times_joined(weight, halves, rows, cols):
    height = weight.shape[0]
    width, own = halves[0].shape[1:]
    if own % 128:
        return rows_times(weight, cols.in_order(halves, 1).T, 0, width, rows, False)
    return product_call(
        rows_joined_kernel,
        "rows_times_joined",
        two_halves(rows.size, (height // rows.size, width), BF16),
        pltpu.VMEM((height, width), F32),
        weight,
        width,
        (rows.sending_first(), cols.sending_first()),
        halves,
    )


def cols_kernel(
    cols_ref, rows_ref, weight_ref, scale_ref, first_ref, second_ref, send_ref, keep_ref, whole_ref
):
    count, _, own = first_ref.shape
    for v in range(2 * count):
        block = rows_ref[(v + count) % (2 * count)]
        there = pl.ds(pl.multiple_of(block * own, 128), own)
        value = (first_ref, second_ref)[v // count][v % count]
        whole_ref[:, there] = (value.astype(F32) * scale_ref[:, there]).astype(BF16)

    half, _, block = send_ref.shape
    for part, out_ref in enumerate((send_ref, keep_ref)):

        @pl.loop(0, half)
        def _(i):
            here = pl.ds(pl.multiple_of(cols_ref[i + half * part] * block, 128), block)
            out_ref[i] = dot(whole_ref[...], weight_ref[:, here]).astype(out_ref.dtype)


def cols_times_joined(weight, scale, halves, rows, cols):
    height, depth = weight.shape
    block = depth // cols.size
    width, own = halves[0].shape[1:]
    if own % 128 or block % 128:
        left = (scale * rows.in_order(halves, 1)).astype(BF16)
        full = dot(left, weight).reshape(width, cols.size, block)
        order = cols.sending_first()
        full = jnp.stack([full[:, order[i]] for i in range(cols.size)])
        return full[: cols.size // 2].astype(BF16), full[cols.size // 2 :]
    return product_call(
        cols_kernel,
        "cols_times_joined",
        two_halves(cols.size, (width, block), BF16),
        pltpu.VMEM((width, height), BF16),
        weight,
        width,
        (cols.sending_first(), rows.sending_first()),
        (scale[None], *halves),
    )


def rank_kernel(weight_ref, basis_ref, out_ref):
    depth = weight_ref.shape[1]
    tile = math.gcd(depth, 512)

    @pl.loop(0, depth // tile)
    def _(i):
        here = pl.ds(pl.multiple_of(i * tile, tile), tile)
        out_ref[:, here] = dot(basis_ref[...], weight_ref[:, here]).astype(BF16)


def rank_times(weight, basis):
    height, depth = weight.shape
    if depth % 512:
        return dot(basis, weight).astype(BF16)
    vmem = pl.BlockSpec(memory_space=pltpu.VMEM)
    return pl.pallas_call(
        rank_kernel,
        out_shape=jax.ShapeDtypeStruct((basis.shape[0], depth), BF16),
        in_specs=[vmem, vmem],
        out_specs=vmem,
        compiler_params=pltpu.CompilerParams(vmem_limit_bytes=LIMIT),
        cost_estimate=pl.CostEstimate(
            flops=2 * height * depth * basis.shape[0],
            bytes_accessed=2 * (height + basis.shape[0]) * depth,
            transcendentals=0,
        ),
        name="rank_times",
    )(weight, basis)


def settle_kernel(order_ref, *refs):
    out_ref = refs[-1]
    count, block, half = refs[0].shape
    for v in range(2 * count):
        at = order_ref[(v + count) % (2 * count)] * block
        there = pl.ds(pl.multiple_of(at, block), block)
        for part in range(2):
            out_ref[there, part * half : (part + 1) * half] = refs[2 * part + v // count][v % count]


def settle(left, right, rows):
    count, block, half = left[0].shape
    if half % 128 or block % 16:
        return jnp.concatenate([rows.in_order(side, 0) for side in (left, right)], 1)
    vmem = pl.BlockSpec(memory_space=pltpu.VMEM)
    return pl.pallas_call(
        settle_kernel,
        out_shape=jax.ShapeDtypeStruct((2 * count * block, 2 * half), BF16),
        in_specs=[pl.BlockSpec(memory_space=pltpu.SMEM)] + [vmem] * 4,
        out_specs=vmem,
        compiler_params=pltpu.CompilerParams(vmem_limit_bytes=LIMIT),
        cost_estimate=pl.CostEstimate(
            flops=0, bytes_accessed=16 * count * block * half, transcendentals=0
        ),
        name="settle",
    )(rows.sending_first(), *left, *right)


def local(activations, out_grads, valid_len, weight, sketch):
    width = activations.shape[2]
    rows_here, cols_here = weight.shape
    rank = sketch.shape[1]
    half = rank // 2
    row_count, col_count = lax.axis_size("row"), lax.axis_size("col")
    row, col = lax.axis_index("row"), lax.axis_index("col")
    own_rows = rows_here // col_count
    over_col, over_row = Halving("col"), Halving("row")

    raw, later = (rows_times(weight, sketch, part, half, over_col, True) for part in range(2))
    mass = local_mass(activations, out_grads, valid_len, later[1])
    mass = mass.reshape(-1, own_rows)
    raw = over_col.scatter_sum(*raw)
    later, fisher = over_col.scatter_sum(*later, mass)
    fisher = sum_everywhere(fisher, col=False).reshape(width)
    mean = jnp.sum(fisher) / width + 1e-06
    square_scale = lax.dynamic_slice_in_dim(fisher, row * rows_here, rows_here) / mean
    own_square = lax.dynamic_slice_in_dim(square_scale, col * own_rows, own_rows)

    def second_of(first, scale):
        first = over_col.gather(first.astype(BF16))
        parts = cols_times_joined(weight, scale, first, over_col, over_row)
        projected = over_row.gather(over_row.scatter_sum(*parts).astype(BF16))
        parts = rows_times_joined(weight, projected, over_col, over_row)
        return over_col.gather(over_col.scatter_sum(*parts).astype(BF16))

    second = settle(
        second_of(raw, square_scale),
        second_of(own_square * later, jnp.ones_like(square_scale)),
        over_col,
    )

    even = (col & 1) == 0
    mine = lax.dynamic_slice_in_dim(second, (col & 1) * half, half, 1).astype(F32)
    rows_of = ((0,), (0,))
    gram = sum(dot(term, second, rows_of) for term in split(square_scale[:, None] * mine))
    gram = sum_everywhere(gram, col=False)
    other = swap(gram, lambda parity: 0, lambda parity: 1)
    gram = jnp.concatenate([jnp.where(even, gram, other), jnp.where(even, other, gram)])

    inverse = inverse_factor(gram)
    order = over_row.sending_first()
    blocks = inverse.reshape(row_count, rank // row_count, rank)

    def coeffs_of(places):
        part = [lax.dynamic_index_in_dim(blocks, order[i], 0, keepdims=False) for i in places]
        high, low = split(jnp.concatenate(part))
        basis = (dot(high, second, NT) + dot(low, second, NT)) * square_scale
        return rank_times(weight, basis.astype(BF16)).reshape(len(part), -1, cols_here)

    coeffs = over_row.scatter_sum(
        coeffs_of(range(row_count // 2)), coeffs_of(range(row_count // 2, row_count))
    )

    own = lax.dynamic_slice_in_dim(second, col * own_rows, own_rows)
    basis = sum(dot(own, term, NT) for term in split(inverse))
    basis = basis * (jnp.sqrt(own_square)[:, None] * math.sqrt(width))
    return basis, coeffs * math.sqrt(cols_here * col_count)


def solution(mesh):
    placed = (
        P("row", None, None),
        P("row", None, "col"),
        P("row"),
        P("row", "col"),
        P("col", None),
    )
    return jax.shard_map(
        local,
        mesh=mesh,
        in_specs=placed,
        out_specs=(P(("row", "col"), None), P("row", "col")),
        check_vma=False,
    )
```

```python
import functools
import math

import jax
import jax.numpy as jnp
from jax import lax
from jax.experimental import pallas as pl
from jax.experimental.pallas import tpu as pltpu
from jax.sharding import PartitionSpec as P

AXES = ("row", "col")
F32 = jnp.float32
BF16 = jnp.bfloat16


def swap(block, row_bit, col_bit):
    rows, cols = lax.axis_size("row"), lax.axis_size("col")
    pairs = []
    for row in range(rows):
        for col in range(cols):
            other = (row ^ row_bit(col & 1)) * cols + (col ^ col_bit(col & 1))
            pairs.append((row * cols + col, other))
    return lax.ppermute(block, AXES, pairs)


def split(value):
    high = lax.reduce_precision(value, 8, 7)
    return high.astype(BF16), (value - high).astype(BF16)


class Halving:
    def __init__(self, axis):
        self.axis = axis
        self.size = lax.axis_size(axis)
        bits = list(range(self.size.bit_length() - 1))
        if axis == "col":
            self.orders = (bits, bits[:1] + bits[:0:-1])
        else:
            self.orders = (bits, bits[::-1])
        self.me = lax.axis_index(axis)
        self.odd = lax.axis_index("col") & 1
        steps = len(bits)
        self.masks = tuple(
            [
                sum(1 << order[t] for t in range(steps) if v >> (steps - 1 - t) & 1)
                for v in range(self.size)
            ]
            for order in self.orders
        )
        if axis == "col":
            half = self.size // 2
            even, odd = (masks[:half] for masks in self.masks)
            self.masks = (even + [1 ^ mask for mask in odd], odd + [1 ^ mask for mask in even])

    def block(self, v):
        even, odd = (masks[v] for masks in self.masks)
        return self.me ^ (even if even == odd else jnp.where(self.odd == 0, even, odd))

    def step(self, t, block):
        even, odd = (1 << order[t] for order in self.orders)
        pick = lambda parity: odd if parity else even
        none = lambda parity: 0
        return swap(block, *((none, pick) if self.axis == "col" else (pick, none)))

    def sending_first(self):
        half = self.size // 2
        places = [*range(half, self.size), *range(half)]
        return jnp.stack([self.block(v) for v in places]).astype(jnp.int32)

    def scatter_sum(self, send, keep, rider=None):
        terms = [keep]
        for t in range(len(self.orders[0])):
            came = self.step(t, send)
            if rider is not None:
                if t == 0:
                    rider = rider + self.step(t, rider)
                else:
                    height = rider.shape[0]
                    *parts, blocks = jnp.split(came, [height, 2 * height])
                    rider = rider + sum(part.astype(F32) for part in parts)
                    came = blocks.reshape(terms[0].shape)
            terms.append(came)
            half = terms[0].shape[0] // 2
            add = lambda part: sum(term[part].astype(F32) for term in terms)
            if half:
                send = add(slice(half, None)).astype(BF16)
                terms = [term[:half] for term in terms]
                if rider is not None:
                    parts = split(rider)
                    rider = sum(part.astype(F32) for part in parts)
                    send = jnp.concatenate([*parts, send.reshape(-1, send.shape[-1])])
        return add(0) if rider is None else (add(0), rider)

    def gather(self, own):
        now = own[None]
        for t in reversed(range(len(self.orders[0]))):
            came = self.step(t, now)
            if t:
                now = jnp.concatenate([now, came])
        return now, came

    def in_order(self, halves, axis):
        virtual = jnp.concatenate(halves)
        places = []
        for masks in self.masks:
            inverse = [0] * self.size
            for v, mask in enumerate(masks):
                inverse[mask] = v
            places.append(jnp.array(inverse, jnp.int32))
        place = jnp.where(self.odd == 0, places[0], places[1])
        take = lambda j: lax.dynamic_index_in_dim(
            virtual, place[self.me ^ j], 0, keepdims=False
        )
        return jnp.concatenate([take(j) for j in range(self.size)], axis)


def sum_everywhere(value, row=True, col=True):
    none = lambda parity: 0
    if col:
        for bit in range(lax.axis_size("col").bit_length() - 1):
            value = value + swap(value, none, lambda parity: 1 << bit)
    if row:
        steps = lax.axis_size("row").bit_length() - 1
        for t in range(steps):
            pick = lambda parity: 1 << (steps - 1 - t if parity else t)
            value = value + swap(value, pick, none)
    return value


def token_gram_kernel(valid_ref, grads_ref, after_ref, gram_ref, scale_ref):
    seq = pl.program_id(0)
    length = grads_ref.shape[1]
    tokens = lax.broadcasted_iota(jnp.int32, (length, 1), 0)
    grads = grads_ref[0].astype(F32)
    grads = jnp.where(tokens < valid_ref[seq], grads, 0.0)
    largest = jnp.max(jnp.abs(grads), axis=1, keepdims=True)
    scale = jnp.ones_like(largest)
    shrink = jnp.ones_like(largest)
    for power in (16, 48, 80):
        step = 2.0 ** (power + 16)
        high, low = largest >= 2.0**power, largest < 2.0**-power
        scale = jnp.where(high, step, jnp.where(low, 1.0 / step, scale))
        shrink = jnp.where(high, 1.0 / step, jnp.where(low, step, shrink))
    near = (grads * shrink).astype(BF16)
    gram = lax.dot_general(near, near, (((1,), (1,)), ((), ())), preferred_element_type=F32)
    high = gram.astype(BF16)
    gram_ref[0, :length] = high
    gram_ref[0, length:] = (gram - high.astype(F32)).astype(BF16)
    scale_ref[0] = jnp.broadcast_to(scale, (length, 128))


def row_mass_kernel(acts_ref, gram_ref, scale_ref, mass_ref):
    length = acts_ref.shape[1]
    total = jnp.zeros((1, acts_ref.shape[2]), F32)
    for seq in range(acts_ref.shape[0]):
        acts = acts_ref[seq].astype(F32) * scale_ref[seq][:, :1]
        spread = jnp.dot(gram_ref[seq], acts.astype(BF16), preferred_element_type=F32)
        spread = spread[:length] + spread[length:]
        total = total + jnp.sum(spread * acts, axis=0, keepdims=True)
    mass_ref[...] = total


def local_mass(activations, out_grads, valid_len, after):
    seqs, length, width = activations.shape
    cols = out_grads.shape[2]
    whole = lambda seq, valid: (seq, 0, 0)
    gram, scale = pl.pallas_call(
        token_gram_kernel,
        out_shape=(
            jax.ShapeDtypeStruct((seqs, 2 * length, length), BF16),
            jax.ShapeDtypeStruct((seqs, length, 128), F32),
        ),
        grid_spec=pltpu.PrefetchScalarGridSpec(
            num_scalar_prefetch=1,
            grid=(seqs,),
            in_specs=[
                pl.BlockSpec((1, length, cols), whole),
                pl.BlockSpec(memory_space=pl.ANY),
            ],
            out_specs=(
                pl.BlockSpec((1, 2 * length, length), whole),
                pl.BlockSpec((1, length, 128), whole),
            ),
        ),
        compiler_params=pltpu.CompilerParams(vmem_limit_bytes=LIMIT),
        cost_estimate=pl.CostEstimate(
            flops=2 * seqs * length * length * cols,
            bytes_accessed=2 * out_grads.size,
            transcendentals=0,
        ),
        name="token_gram",
    )(valid_len, out_grads, after)
    tile = math.gcd(width, 1024)
    fixed = lambda i: (0, 0, 0)
    mass = pl.pallas_call(
        row_mass_kernel,
        out_shape=jax.ShapeDtypeStruct((1, width), F32),
        grid=(width // tile,),
        in_specs=[
            pl.BlockSpec((seqs, length, tile), lambda i: (0, 0, i)),
            pl.BlockSpec((seqs, 2 * length, length), fixed),
            pl.BlockSpec((seqs, length, 128), fixed),
        ],
        out_specs=pl.BlockSpec((1, tile), lambda i: (0, i)),
        compiler_params=pltpu.CompilerParams(vmem_limit_bytes=LIMIT),
        cost_estimate=pl.CostEstimate(
            flops=4 * seqs * length * length * width,
            bytes_accessed=2 * activations.size,
            transcendentals=0,
        ),
        name="row_mass",
    )(activations, gram, scale)
    return mass.reshape(width)


def invert_block(tile):
    size = tile.shape[0]
    groups = [tile[i : i + 8] for i in range(0, size, 8)]
    lane = lax.broadcasted_iota(jnp.int32, (8, size), 1)
    sub = lax.broadcasted_iota(jnp.int32, (8, size), 0)
    done = []
    for g in range(size // 8):
        base = 8 * g
        inside = (lane >= base) & (lane < base + 8)
        now = groups[g]
        column = [jnp.broadcast_to(now[:, base + j : base + j + 1], (8, size)) for j in range(8)]
        now = jnp.where(inside, jnp.where(lane - base == sub, 1.0, 0.0), now)
        out, pivots, inverses = (jnp.ones((8, size), F32) for _ in range(3))
        for k in range(8):
            here = sub == k
            pivot = jnp.broadcast_to(column[k][k : k + 1], (8, size))
            inverse = 1.0 / pivot
            out, pivots = jnp.where(here, now, out), jnp.where(here, pivot, pivots)
            inverses = jnp.where(here, inverse, inverses)
            factor = jnp.where(here, 0.0, column[k])
            now = now - factor * jnp.broadcast_to(now[k : k + 1], (8, size)) * inverse
            for j in range(k + 1, 8):
                across = jnp.broadcast_to(column[j][k : k + 1], (8, size))
                column[j] = column[j] - factor * across * inverse
        now = now * inverses
        done.append(jnp.where(lane < base + 8, out * lax.rsqrt(pivots), 0.0))
        rows = [jnp.broadcast_to(now[s : s + 1], (8, size)) for s in range(8)]
        for i in range(g + 1, size // 8):
            left = groups[i]
            kept = jnp.where(inside, 0.0, left)
            for s in range(8):
                weight = jnp.broadcast_to(left[:, base + s : base + s + 1], (8, size))
                kept = kept - weight * rows[s]
            groups[i] = kept
    return jnp.concatenate(done)


def inverse_factor_kernel(gram_ref, out_ref, work_ref):
    size = gram_ref.shape[0]
    block = 128
    count = size // block
    work_ref[...] = gram_ref[...]
    lane = lax.broadcasted_iota(jnp.int32, (block, size), 1)

    def step(k, carry):
        base = pl.multiple_of(k * block, block)
        here = pl.ds(base, block)
        small = invert_block(work_ref[here, here])
        inside = (lane >= base) & (lane < base + block)
        eye = lax.broadcasted_iota(jnp.int32, (block, size), 0) == lane - base
        rows = jnp.where(inside, jnp.where(eye, 1.0, 0.0), work_ref[here, :])
        rows = jnp.dot(small, rows, precision=lax.Precision.HIGHEST, preferred_element_type=F32)
        out_ref[here, :] = jnp.where(lane < base + block, rows, 0.0)
        work_ref[here, :] = rows

        def update(i, carry):
            there = pl.ds(pl.multiple_of(i * block, block), block)
            left = work_ref[here, there]
            old = jnp.where(inside, 0.0, work_ref[there, :])
            work_ref[there, :] = old - lax.dot_general(
                left,
                rows,
                (((0,), (0,)), ((), ())),
                precision=lax.Precision.HIGHEST,
                preferred_element_type=F32,
            )
            return carry

        return lax.fori_loop(k + 1, count, update, carry)

    lax.fori_loop(0, count, step, 0)


def inverse_factor(gram):
    size = gram.shape[0]
    return pl.pallas_call(
        inverse_factor_kernel,
        out_shape=jax.ShapeDtypeStruct((size, size), F32),
        in_specs=[pl.BlockSpec(memory_space=pltpu.VMEM)],
        out_specs=pl.BlockSpec(memory_space=pltpu.VMEM),
        scratch_shapes=[pltpu.VMEM((size, size), F32)],
        compiler_params=pltpu.CompilerParams(vmem_limit_bytes=LIMIT),
        cost_estimate=pl.CostEstimate(
            flops=40 * size**3, bytes_accessed=8 * size * size, transcendentals=size
        ),
        name="inverse_factor",
    )(gram)


LIMIT = 10 << 20


def dot(left, right, dims=((1,), (0,))):
    return lax.dot_general(left, right, (dims, ((), ())), preferred_element_type=F32)


NT = ((1,), (1,))


def gather_rows(order_ref, sum_ref, send_ref, keep_ref, turned):
    half = send_ref.shape[0]
    block = sum_ref.shape[0] // (2 * half)
    for i in range(2 * half):
        here = pl.ds(pl.multiple_of(order_ref[i] * block, block), block)
        value = sum_ref[here, :]
        value = value.T if turned else value
        target = send_ref if i < half else keep_ref
        target[i % half] = value.astype(target.dtype)


def two_halves(size, shape, send_type):
    dims = (size // 2,) + shape
    return (jax.ShapeDtypeStruct(dims, send_type), jax.ShapeDtypeStruct(dims, F32))


def product_call(kernel, name, out_shape, scratch, weight, width, indices, arrays):
    height, depth = weight.shape
    smem, vmem = (pl.BlockSpec(memory_space=space) for space in (pltpu.SMEM, pltpu.VMEM))
    return pl.pallas_call(
        kernel,
        out_shape=out_shape,
        in_specs=[smem] * len(indices) + [vmem] * (1 + len(arrays)),
        out_specs=(vmem, vmem),
        scratch_shapes=[scratch],
        compiler_params=pltpu.CompilerParams(vmem_limit_bytes=LIMIT),
        cost_estimate=pl.CostEstimate(
            flops=2 * height * depth * width,
            bytes_accessed=2 * (height + width) * depth,
            transcendentals=0,
        ),
        name=name,
    )(*indices, weight, *arrays)


def rows_plain_kernel(
    part, width, turned, order_ref, weight_ref, right_ref, send_ref, keep_ref, sum_ref
):
    depth = weight_ref.shape[1]
    chunk = 512 if depth % 512 == 0 else depth

    def term(start):
        here = pl.ds(start, chunk)
        return dot(weight_ref[:, here], right_ref[here, part * width : (part + 1) * width])

    sum_ref[...] = term(0)

    @pl.loop(1, depth // chunk)
    def _(i):
        sum_ref[...] += term(pl.multiple_of(i * chunk, chunk))

    gather_rows(order_ref, sum_ref, send_ref, keep_ref, turned)


def rows_times(weight, right, part, width, rows, turned):
    height = weight.shape[0]
    block = height // rows.size
    shapes = two_halves(rows.size, (width, block) if turned else (block, width), F32)
    return product_call(
        functools.partial(rows_plain_kernel, part, width, turned),
        "rows_times",
        shapes,
        pltpu.VMEM((height, width), F32),
        weight,
        width,
        (rows.sending_first(),),
        (right,),
    )


def rows_joined_kernel(rows_ref, cols_ref, weight_ref, first_ref, second_ref, send_ref, keep_ref, sum_ref):
    half, _, own = first_ref.shape

    def term(part, i):
        block = cols_ref[i + half * (1 - part)]
        here = pl.ds(pl.multiple_of(block * own, 128), own)
        return dot(weight_ref[:, here], (first_ref, second_ref)[part][i], NT)

    sum_ref[...] = term(0, 0)
    for part in range(2):

        @pl.loop(1 - part, half)
        def _(i):
            sum_ref[...] += term(part, i)

    gather_rows(rows_ref, sum_ref, send_ref, keep_ref, False)


def rows_times_joined(weight, halves, rows, cols):
    height = weight.shape[0]
    width, own = halves[0].shape[1:]
    if own % 128:
        return rows_times(weight, cols.in_order(halves, 1).T, 0, width, rows, False)
    return product_call(
        rows_joined_kernel,
        "rows_times_joined",
        two_halves(rows.size, (height // rows.size, width), BF16),
        pltpu.VMEM((height, width), F32),
        weight,
        width,
        (rows.sending_first(), cols.sending_first()),
        halves,
    )


def cols_kernel(
    cols_ref, rows_ref, weight_ref, scale_ref, first_ref, second_ref, send_ref, keep_ref, whole_ref
):
    count, _, own = first_ref.shape
    for v in range(2 * count):
        block = rows_ref[(v + count) % (2 * count)]
        there = pl.ds(pl.multiple_of(block * own, 128), own)
        value = (first_ref, second_ref)[v // count][v % count]
        whole_ref[:, there] = (value.astype(F32) * scale_ref[:, there]).astype(BF16)

    half, _, block = send_ref.shape
    for part, out_ref in enumerate((send_ref, keep_ref)):

        @pl.loop(0, half)
        def _(i):
            here = pl.ds(pl.multiple_of(cols_ref[i + half * part] * block, 128), block)
            out_ref[i] = dot(whole_ref[...], weight_ref[:, here]).astype(out_ref.dtype)


def cols_times_joined(weight, scale, halves, rows, cols):
    height, depth = weight.shape
    block = depth // cols.size
    width, own = halves[0].shape[1:]
    if own % 128 or block % 128:
        left = (scale * rows.in_order(halves, 1)).astype(BF16)
        full = dot(left, weight).reshape(width, cols.size, block)
        order = cols.sending_first()
        full = jnp.stack([full[:, order[i]] for i in range(cols.size)])
        return full[: cols.size // 2].astype(BF16), full[cols.size // 2 :]
    return product_call(
        cols_kernel,
        "cols_times_joined",
        two_halves(cols.size, (width, block), BF16),
        pltpu.VMEM((width, height), BF16),
        weight,
        width,
        (cols.sending_first(), rows.sending_first()),
        (scale[None], *halves),
    )


def rank_kernel(weight_ref, basis_ref, out_ref):
    depth = weight_ref.shape[1]
    tile = math.gcd(depth, 512)

    @pl.loop(0, depth // tile)
    def _(i):
        here = pl.ds(pl.multiple_of(i * tile, tile), tile)
        out_ref[:, here] = dot(basis_ref[...], weight_ref[:, here]).astype(BF16)


def rank_times(weight, basis):
    height, depth = weight.shape
    if depth % 512:
        return dot(basis, weight).astype(BF16)
    vmem = pl.BlockSpec(memory_space=pltpu.VMEM)
    return pl.pallas_call(
        rank_kernel,
        out_shape=jax.ShapeDtypeStruct((basis.shape[0], depth), BF16),
        in_specs=[vmem, vmem],
        out_specs=vmem,
        compiler_params=pltpu.CompilerParams(vmem_limit_bytes=LIMIT),
        cost_estimate=pl.CostEstimate(
            flops=2 * height * depth * basis.shape[0],
            bytes_accessed=2 * (height + basis.shape[0]) * depth,
            transcendentals=0,
        ),
        name="rank_times",
    )(weight, basis)


def settle_kernel(order_ref, *refs):
    out_ref = refs[-1]
    count, block, half = refs[0].shape
    for v in range(2 * count):
        at = order_ref[(v + count) % (2 * count)] * block
        there = pl.ds(pl.multiple_of(at, block), block)
        for part in range(2):
            out_ref[there, part * half : (part + 1) * half] = refs[2 * part + v // count][v % count]


def settle(left, right, rows):
    count, block, half = left[0].shape
    if half % 128 or block % 16:
        return jnp.concatenate([rows.in_order(side, 0) for side in (left, right)], 1)
    vmem = pl.BlockSpec(memory_space=pltpu.VMEM)
    return pl.pallas_call(
        settle_kernel,
        out_shape=jax.ShapeDtypeStruct((2 * count * block, 2 * half), BF16),
        in_specs=[pl.BlockSpec(memory_space=pltpu.SMEM)] + [vmem] * 4,
        out_specs=vmem,
        compiler_params=pltpu.CompilerParams(vmem_limit_bytes=LIMIT),
        cost_estimate=pl.CostEstimate(
            flops=0, bytes_accessed=16 * count * block * half, transcendentals=0
        ),
        name="settle",
    )(rows.sending_first(), *left, *right)


def local(activations, out_grads, valid_len, weight, sketch):
    width = activations.shape[2]
    rows_here, cols_here = weight.shape
    rank = sketch.shape[1]
    half = rank // 2
    row_count, col_count = lax.axis_size("row"), lax.axis_size("col")
    row, col = lax.axis_index("row"), lax.axis_index("col")
    own_rows = rows_here // col_count
    over_col, over_row = Halving("col"), Halving("row")

    raw, later = (rows_times(weight, sketch, part, half, over_col, True) for part in range(2))
    mass = local_mass(activations, out_grads, valid_len, later[1])
    mass = mass.reshape(-1, own_rows)
    raw = over_col.scatter_sum(*raw)
    later, fisher = over_col.scatter_sum(*later, mass)
    fisher = sum_everywhere(fisher, col=False).reshape(width)
    mean = jnp.sum(fisher) / width + 1e-06
    square_scale = lax.dynamic_slice_in_dim(fisher, row * rows_here, rows_here) / mean
    own_square = lax.dynamic_slice_in_dim(square_scale, col * own_rows, own_rows)

    def second_of(first, scale):
        first = over_col.gather(first.astype(BF16))
        parts = cols_times_joined(weight, scale, first, over_col, over_row)
        projected = over_row.gather(over_row.scatter_sum(*parts).astype(BF16))
        parts = rows_times_joined(weight, projected, over_col, over_row)
        return over_col.gather(over_col.scatter_sum(*parts).astype(BF16))

    second = settle(
        second_of(raw, square_scale),
        second_of(own_square * later, jnp.ones_like(square_scale)),
        over_col,
    )

    even = (col & 1) == 0
    mine = lax.dynamic_slice_in_dim(second, (col & 1) * half, half, 1).astype(F32)
    rows_of = ((0,), (0,))
    gram = sum(dot(term, second, rows_of) for term in split(square_scale[:, None] * mine))
    gram = sum_everywhere(gram, col=False)
    other = swap(gram, lambda parity: 0, lambda parity: 1)
    gram = jnp.concatenate([jnp.where(even, gram, other), jnp.where(even, other, gram)])

    inverse = inverse_factor(gram)
    order = over_row.sending_first()
    blocks = inverse.reshape(row_count, rank // row_count, rank)

    def coeffs_of(places):
        part = [lax.dynamic_index_in_dim(blocks, order[i], 0, keepdims=False) for i in places]
        high, low = split(jnp.concatenate(part))
        basis = (dot(high, second, NT) + dot(low, second, NT)) * square_scale
        return rank_times(weight, basis.astype(BF16)).reshape(len(part), -1, cols_here)

    coeffs = over_row.scatter_sum(
        coeffs_of(range(row_count // 2)), coeffs_of(range(row_count // 2, row_count))
    )

    own = lax.dynamic_slice_in_dim(second, col * own_rows, own_rows)
    basis = sum(dot(own, term, NT) for term in split(inverse))
    basis = basis * (jnp.sqrt(own_square)[:, None] * math.sqrt(width))
    return basis, coeffs * math.sqrt(cols_here * col_count)


def solution(mesh):
    placed = (
        P("row", None, None),
        P("row", None, "col"),
        P("row"),
        P("row", "col"),
        P("col", None),
    )
    return jax.shard_map(
        local,
        mesh=mesh,
        in_specs=placed,
        out_specs=(P(("row", "col"), None), P("row", "col")),
        check_vma=False,
    )
```
